32 devices in a mesh: section: 2 (over x), dp: 4 (over z), tensor: 4 (over y, core).
Axes of the slice: x: 2, y: 2, z: 4, core: 2. Of those that a mesh axis runs over, the one named last changes fastest.
Arguments:
- block_input: bfloat16 [2, 4, 1024, 1536], P(None, 'dp', 'tensor'), may hold values from -6 to 6
- out_cotangent: bfloat16 [2, 4, 1024, 1536], P(None, 'dp', 'tensor'), may hold values from -6 to 6
- routes: int32 [2, 4, 1024, 4], P(None, 'dp'), may hold values from 0 to 7, all different within a row; in each aligned block of 1024 rows (0 to 1023, 1024 to 2047, ..., all dimensions but the last counted through in order) at most 576 rows name the same one
- attn_gain: bfloat16 [2, 1536], P('section', ('dp', 'tensor')), may hold values from 0.5 to 1.5
- ffn_gain: bfloat16 [2, 1536], P('section', ('dp', 'tensor')), may hold values from 0.5 to 1.5
- key_projection_weight: bfloat16 [2, 1536, 256], P('section', ('dp', 'tensor')), may hold values from -0.15625 to 0.15625
- value_projection_weight: bfloat16 [2, 1536, 256], P('section', ('dp', 'tensor')), may hold values from -0.15625 to 0.15625
- router_weight: bfloat16 [2, 1536, 8], P('section', ('dp', 'tensor')), may hold values from -0.078125 to 0.078125
- query_weight: bfloat16 [2, 1536, 1536], P('section', 'dp', 'tensor'), may hold values from -0.15625 to 0.15625
- output_weight: bfloat16 [2, 1536, 1536], P('section', 'tensor', 'dp'), may hold values from -1.25 to 1.25
- expert_gate: bfloat16 [2, 8, 1536, 768], P('section', None, 'dp', 'tensor'), may hold values from -0.15625 to 0.15625
- expert_up: bfloat16 [2, 8, 1536, 768], P('section', None, 'dp', 'tensor'), may hold values from -0.15625 to 0.15625
- expert_down: bfloat16 [2, 8, 768, 1536], P('section', None, 'tensor', 'dp'), may hold values from -0.625 to 0.625
Outputs:
- section_outputs: bfloat16 [2, 2, 4, 1024, 1536], P('section', None, 'dp', 'tensor')
- input_grads: bfloat16 [2, 2, 4, 1024, 1536], P('section', None, 'dp', 'tensor')
- attn_gain_grad: float32 [2, 1536], P('section', ('dp', 'tensor'))
- ffn_gain_grad: float32 [2, 1536], P('section', ('dp', 'tensor'))
- key_grad: float32 [2, 1536, 256], P('section', ('dp', 'tensor'))
- value_grad: float32 [2, 1536, 256], P('section', ('dp', 'tensor'))
- router_grad: float32 [2, 1536, 8], P('section', ('dp', 'tensor'))
- query_grad: float32 [2, 1536, 1536], P('section', 'dp', 'tensor')
- output_grad: float32 [2, 1536, 1536], P('section', 'tensor', 'dp')
- gate_grad: float32 [2, 8, 1536, 768], P('section', None, 'dp', 'tensor')
- up_grad: float32 [2, 8, 1536, 768], P('section', None, 'dp', 'tensor')
- down_grad: float32 [2, 8, 768, 1536], P('section', None, 'tensor', 'dp')
The draws below stay inside these ranges and needn't reach their ends.
Inputs may be any that keep to these rules, and one draw needn't show every extreme that they name: `routes`: each row names 4 different experts. In each aligned block of 1024 rows (one dp index's sequences of one micro-batch) no expert is named by more than 576 rows, a bound that some block reaches.
All inputs are finite; a program needn't handle non-finite values.
Results may differ from the reference program's by a relative error of at most 0.035.
Values may be sent and summed in bfloat16 or wider, within the bound.
No kernel may reach another device: no remote copies, remote signals or barrier semaphores. Data moves between devices by JAX's collectives and lax.ppermute only.
A program may use at most 328 MiB of HBM per device.

```python
import math
import jax
import jax.numpy as jnp
import numpy as np
from jax import lax

MODEL_WIDTH = 1536
QUERY_HEADS = 12
KEY_VALUE_HEADS = 2
HEAD_SIZE = 128
FF = 768
TOP = 4
E = 8
SEQUENCE_LENGTH = 1024
MICRO = 2
SEQ_DEV = 1
SEQS = 4
CAP = 576


def raised(drawn, stream_key, source, target, parts, factor):
    def block_of(position):
        return (jnp.arange(drawn.shape[position]) // (drawn.shape[position] // parts)).reshape((-1,) + (1,) * (drawn.ndim - 1 - position))

    near = jax.random.permutation(stream_key, parts)[block_of(target)]
    far = (block_of(target) + parts // 2) % parts
    return jnp.where((block_of(source) == near) | (block_of(source) == far), factor * drawn, drawn)


def shard_levels(key, dims, split, low, largest):
    loudness, own = 1.0, jax.random.fold_in(key, 6)
    for axis_at, parts in split:
        steps = jnp.exp(jax.random.uniform(jax.random.fold_in(own, axis_at), (parts,), jnp.float32, low / len(split), largest / len(split)))
        loudness = loudness * jnp.repeat(steps, dims[axis_at] // parts).reshape([-1 if axis == axis_at else 1 for axis in range(len(dims))])
    return loudness


def shared_out(rng, own, number, rows, amount, top, limit, slope):
    order = jax.random.permutation(rng, amount)
    packed, common = load_shares(amount, rows * top, limit, slope, True), load_shares(amount, rows * top, limit, slope, False)
    places = jnp.arange(amount)

    def named(lengths, turn):
        used = int((lengths > 0).sum())
        fixed = max(1, used // 4)
        passed = fixed + (places - fixed + turn * (used - fixed)) % max(1, amount - fixed)
        return jnp.zeros((amount,), jnp.int32).at[order[jnp.where(places < fixed, places, passed)]].set(jnp.asarray(lengths, jnp.int32))

    lengths = jnp.where(number % 4 == 0, named(packed, number // 4), named(common, number - number // 4 - 1))
    mixed = jax.random.permutation(jax.random.fold_in(own, 3), amount)
    giver, sink = mixed[0:amount // 2 * 2:2], mixed[1:amount // 2 * 2:2]
    slack = jnp.minimum(lengths[giver] - 1, limit - lengths[sink]) // 2
    slack = jnp.where((giver == order[0]) | (sink == order[0]) | (lengths[sink] == 0), 0, jnp.maximum(slack, 0))
    passed = jax.random.randint(jax.random.fold_in(own, 4), (amount // 2,), 0, 1 << 20) % (slack + 1)
    lengths = lengths.at[giver].add(-passed).at[sink].add(passed)
    labels = jnp.searchsorted(jnp.cumsum(lengths), jnp.arange(rows * top), side="right").astype(jnp.int32)
    grid = labels.reshape(top, rows).T
    grid = grid[jax.random.permutation(jax.random.fold_in(own, 1), rows)]
    turn = jax.random.randint(jax.random.fold_in(own, 2), (rows, 1), 0, top)
    return jnp.take_along_axis(grid, (jnp.arange(top)[None, :] + turn) % top, axis=1)


def load_shares(amount, total, most, lean, full):
    portions = [(1 << 20) // math.isqrt(rank ** lean) + 1 for rank in range(1, amount + 1)]
    largest = most if full else min(most, max(-(-total // amount), total * portions[0] // sum(portions)))
    least = 1 if total - largest >= amount - 1 else 0
    counts, rest = [largest] + [least] * (amount - 1), total - largest - least * (amount - 1)
    while rest > 0:
        movable = [i for i in range(1, amount) if counts[i] < largest] or [i for i in range(1, amount) if counts[i] < most]
        mass, remaining = sum([portions[i] for i in movable]), rest
        for i in movable:
            addition = min(most - counts[i], max(1, remaining * portions[i] // mass), rest)
            counts[i] = counts[i] + addition
            rest = rest - addition
    return np.array(counts)


def bell_draw(key, extent, deviation, limit, shards=(), kind=jnp.bfloat16):
    level = shard_levels(key, extent, shards, -0.22, 0.18) if shards else 1.0
    values = jax.random.normal(key, extent, jnp.float32) * deviation * level
    return jnp.minimum(jnp.maximum(values, -limit), limit).astype(kind)


def noise_with(key, dims, deviation, limit, shards, heavy, kind=jnp.bfloat16):
    drawn = deviation * jax.random.normal(key, dims, jnp.float32)
    if shards:
        drawn = drawn * shard_levels(key, dims, shards, -0.22, 0.18)
    return jnp.clip(raised(drawn, jax.random.fold_in(key, 3), *heavy), -limit, limit).astype(kind)


def setup_inputs(seed: int = 0) -> dict:
    key_of = jax.random.split(jax.random.key(seed), 14)
    block_input = noise_with(key_of[0], (MICRO, SEQS, SEQUENCE_LENGTH, MODEL_WIDTH), 1.0, 6.0, ((1, 4), (2, 4)), (1, 3, 4, 2.0))
    out_cotangent = noise_with(key_of[1], (MICRO, SEQS, SEQUENCE_LENGTH, MODEL_WIDTH), 1.0, 6.0, ((1, 4), (2, 4)), (1, 3, 4, 2.0))
    routes_keys = jax.random.split(jax.random.fold_in(key_of[2], 1), MICRO * SEQS * SEQUENCE_LENGTH // (SEQ_DEV * SEQUENCE_LENGTH))
    routes_turns = jax.random.permutation(jax.random.fold_in(key_of[2], 3), MICRO * SEQS * SEQUENCE_LENGTH // (SEQ_DEV * SEQUENCE_LENGTH))
    routes = jax.vmap(lambda own, number: shared_out(jax.random.fold_in(key_of[2], 2), own, number, SEQ_DEV * SEQUENCE_LENGTH, E, TOP, CAP, 0))(routes_keys, routes_turns).reshape((MICRO, SEQS, SEQUENCE_LENGTH, TOP))
    attn_gain = jnp.clip(0.5 + 1.0 * jax.random.uniform(key_of[3], (2, MODEL_WIDTH), jnp.float32) ** shard_levels(key_of[3], (2, MODEL_WIDTH), ((0, 2), (1, 16)), -0.2, 0.2), 0.5, 1.5).astype(jnp.bfloat16)
    ffn_gain = jnp.clip(0.5 + 1.0 * jax.random.uniform(key_of[4], (2, MODEL_WIDTH), jnp.float32) ** shard_levels(key_of[4], (2, MODEL_WIDTH), ((0, 2), (1, 16)), -0.2, 0.2), 0.5, 1.5).astype(jnp.bfloat16)
    key_projection_weight = bell_draw(key_of[5], (2, MODEL_WIDTH, KEY_VALUE_HEADS * HEAD_SIZE), MODEL_WIDTH ** -0.5, 0.15625, ((0, 2), (1, 16)))
    value_projection_weight = bell_draw(key_of[6], (2, MODEL_WIDTH, KEY_VALUE_HEADS * HEAD_SIZE), MODEL_WIDTH ** -0.5, 0.15625, ((0, 2), (1, 16)))
    router_weight = bell_draw(key_of[7], (2, MODEL_WIDTH, E), (4 * MODEL_WIDTH) ** -0.5, 0.078125, ((0, 2), (1, 16)))
    query_weight = bell_draw(key_of[8], (2, MODEL_WIDTH, QUERY_HEADS * HEAD_SIZE), MODEL_WIDTH ** -0.5, 0.15625, ((0, 2), (1, 4), (2, 4)))
    output_weight = bell_draw(key_of[9], (2, QUERY_HEADS * HEAD_SIZE, MODEL_WIDTH), (QUERY_HEADS * HEAD_SIZE // 64) ** -0.5, 1.25, ((0, 2), (1, 4), (2, 4)))
    expert_gate = bell_draw(key_of[10], (2, E, MODEL_WIDTH, FF), MODEL_WIDTH ** -0.5, 0.15625, ((0, 2), (2, 4), (3, 4)))
    expert_up = bell_draw(key_of[11], (2, E, MODEL_WIDTH, FF), MODEL_WIDTH ** -0.5, 0.15625, ((0, 2), (2, 4), (3, 4)))
    expert_down = bell_draw(key_of[12], (2, E, FF, MODEL_WIDTH), (FF // 8) ** -0.5, 0.625, ((0, 2), (2, 4), (3, 4)))
    return dict(block_input=block_input, out_cotangent=out_cotangent, routes=routes, attn_gain=attn_gain, ffn_gain=ffn_gain, key_projection_weight=key_projection_weight, value_projection_weight=value_projection_weight, router_weight=router_weight, query_weight=query_weight, output_weight=output_weight, expert_gate=expert_gate, expert_up=expert_up, expert_down=expert_down)


EPS = 1e-06
NEG = -1e+30

@jax.custom_vjp
def lower_section(v):
    return lax.optimization_barrier(v.astype(jnp.bfloat16)).astype(jnp.float32)

@jax.custom_vjp
def lower_section_backward(v):
    return v

def low_keep(v):
    return (lower_section(v), None)

def low_pass(kept, grad):
    return (grad,)

def back_keep(v):
    return (v, None)

def back_low(kept, grad):
    return (lower_section(grad),)
lower_section.defvjp(low_keep, low_pass)
lower_section_backward.defvjp(back_keep, back_low)

def rms_norm(vector, gain_vec):
    inverse = lax.rsqrt(lax.optimization_barrier(jnp.mean(vector * vector, -1, keepdims=True)) + EPS)
    return vector * inverse * gain_vec

def tables(length, head_width):
    halfway = head_width // 2
    places = jnp.arange(length).astype(jnp.float32)
    freq_rates = 10000.0 ** (-(jnp.arange(halfway).astype(jnp.float32) * 2.0) / head_width)
    angles = places[:, None] * freq_rates[None, :]
    return (jnp.cos(angles)[:, None, :], jnp.sin(angles)[:, None, :])

def rotate(vector, cosine, sine_val):
    halfway = vector.shape[-1] // 2
    first_half = vector[..., :halfway]
    second_half = vector[..., halfway:]
    return jnp.concatenate([first_half * cosine - second_half * sine_val, first_half * sine_val + second_half * cosine], -1)

def attend(normalized_input, query_w, key_matrix, value_matrix, output_w, cosine, sine_val):
    highest_precision = lax.Precision.HIGHEST
    query_group_count = QUERY_HEADS // KEY_VALUE_HEADS
    q_raw = lower_section_backward(jnp.dot(normalized_input, query_w, precision=highest_precision)).reshape(SEQUENCE_LENGTH, QUERY_HEADS, HEAD_SIZE)
    unrotated_keys = lower_section_backward(jnp.repeat(jnp.dot(normalized_input, key_matrix, precision=highest_precision).reshape(SEQUENCE_LENGTH, KEY_VALUE_HEADS, HEAD_SIZE), query_group_count, axis=1))
    repeated_values = lower_section_backward(jnp.repeat(lower_section(jnp.dot(normalized_input, value_matrix, precision=highest_precision)).reshape(SEQUENCE_LENGTH, KEY_VALUE_HEADS, HEAD_SIZE), query_group_count, axis=1))
    queries = lower_section(rotate(q_raw, cosine, sine_val))
    key_rot = lower_section(rotate(unrotated_keys, cosine, sine_val))
    scores = lower_section_backward(jnp.einsum('qhe,khe->hqk', queries, key_rot, precision=highest_precision))
    allowed = jnp.arange(SEQUENCE_LENGTH)[None, :] <= jnp.arange(SEQUENCE_LENGTH)[:, None]
    masked = jnp.where(allowed, scores * HEAD_SIZE ** (-0.5), NEG)
    row_max = lax.optimization_barrier(jnp.max(masked, -1, keepdims=True))
    exponent = jnp.exp(masked - row_max)
    low_probs = lower_section(exponent / lax.optimization_barrier(jnp.sum(exponent, -1, keepdims=True)))
    attended = lower_section_backward(lower_section(jnp.einsum('hqk,khe->qhe', low_probs, repeated_values, precision=highest_precision)))
    return lower_section_backward(jnp.dot(attended.reshape(SEQUENCE_LENGTH, QUERY_HEADS * HEAD_SIZE), output_w, precision=highest_precision))

def block_layer(inputs_val, routes, attn_g, ffn_g, key_matrix, value_matrix, router_w, query_w, output_w, gate_w, up_w, down_w):
    highest_precision = lax.Precision.HIGHEST
    act_shape = inputs_val.shape
    normed_one = lower_section(rms_norm(inputs_val, attn_g)).reshape(-1, SEQUENCE_LENGTH, MODEL_WIDTH)
    cosine, sine_val = tables(SEQUENCE_LENGTH, HEAD_SIZE)

    def attend_one(normalized_input):
        return attend(normalized_input, query_w, key_matrix, value_matrix, output_w, cosine, sine_val)
    attn_out = lax.map(jax.checkpoint(attend_one), normed_one)
    mid = inputs_val + attn_out.reshape(act_shape)
    normed_two = lower_section(rms_norm(mid, ffn_g)).reshape(-1, MODEL_WIDTH)
    logits = jnp.dot(normed_two, router_w, precision=highest_precision)
    flat_routes = routes.reshape(-1, TOP)
    gate_probs = jax.nn.softmax(jnp.take_along_axis(logits, flat_routes, 1), -1)
    onehot = (flat_routes[:, :, None] == jnp.arange(E)[None, None, :]).astype(jnp.float32)
    gate_share = lax.optimization_barrier(jnp.sum(gate_probs[:, :, None] * onehot, 1))

    def expert(running, expert_pack):
        gate_e, up_e, down_e, share_col = expert_pack
        pre_gate = lower_section_backward(jnp.dot(normed_two, gate_e, precision=highest_precision))
        pre_up = lower_section_backward(jnp.dot(normed_two, up_e, precision=highest_precision))
        hidden = lower_section(jax.nn.silu(pre_gate) * pre_up)
        expert_out = lower_section_backward(jnp.dot(hidden, down_e, precision=highest_precision))
        return (running + share_col[:, None] * expert_out, None)
    moe_out, _ = lax.scan(jax.checkpoint(expert), jnp.zeros_like(normed_two), (gate_w, up_w, down_w, gate_share.T))
    return mid + moe_out.reshape(act_shape)

def reference(block_input, out_cotangent, routes, attn_gain, ffn_gain, key_projection_weight, value_projection_weight, router_weight, query_weight, output_weight, expert_gate, expert_up, expert_down):

    def to_float(array_val):
        return array_val.astype(jnp.float32)
    inputs_val = to_float(block_input)
    cotangent = to_float(out_cotangent)
    weight_list = [to_float(entry) for entry in (attn_gain, ffn_gain, key_projection_weight, value_projection_weight, router_weight, query_weight, output_weight, expert_gate, expert_up, expert_down)]

    def apply_layer(layer_in, *weight_args):
        return block_layer(layer_in, routes, *weight_args)
    first_out, first_back = jax.vjp(apply_layer, inputs_val, *[entry[0] for entry in weight_list])
    link_value = lax.optimization_barrier(first_out.astype(jnp.bfloat16)).astype(jnp.float32)
    second_out, second_back = jax.vjp(apply_layer, link_value, *[entry[1] for entry in weight_list])
    second_grads = second_back(cotangent)
    link_grad = lax.optimization_barrier(second_grads[0].astype(jnp.bfloat16)).astype(jnp.float32)
    first_grads = first_back(link_grad)
    section_outputs = jnp.stack([first_out, second_out]).astype(jnp.bfloat16)
    input_grads = jnp.stack([first_grads[0], second_grads[0]]).astype(jnp.bfloat16)
    weight_grads = [jnp.stack([one_grad, two_grad]).astype(jnp.float32) for one_grad, two_grad in zip(first_grads[1:], second_grads[1:])]
    return (section_outputs, input_grads, weight_grads[0], weight_grads[1], weight_grads[2], weight_grads[3], weight_grads[4], weight_grads[5], weight_grads[6], weight_grads[7], weight_grads[8], weight_grads[9])
```

```python
import jax
import jax.numpy as jnp
from jax import lax
from jax.sharding import PartitionSpec as P

QUERY_HEADS = 12
KEY_VALUE_HEADS = 2
HEAD_SIZE = 128
TOP = 4
E = 8

EPS = 1e-06
NEG = -1e30
BF = jnp.bfloat16
F32 = jnp.float32


def swap_x(value):
    return lax.ppermute(value, "section", [(0, 1), (1, 0)])


def swap_y(value):
    return lax.ppermute(value, "tensor", [(t, t ^ 2) for t in range(4)])


def swap_c(value):
    return lax.ppermute(value, "tensor", [(t, t ^ 1) for t in range(4)])


def gather_chips(value):
    half = value.shape[0] // 2
    from_x = swap_x(value)
    from_y = swap_y(value)
    top = swap_x(from_y[:half])
    low = swap_y(from_x[half:])
    return jnp.stack([value, from_y, from_x, jnp.concatenate([top, low], 0)])


def gather_group(value):
    chips = gather_chips(value)
    return jnp.stack([chips, swap_c(chips)])


def add(one, two):
    return one.astype(F32) + two.astype(F32)


def scatter_chips(parts):
    half = parts.shape[1] // 2
    top = swap_x(parts[3][:half])
    low = swap_y(parts[3][half:])
    to_y = jnp.concatenate([add(parts[1][:half], top).astype(BF), parts[1][half:].astype(BF)], 0)
    to_x = jnp.concatenate([parts[2][:half].astype(BF), add(parts[2][half:], low).astype(BF)], 0)
    return parts[0].astype(F32) + swap_y(to_y).astype(F32) + swap_x(to_x).astype(F32)


def scatter_group(near, far):
    return scatter_chips(add(near, swap_c(far)).astype(BF))


def rope_tables(length, head_width):
    halfway = head_width // 2
    places = jnp.arange(length, dtype=F32)
    rates = 10000.0 ** (-(jnp.arange(halfway, dtype=F32) * 2.0) / head_width)
    angles = places[:, None] * rates[None, :]
    return jnp.cos(angles), jnp.sin(angles)


def rotate(vector, cosine, sine):
    halfway = vector.shape[-1] // 2
    a, b = vector[..., :halfway], vector[..., halfway:]
    return jnp.concatenate([a * cosine - b * sine, a * sine + b * cosine], -1)


def unrotate(vector, cosine, sine):
    return rotate(vector, cosine, -sine)


def mm(a, b):
    return lax.dot_general(a, b, (((1,), (0,)), ((), ())), preferred_element_type=F32)


def mm_nt(a, b):
    return lax.dot_general(a, b, (((1,), (1,)), ((), ())), preferred_element_type=F32)


def mm_tn(a, b):
    return lax.dot_general(a, b, (((0,), (0,)), ((), ())), preferred_element_type=F32)


def norm_forward(value, gain):
    inverse = lax.rsqrt(jnp.mean(value * value, -1, keepdims=True) + EPS)
    return value * inverse * gain


def norm_backward(value, gain, grad):
    inverse = lax.rsqrt(jnp.mean(value * value, -1, keepdims=True) + EPS)
    scaled = value * inverse
    weighted = grad * gain
    gain_grad = jnp.sum(grad * scaled, axis=0)
    return inverse * (weighted - scaled * jnp.mean(weighted * scaled, -1, keepdims=True)), gain_grad


def per_device(
    block_input,
    out_cotangent,
    routes,
    attn_gain,
    ffn_gain,
    key_projection_weight,
    value_projection_weight,
    router_weight,
    query_weight,
    output_weight,
    expert_gate,
    expert_up,
    expert_down,
):
    own = block_input.shape[2]
    width = block_input.shape[3]
    length = routes.shape[2]
    ff = expert_gate.shape[3]
    shard = expert_gate.shape[2]
    half_e = E // 2
    group = QUERY_HEADS // KEY_VALUE_HEADS
    section = lax.axis_index("section")
    tensor = lax.axis_index("tensor")
    first = section == 0
    chip = tensor // 2
    scale = HEAD_SIZE ** (-0.5)

    extras = jnp.concatenate(
        [
            router_weight[0],
            attn_gain[0][:, None],
            ffn_gain[0][:, None],
            jnp.zeros((attn_gain.shape[1], 128 - E - 2), BF),
        ],
        -1,
    )
    small = jnp.concatenate([key_projection_weight[0], value_projection_weight[0], extras], -1)
    small_all = lax.all_gather(small, ("section", "dp", "tensor"), axis=0, tiled=True)
    small_all = small_all.reshape(2, width, small.shape[-1])
    kv_cols = 2 * KEY_VALUE_HEADS * HEAD_SIZE

    output_t = output_weight[0].T
    query = query_weight[0]
    got = swap_x(jnp.where(first, output_t, query))
    kept = jnp.where(first, query, output_t)
    attn_shard = [jnp.where(first, kept, got), jnp.where(first, got, kept)]

    def attn_weights(layer):
        part = lax.all_gather(attn_shard[layer], "dp", axis=0, tiled=True)
        blocks = gather_group(part).reshape((2, 2, 2) + part.shape)
        mine = jnp.where(first, blocks[:, 0], blocks[:, 1])
        other = jnp.where(first, blocks[:, 1], blocks[:, 0])
        query_w = mine.transpose(2, 1, 0, 3).reshape(width, -1)
        output_w = other.transpose(2, 1, 0, 3).reshape(width, -1)
        return query_w, output_w

    def expert_pack(start):
        def cols(weight):
            piece = lax.dynamic_slice_in_dim(weight[0], start, half_e, 0)
            return piece.transpose(1, 0, 2).reshape(shard, half_e * ff)

        down = lax.dynamic_slice_in_dim(expert_down[0], start, half_e, 0).reshape(half_e * ff, shard)
        return jnp.concatenate([cols(expert_gate), cols(expert_up)], -1), down

    kept_up, kept_down = expert_pack(half_e * section)
    sent_up, sent_down = expert_pack(half_e * (1 - section))
    got_up, got_down = swap_x(sent_up), swap_x(sent_down)
    up_shard = [jnp.where(first, kept_up, got_up), jnp.where(first, got_up, kept_up)]
    down_shard = [jnp.where(first, kept_down, got_down), jnp.where(first, got_down, kept_down)]

    def expert_weights(layer):
        up = lax.all_gather(up_shard[layer], "dp", axis=0, tiled=True)
        down = lax.all_gather(down_shard[layer], "dp", axis=1, tiled=True)
        return up, down

    def hits_of(core):
        pieces = []
        for rel_x in range(2):
            for rel_y in range(2):
                mb = section ^ rel_x
                start = (tensor ^ (2 * rel_y + core)) * own
                piece = lax.dynamic_slice(routes, (mb, 0, start, 0), (1, 1, own, TOP))
                pieces.append(piece.reshape(own, TOP))
        picked = jnp.concatenate(pieces, 0)
        ids = (jnp.arange(E, dtype=jnp.int32) + half_e * section) % E
        return jnp.any(picked[:, :, None] == ids[None, None, :], 1)

    hits = [hits_of(0), hits_of(1)]

    def rolled(columns):
        return jnp.where(first, columns, jnp.roll(columns, half_e, -1))

    def gates_of(rows, router, hit):
        logits = jnp.where(hit, mm(rows, router), NEG)
        top = jnp.max(logits, -1, keepdims=True)
        exps = jnp.where(hit, jnp.exp(logits - top), 0.0)
        return exps / jnp.sum(exps, -1, keepdims=True)

    def expand(gates):
        return jnp.repeat(gates[:, :half_e], ff, axis=1)

    cos_all, sin_all = rope_tables(length, HEAD_SIZE)
    cosine = lax.dynamic_slice_in_dim(cos_all, tensor * own, own, 0)
    sine = lax.dynamic_slice_in_dim(sin_all, tensor * own, own, 0)
    row_pos = tensor * own + jnp.arange(own)
    key_pos = jnp.concatenate(
        [
            (tensor ^ (2 * rel_y + core)) * own + jnp.arange(own)
            for core in range(2)
            for rel_y in range(2)
        ]
    )
    allowed = key_pos[None, :] <= row_pos[:, None]

    def rel_heads(kv):
        return jnp.where(chip == 0, kv, kv[:, ::-1])

    def gather_rows(kv):
        near = jnp.stack([kv, swap_y(kv)])
        return jnp.stack([near, swap_c(near)])

    def layer_forward(x, layer, attn_w, experts):
        query_w, output_w = attn_w
        extra = small_all[layer][:, kv_cols:]
        gain_one = extra[:, E].astype(F32)
        gain_two = extra[:, E + 1].astype(F32)
        router = rolled(extra[:, :E])
        n_one = norm_forward(x, gain_one).astype(BF)
        q_raw = mm(n_one, query_w).reshape(own, QUERY_HEADS, HEAD_SIZE)
        queries = rotate(q_raw, cosine[:, None], sine[:, None]).astype(BF)
        kv_raw = mm(n_one, small_all[layer][:, :kv_cols])
        keys = kv_raw[:, : kv_cols // 2].reshape(own, KEY_VALUE_HEADS, HEAD_SIZE)
        keys = rotate(keys, cosine[:, None], sine[:, None]).reshape(own, -1)
        kv_own = jnp.concatenate([keys.astype(BF), kv_raw[:, kv_cols // 2 :].astype(BF)], -1)
        kv = gather_rows(kv_own).reshape(length, 2, KEY_VALUE_HEADS, HEAD_SIZE)
        key_rot = rel_heads(kv[:, 0])
        values = rel_heads(kv[:, 1])
        q_group = queries.reshape(own, KEY_VALUE_HEADS, group, HEAD_SIZE)
        scores = (
            jnp.einsum("qgje,kge->gjqk", q_group, key_rot, preferred_element_type=F32) * scale
        )
        scores = jnp.where(allowed, scores, NEG)
        row_max = jnp.max(scores, -1, keepdims=True)
        exps = jnp.exp(scores - row_max)
        total = jnp.sum(exps, -1, keepdims=True)
        low_probs = (exps / total).astype(BF)
        attended = (
            jnp.einsum("gjqk,kge->qgje", low_probs, values, preferred_element_type=F32)
            .astype(BF)
            .reshape(own, -1)
        )
        log_sum = row_max + jnp.log(total)
        mid = x + mm_nt(attended, output_w)
        n_two = norm_forward(mid, gain_two).astype(BF)
        chips_near = gather_chips(n_two)
        rows_near = chips_near.reshape(4 * own, width)
        rows_far = swap_c(chips_near).reshape(4 * own, width)
        up_w, down_w = experts
        outs = []
        kept_experts = []
        for rows, hit in zip((rows_near, rows_far), hits):
            gates = gates_of(rows, router, hit)
            both = mm(rows, up_w)
            pre_gate, pre_up = both[:, : half_e * ff], both[:, half_e * ff :]
            hidden = jax.nn.silu(pre_gate) * pre_up
            gated = (hidden * expand(gates)).astype(BF)
            outs.append(mm(gated, down_w).astype(BF).reshape(4, own, width))
            kept_experts.append(
                (rows, gates, pre_gate.astype(BF), pre_up.astype(BF), hidden.astype(BF), gated)
            )
        moe = scatter_group(outs[0], outs[1])
        kept = (x, n_one, queries, key_rot, values, attended, log_sum, mid, n_two, kept_experts)
        return (mid + moe).astype(BF), kept

    def layer_backward(grad, grad_rows, layer, attn_w, experts, kept):
        query_w, output_w = attn_w
        up_w, down_w = experts
        extra = small_all[layer][:, kv_cols:]
        gain_one = extra[:, E].astype(F32)
        gain_two = extra[:, E + 1].astype(F32)
        router = rolled(extra[:, :E])
        x, n_one, queries, key_rot, values, attended, log_sum, mid, n_two, kept_experts = kept
        outs = []
        up_grad = 0.0
        down_grad = 0.0
        for rows_g, (rows, gates, pre_gate, pre_up, hidden, gated) in zip(grad_rows, kept_experts):
            back = mm_nt(rows_g, down_w)
            pre_gate = pre_gate.astype(F32)
            pre_up = pre_up.astype(F32)
            d_gates = jnp.sum(
                (hidden.astype(F32) * back).reshape(4 * own, half_e, ff), -1
            )
            d_hidden = back * expand(gates)
            sig = jax.nn.sigmoid(pre_gate)
            d_gate = (d_hidden * pre_up * sig * (1.0 + pre_gate * (1.0 - sig))).astype(BF)
            d_up = (d_hidden * pre_gate * sig).astype(BF)
            d_both = jnp.concatenate([d_gate, d_up], -1)
            up_grad = up_grad + mm_tn(rows, d_both)
            down_grad = down_grad + mm_tn(rows_g, gated)
            d_rows = mm_nt(d_both, up_w)
            d_gates = rolled(jnp.pad(d_gates, ((0, 0), (0, half_e))))
            tail = jnp.pad(d_gates, ((0, 0), (0, 128 - E)))
            outs.append(jnp.concatenate([d_rows, tail], -1).astype(BF).reshape(4, own, width + 128))
        expert_grads = jnp.concatenate([up_grad.astype(BF), down_grad.astype(BF)], -1)
        summed = scatter_group(outs[0], outs[1])
        d_gates = rolled(summed[:, width : width + E])
        gates = kept_experts[0][1][:own]
        spread = gates * (d_gates - jnp.sum(gates * d_gates, -1, keepdims=True))
        spread_low = spread.astype(BF)
        router_grad = rolled(mm_tn(n_two, spread_low))
        d_n_two = summed[:, :width] + mm_nt(spread_low, router)
        d_norm, gain_two_grad = norm_backward(mid, gain_two, d_n_two)
        d_mid = grad.astype(F32) + d_norm
        d_attn = d_mid.astype(BF)
        output_grad = mm_tn(d_attn, attended)
        d_attended = mm(d_attn, output_w).astype(BF)
        q_group = queries.reshape(own, KEY_VALUE_HEADS, group, HEAD_SIZE)
        g_group = d_attended.reshape(own, KEY_VALUE_HEADS, group, HEAD_SIZE)
        scores = (
            jnp.einsum("qgje,kge->gjqk", q_group, key_rot, preferred_element_type=F32) * scale
        )
        probs = jnp.exp(jnp.where(allowed, scores, NEG) - log_sum)
        low_probs = probs.astype(BF)
        d_values = jnp.einsum("gjqk,qgje->kge", low_probs, g_group, preferred_element_type=F32)
        d_probs = jnp.einsum("qgje,kge->gjqk", g_group, values, preferred_element_type=F32)
        delta = jnp.sum(probs * d_probs, -1, keepdims=True)
        d_scores = (probs * (d_probs - delta) * scale).astype(BF)
        d_q = jnp.einsum("gjqk,kge->qgje", d_scores, key_rot, preferred_element_type=F32)
        d_keys = jnp.einsum("gjqk,qgje->kge", d_scores, q_group, preferred_element_type=F32)
        d_kv = jnp.concatenate(
            [rel_heads(d_keys).reshape(length, -1), rel_heads(d_values).reshape(length, -1)], -1
        )
        d_kv = d_kv.astype(BF).reshape(2, 2, own, kv_cols)
        d_kv = add(d_kv[0], swap_c(d_kv[1]))
        d_kv = d_kv[0] + swap_y(d_kv[1].astype(BF)).astype(F32)
        d_queries = unrotate(
            d_q.reshape(own, QUERY_HEADS, HEAD_SIZE), cosine[:, None], sine[:, None]
        )
        d_queries = d_queries.astype(BF).reshape(own, -1)
        d_keys = unrotate(
            d_kv[:, : kv_cols // 2].reshape(own, KEY_VALUE_HEADS, HEAD_SIZE),
            cosine[:, None],
            sine[:, None],
        ).reshape(own, -1)
        d_kv = jnp.concatenate([d_keys, d_kv[:, kv_cols // 2 :]], -1).astype(BF)
        query_grad = mm_tn(n_one, d_queries)
        kv_grad = mm_tn(n_one, d_kv)
        d_n_one = mm_nt(d_queries, query_w) + mm_nt(d_kv, small_all[layer][:, :kv_cols])
        d_norm, gain_one_grad = norm_backward(x, gain_one, d_n_one)
        d_in = (d_mid + d_norm).astype(BF)
        small_grad = jnp.concatenate(
            [
                kv_grad,
                router_grad,
                gain_one_grad[:, None],
                gain_two_grad[:, None],
                jnp.zeros((width, 128 - E - 2), F32),
            ],
            -1,
        )

        def blocks(value):
            return value.astype(BF).reshape(width, 2, 2, -1).transpose(2, 1, 0, 3)

        q_blocks, o_blocks = blocks(query_grad), blocks(output_grad)
        mine = jnp.where(first, q_blocks, o_blocks)
        other = jnp.where(first, o_blocks, q_blocks)
        parts = jnp.stack([mine, other], 1).reshape(2, 4, width, -1)
        attn_part = scatter_group(parts[0], parts[1])
        return d_in, expert_grads, attn_part, small_grad

    def reduce_dp(value):
        return lax.psum_scatter(value.astype(BF), "dp", scatter_dimension=0, tiled=True)

    own_cot = lax.dynamic_index_in_dim(out_cotangent, section, 0, keepdims=False)[0]
    own_in = lax.dynamic_index_in_dim(block_input, section, 0, keepdims=False)[0]
    attn_0 = attn_weights(0)
    experts_0 = expert_weights(0)
    attn_1 = attn_weights(1)
    experts_1 = expert_weights(1)

    cot = jnp.where(first, out_cotangent[:, 0], out_cotangent[::-1, 0])
    cot_near = jnp.stack([cot, swap_y(cot)], 1)
    cot_far = swap_c(cot_near)
    cot_rows = [v.reshape(4 * own, width) for v in (cot_near, cot_far)]

    out_0, kept_0 = layer_forward(own_in.astype(F32), 0, attn_0, experts_0)
    out_1, kept_1 = layer_forward(out_0.astype(F32), 1, attn_1, experts_1)
    link, experts_g1, attn_g1, small_g1 = layer_backward(
        own_cot, cot_rows, 1, attn_1, experts_1, kept_1
    )
    experts_g1 = reduce_dp(experts_g1)
    attn_g1 = reduce_dp(attn_g1)
    link_near = gather_chips(link)
    link_far = swap_c(link_near)
    link_rows = [v.reshape(4 * own, width) for v in (link_near, link_far)]
    grad_in, experts_g0, attn_g0, small_g0 = layer_backward(
        link, link_rows, 0, attn_0, experts_0, kept_0
    )
    experts_g0 = reduce_dp(experts_g0)
    attn_g0 = reduce_dp(attn_g0)
    small_g = lax.psum_scatter(
        jnp.concatenate([small_g0, small_g1], 0).astype(BF),
        ("section", "dp", "tensor"),
        scatter_dimension=0,
        tiled=True,
    ).astype(F32)

    def both_batches(value_0, value_1):
        got = swap_x(jnp.where(first, value_1, value_0))
        mine = jnp.where(first, value_0, value_1)
        return jnp.where(first, jnp.stack([mine, got]), jnp.stack([got, mine]))[None, :, None]

    section_outputs = both_batches(out_0, out_1)
    input_grads = both_batches(grad_in, link)

    def to_owner(value_0, value_1):
        got = swap_x(jnp.where(first, value_1, value_0))
        mine = jnp.where(first, value_0, value_1)
        return jnp.where(first, mine, got), jnp.where(first, got, mine)

    query_g, output_g = to_owner(attn_g0, attn_g1)
    low_e, high_e = to_owner(experts_g0, experts_g1)

    def split(low, high, at):
        cols = slice(at * half_e * ff, (at + 1) * half_e * ff)
        both = jnp.stack([low[:, cols], high[:, cols]], 0).astype(F32)
        return both.reshape(2, shard, half_e, ff)

    gate_g = split(low_e, high_e, 0).transpose(0, 2, 1, 3).reshape(E, shard, ff)
    up_g = split(low_e, high_e, 1).transpose(0, 2, 1, 3).reshape(E, shard, ff)
    down_g = split(low_e, high_e, 2).transpose(0, 2, 3, 1).reshape(E, ff, shard)
    half_kv = kv_cols // 2
    return (
        section_outputs,
        input_grads,
        small_g[:, kv_cols + E][None],
        small_g[:, kv_cols + E + 1][None],
        small_g[:, :half_kv][None],
        small_g[:, half_kv:kv_cols][None],
        small_g[:, kv_cols : kv_cols + E][None],
        query_g.astype(F32)[None],
        output_g.T.astype(F32)[None],
        gate_g[None],
        up_g[None],
        down_g[None],
    )


def solution(mesh):
    placed = (
        P(None, "dp", "tensor", None),
        P(None, "dp", "tensor", None),
        P(None, "dp", None, None),
        P("section", ("dp", "tensor")),
        P("section", ("dp", "tensor")),
        P("section", ("dp", "tensor"), None),
        P("section", ("dp", "tensor"), None),
        P("section", ("dp", "tensor"), None),
        P("section", "dp", "tensor"),
        P("section", "tensor", "dp"),
        P("section", None, "dp", "tensor"),
        P("section", None, "dp", "tensor"),
        P("section", None, "tensor", "dp"),
    )
    return jax.shard_map(
        per_device,
        mesh=mesh,
        in_specs=placed,
        out_specs=(
            P("section", None, "dp", "tensor", None),
            P("section", None, "dp", "tensor", None),
            P("section", ("dp", "tensor")),
            P("section", ("dp", "tensor")),
            P("section", ("dp", "tensor"), None),
            P("section", ("dp", "tensor"), None),
            P("section", ("dp", "tensor"), None),
            P("section", "dp", "tensor"),
            P("section", "tensor", "dp"),
            P("section", None, "dp", "tensor"),
            P("section", None, "dp", "tensor"),
            P("section", None, "tensor", "dp"),
        ),
        check_vma=False,
    )
```

```python
import jax
import jax.numpy as jnp
from jax import lax
from jax.sharding import PartitionSpec as P

QUERY_HEADS = 12
KEY_VALUE_HEADS = 2
HEAD_SIZE = 128
TOP = 4
E = 8
EPS = 1e-06
NEG = -1e30
BF = jnp.bfloat16
F32 = jnp.float32


def dot(a, b, contract):
    return lax.dot_general(a, b, (contract, ((), ())), preferred_element_type=F32)


def mm(a, b):
    return dot(a, b, ((1,), (0,)))


def mm_nt(a, b):
    return dot(a, b, ((1,), (1,)))


def mm_tn(a, b):
    return dot(a, b, ((0,), (0,)))


def masked_softmax(logits, hit):
    logits = jnp.where(hit, logits, NEG)
    top = jnp.max(logits, -1, keepdims=True)
    exps = jnp.where(hit, jnp.exp(logits - top), 0.0)
    return exps / jnp.sum(exps, -1, keepdims=True)


def spread(gates, ff):
    count = E // 2
    lane = lax.broadcasted_iota(jnp.int32, (gates.shape[0], count * ff), 1)
    wide = jnp.broadcast_to(gates[:, count - 1][:, None], lane.shape)
    for e in range(count - 2, -1, -1):
        wide = jnp.where(lane < (e + 1) * ff, gates[:, e][:, None], wide)
    return wide


def experts_call(ff, weight, forward=None, backward=None, kept=None):
    cols = (E // 2) * ff
    outs = []
    if forward:
        rows, hit, router = forward
        gates = masked_softmax(mm(rows, router[:, :E]), hit > 0.0)
        both = mm(rows, weight[:, : 2 * cols])
        pre_gate, pre_up = both[:, :cols], both[:, cols:]
    else:
        gates, pre_gate, pre_up = kept
        pre_gate, pre_up = pre_gate.astype(F32), pre_up.astype(F32)
    wide = spread(gates, ff)
    sig = jax.nn.sigmoid(pre_gate)
    active = pre_gate * sig
    hidden = active * pre_up
    gated = (hidden * wide).astype(BF)
    if forward:
        outs += [mm_nt(gated, weight[:, 2 * cols :]).astype(BF), gates]
        if not backward:
            outs += [pre_gate.astype(BF), pre_up.astype(BF)]
    if backward:
        grad, sums = backward
        back = mm(grad, weight[:, 2 * cols :])
        tail = mm((hidden * back).astype(BF), sums)
        d_hidden = back * wide
        d_gate = (d_hidden * pre_up * (sig * (1.0 + pre_gate * (1.0 - sig)))).astype(BF)
        d_both = jnp.concatenate([d_gate, (d_hidden * active).astype(BF)], -1)
        d_rows = mm_nt(d_both, weight[:, : 2 * cols]).astype(BF)
        outs += [jnp.concatenate([d_rows, tail.astype(BF)], -1), d_both, gated]
    return outs


def expert_grads(rows, grads, d_both, gated):
    up = mm_tn(rows[1], d_both[1]) + mm_tn(rows[0], d_both[0])
    down = mm_tn(grads[1], gated[1]) + mm_tn(grads[0], gated[0])
    return jnp.concatenate([up.astype(BF), down.astype(BF)], -1)


def turn(value, cosine, sine):
    heads = value.reshape(value.shape[0], -1, HEAD_SIZE)
    moved = jnp.roll(heads, HEAD_SIZE // 2, -1)
    return (heads * cosine[:, None] + moved * sine[:, None]).reshape(value.shape)


def relative_heads(place, value):
    value = value.reshape(value.shape[0], 2, KEY_VALUE_HEADS, HEAD_SIZE)
    return jnp.where(place[4] == 0, value, value[:, :, ::-1])


def seen(place, own):
    key = jnp.arange(own, dtype=jnp.int32)
    key = jnp.concatenate([key + place[b] for b in range(4)])
    return key[None, :] <= jnp.arange(own, dtype=jnp.int32)[:, None]


def attend(place, q_raw, near, far, cosine, sine):
    own, width = q_raw.shape
    queries = turn(q_raw, cosine, sine).astype(BF)
    q_group = queries.reshape(own, KEY_VALUE_HEADS, -1, HEAD_SIZE)
    kv = relative_heads(place, jnp.concatenate([near, far], 0))
    scores = jnp.einsum("qgje,kge->gjqk", q_group, kv[:, 0], preferred_element_type=F32)
    scores = jnp.where(seen(place, own), scores * HEAD_SIZE ** (-0.5), NEG)
    top = jnp.max(scores, -1, keepdims=True)
    exps = jnp.exp(scores - top)
    total = jnp.sum(exps, -1, keepdims=True)
    low = (exps / total).astype(BF)
    attended = jnp.einsum("gjqk,kge->qgje", low, kv[:, 1], preferred_element_type=F32)
    return queries, attended.astype(BF).reshape(own, width), top + jnp.log(total)


def attend_back(place, queries, grad, near, far, lse, cosine, sine):
    own, width = queries.shape
    scale = HEAD_SIZE ** (-0.5)
    q_group = queries.reshape(own, KEY_VALUE_HEADS, -1, HEAD_SIZE)
    g_group = grad.reshape(own, KEY_VALUE_HEADS, -1, HEAD_SIZE)
    kv = relative_heads(place, jnp.concatenate([near, far], 0))
    scores = jnp.einsum("qgje,kge->gjqk", q_group, kv[:, 0], preferred_element_type=F32)
    probs = jnp.exp(jnp.where(seen(place, own), scores * scale, NEG) - lse)
    d_probs = jnp.einsum("qgje,kge->gjqk", g_group, kv[:, 1], preferred_element_type=F32)
    weighed = probs * d_probs
    delta = jnp.sum(weighed, -1, keepdims=True)
    d_scores = ((weighed - probs * delta) * scale).astype(BF)
    low, d_scores = lax.optimization_barrier((probs.astype(BF), d_scores))
    d_values = jnp.einsum("gjqk,qgje->kge", low, g_group, preferred_element_type=F32)
    d_keys = jnp.einsum("gjqk,qgje->kge", d_scores, q_group, preferred_element_type=F32)
    dq = jnp.einsum("gjqk,kge->qgje", d_scores, kv[:, 0], preferred_element_type=F32)
    dq = turn(dq.reshape(own, width), cosine, -sine).astype(BF)
    d_kv = jnp.stack([d_keys, d_values], 1).astype(BF).reshape(near.shape[0] * 2, -1)
    d_kv = relative_heads(place, d_kv).reshape(d_kv.shape)
    return dq, d_kv[: near.shape[0]], d_kv[near.shape[0] :]


def swap_x(value):
    return lax.ppermute(value, "section", [(0, 1), (1, 0)])


def swap_y(value):
    return lax.ppermute(value, "tensor", [(t, t ^ 2) for t in range(4)])


def swap_c(value):
    return lax.ppermute(value, "tensor", [(t, t ^ 1) for t in range(4)])


def after(value, *first):
    return lax.optimization_barrier((value, first))[0]


def gather_chips(value):
    half = value.shape[0] // 2
    from_x = swap_x(value)
    from_y = swap_y(value)
    top = swap_x(from_y[:half])
    low = swap_y(from_x[half:])
    return jnp.stack([value, from_y, from_x, jnp.concatenate([top, low], 0)])


def add(one, two):
    return one.astype(F32) + two.astype(F32)


def scatter_chips(parts):
    half = parts.shape[1] // 2
    top = swap_x(parts[3][:half])
    low = swap_y(parts[3][half:])
    to_y = jnp.concatenate([add(parts[1][:half], top).astype(BF), parts[1][half:]], 0)
    to_x = jnp.concatenate([parts[2][:half], add(parts[2][half:], low).astype(BF)], 0)
    return parts[0].astype(F32) + swap_y(to_y).astype(F32) + swap_x(to_x).astype(F32)


def scatter_group(near, far):
    return scatter_chips(add(near, swap_c(far)).astype(BF))


def norm_forward(value, gain):
    inverse = lax.rsqrt(jnp.mean(value * value, -1, keepdims=True) + EPS)
    return value * inverse * gain


def norm_backward(value, gain, grad):
    inverse = lax.rsqrt(jnp.mean(value * value, -1, keepdims=True) + EPS)
    scaled = value * inverse
    weighted = grad * gain
    gain_grad = jnp.sum(grad * scaled, axis=0)
    return inverse * (weighted - scaled * jnp.mean(weighted * scaled, -1, keepdims=True)), gain_grad


def per_device(
    block_input,
    out_cotangent,
    routes,
    attn_gain,
    ffn_gain,
    key_projection_weight,
    value_projection_weight,
    router_weight,
    query_weight,
    output_weight,
    expert_gate,
    expert_up,
    expert_down,
):
    own = block_input.shape[2]
    width = block_input.shape[3]
    length = routes.shape[2]
    ff = expert_gate.shape[3]
    shard = expert_gate.shape[2]
    dp = width // shard
    little = attn_gain.shape[1]
    half_e = E // 2
    cols = half_e * ff
    kv_width = KEY_VALUE_HEADS * HEAD_SIZE
    part_cols = query_weight.shape[2]
    section = lax.axis_index("section")
    tensor = lax.axis_index("tensor")
    first = section == 0
    chip = tensor // 2
    core = tensor % 2

    def pick(pair, at):
        return lax.dynamic_index_in_dim(pair, at, 0, keepdims=False)

    extras = jnp.concatenate(
        [
            router_weight[0],
            attn_gain[0][:, None],
            ffn_gain[0][:, None],
            jnp.zeros((little, 128 - E - 2), BF),
        ],
        -1,
    )
    pack_q = jnp.concatenate(
        [query_weight[0], jnp.concatenate([key_projection_weight[0], extras], -1)], 0
    )
    pack_o = jnp.concatenate(
        [output_weight[0].T, jnp.pad(value_projection_weight[0], ((0, 0), (0, 128)))], 0
    )
    got = swap_x(jnp.where(first, pack_o, pack_q))
    kept = jnp.where(first, pack_q, pack_o)
    attn_shard = jnp.concatenate(
        [jnp.where(first, kept, got), jnp.where(first, got, kept)], 0
    )
    pack_rows = shard + little
    attn_parts = lax.all_gather(attn_shard, "dp", axis=0, tiled=True)
    attn_parts = attn_parts.reshape(dp, 2, pack_rows, part_cols)

    def expert_pack(start):
        def across(weight):
            piece = lax.dynamic_slice_in_dim(weight[0], start, half_e, 0)
            return piece.transpose(1, 0, 2).reshape(shard, cols)

        down = lax.dynamic_slice_in_dim(expert_down[0], start, half_e, 0).reshape(cols, shard)
        return jnp.concatenate([across(expert_gate), across(expert_up), down.T], -1)

    kept_e = expert_pack(half_e * section)
    got_e = swap_x(after(expert_pack(half_e * (1 - section)), got))
    expert_shard = [jnp.where(first, kept_e, got_e), jnp.where(first, got_e, kept_e)]

    cot = jnp.where(first, out_cotangent[:, 0], out_cotangent[::-1, 0])
    cot_near = after(jnp.stack([cot, swap_y(after(cot, got))], 1), got_e)
    cot_far = swap_c(cot_near)
    cot_rows = [v.reshape(4 * own, width) for v in (cot_near, cot_far)]

    def absolute(blocks):
        blocks = jnp.where(core == 0, blocks, blocks[::-1])
        return jnp.where(chip == 0, blocks, blocks[:, ::-1])

    def attn_weights(part):
        near = gather_chips(part.reshape(dp * pack_rows, part_cols))
        sides = [
            side.reshape(2, 2, dp, pack_rows, part_cols) for side in (near, swap_c(near))
        ]
        mains, smalls = [], []
        for kind in (section, 1 - section):
            chosen = [pick(side, kind) for side in sides]
            mains.append(
                [
                    chosen[c][y, :, :shard].reshape(width, part_cols)
                    for y in range(2)
                    for c in range(2)
                ]
            )
            small = absolute(jnp.stack([c[:, :, shard:] for c in chosen]))
            smalls.append(small.transpose(2, 1, 0, 3, 4).reshape(width, part_cols))
        extra = smalls[0][:, kv_width:]
        router = jnp.concatenate([rolled(extra[:, :E]), extra[:, E:]], -1)
        kv_w = jnp.concatenate([smalls[0][:, :kv_width], smalls[1][:, :kv_width]], -1)
        gains = extra[:, E : E + 2].astype(F32).T
        return mains[0], mains[1], kv_w, router, gains

    def rolled(columns):
        return jnp.where(first, columns, jnp.roll(columns, half_e, -1))

    def hits_of(rel_core):
        pieces = []
        for rel_x in range(2):
            for rel_y in range(2):
                start = (tensor ^ (2 * rel_y + rel_core)) * own
                piece = lax.dynamic_slice(routes, (section ^ rel_x, 0, start, 0), (1, 1, own, TOP))
                pieces.append(piece.reshape(own, TOP))
        picked = jnp.concatenate(pieces, 0)
        ids = (jnp.arange(E, dtype=jnp.int32) + half_e * section) % E
        return jnp.any(picked[:, :, None] == ids[None, None, :], 1).astype(F32)

    hits = [hits_of(0), hits_of(1)]
    sums = (
        jnp.arange(cols)[:, None] // ff + half_e * section == jnp.arange(128)[None, :]
    ).astype(BF)

    halfway = HEAD_SIZE // 2
    places = (tensor * own + jnp.arange(own)).astype(F32)
    rates = 10000.0 ** (-(jnp.arange(halfway, dtype=F32) * 2.0) / HEAD_SIZE)
    angles = places[:, None] * rates[None, :]
    cosine = jnp.concatenate([jnp.cos(angles)] * 2, -1)
    sine = jnp.concatenate([-jnp.sin(angles), jnp.sin(angles)], -1)
    place = jnp.stack(
        [((tensor ^ (2 * y + c)) - tensor) * own for c in range(2) for y in range(2)]
        + [chip] * 4
    ).astype(jnp.int32)

    def turned(value, sign):
        heads = value.reshape(own, -1, HEAD_SIZE)
        moved = jnp.roll(heads, halfway, -1)
        return (heads * cosine[:, None] + sign * moved * sine[:, None]).reshape(own, -1)

    def gather_rows(value):
        near = gather_chips(value)
        return near.reshape(4 * own, width), swap_c(near).reshape(4 * own, width)

    def forward_attention(x, weights):
        query_w, output_w, kv_w, _, gains = weights
        n_one = norm_forward(x, gains[0]).astype(BF)
        q_raw = jnp.concatenate([mm(n_one, w) for w in query_w], -1)
        kv_raw = mm(n_one, kv_w)
        kv_own = jnp.concatenate([turned(kv_raw[:, :kv_width], 1.0), kv_raw[:, kv_width:]], -1)
        kv_own = kv_own.astype(BF)
        kv_near = jnp.concatenate([kv_own, swap_y(kv_own)], 0)
        kv_far = swap_c(kv_near)
        queries, attended, lse = attend(place, q_raw, kv_near, kv_far, cosine, sine)
        mid = x
        for i, w in enumerate(output_w):
            mid = mid + mm_nt(attended[:, i * part_cols : (i + 1) * part_cols], w)
        n_two = norm_forward(mid, gains[1]).astype(BF)
        kept = (x, n_one, queries, kv_near, kv_far, attended, lse, mid, n_two)
        return mid, n_two, kept

    def halves(value):
        return value.reshape(dp, 2, shard // 2, -1).swapaxes(0, 1)

    def by_section(pair):
        return jnp.where(first, pair, pair[::-1])

    def reduce_group(blocks):
        sides = [jnp.stack([b[s] for s in range(2) for b in side]) for side in blocks]
        return scatter_group(sides[0], sides[1]).astype(BF)

    def part(value, chip_at, core_at):
        at = (2 * chip_at + core_at) * part_cols
        return value[:, at : at + part_cols]

    def backward_attention(grad, summed, gates, weights, kept, first_done=()):
        query_w, output_w, kv_w, router, gains = weights
        x, n_one, queries, kv_near, kv_far, attended, lse, mid, n_two = kept
        d_gates = rolled(summed[:, width : width + E])
        spread = gates * (d_gates - jnp.sum(gates * d_gates, -1, keepdims=True))
        spread_low = spread.astype(BF)
        router_grad = rolled(mm_tn(n_two, spread_low))
        d_n_two = summed[:, :width] + mm_nt(spread_low, router[:, :E])
        d_norm, gain_two_grad = norm_backward(mid, gains[1], d_n_two)
        d_mid = grad.astype(F32) + d_norm
        d_attn = d_mid.astype(BF)
        d_attended = jnp.concatenate([mm(d_attn, w) for w in output_w], -1).astype(BF)
        out_part = reduce_group(
            [
                [
                    by_section(halves(mm_tn(d_attn, part(attended, y, c)).astype(BF)))
                    .reshape(2, width // 2, part_cols)
                    for y in range(2)
                ]
                for c in range(2)
            ]
        )
        dq, d_near, d_far = after(
            attend_back(place, queries, d_attended, kv_near, kv_far, lse, cosine, sine),
            out_part,
            first_done,
        )
        d_kv = add(d_near, swap_c(d_far))
        d_kv = d_kv[:own] + swap_y(d_kv[own:].astype(BF)).astype(F32)
        d_kv = jnp.concatenate([turned(d_kv[:, :kv_width], -1.0), d_kv[:, kv_width:]], -1)
        d_kv = d_kv.astype(BF)
        d_n_one = mm_nt(d_kv, kv_w)
        for i, w in enumerate(query_w):
            d_n_one = d_n_one + mm_nt(dq[:, i * part_cols : (i + 1) * part_cols], w)
        d_norm, gain_one_grad = norm_backward(x, gains[0], d_n_one)
        d_in = (d_mid + d_norm).astype(BF)
        pieces = (n_one, dq, d_kv, router_grad, gain_one_grad, gain_two_grad)
        return d_in, out_part.reshape(dp, -1, part_cols), pieces

    def attn_grads(pieces):
        n_one, dq, d_kv, router_grad, gain_one_grad, gain_two_grad = pieces
        kv_grad = mm_tn(n_one, d_kv)
        extra = jnp.concatenate(
            [
                router_grad,
                gain_one_grad[:, None],
                gain_two_grad[:, None],
                jnp.zeros((width, 128 - E - 2), F32),
            ],
            -1,
        )
        small = jnp.stack(
            [
                jnp.concatenate([kv_grad[:, :kv_width], extra], -1),
                jnp.pad(kv_grad[:, kv_width:], ((0, 0), (0, 128))),
            ]
        ).astype(BF)
        small = small.reshape(2, dp, 2, 2, little, part_cols).transpose(3, 2, 0, 1, 4, 5)
        small = absolute(small)
        late = []
        for c in range(2):
            side = []
            for y in range(2):
                main = halves(mm_tn(n_one, part(dq, y, c)).astype(BF))
                main = main.reshape(2, dp, shard // 2, part_cols)
                both = jnp.concatenate([main, small[c, y]], 2)
                side.append(by_section(both.reshape(2, -1, part_cols)))
            late.append(side)
        return reduce_group(late).reshape(dp, -1, part_cols)

    def reduce_dp(value):
        return lax.psum_scatter(value, "dp", scatter_dimension=0, tiled=True)

    def blocks4(value):
        return value.reshape(4, own, -1)

    def both_batches(value_0, value_1):
        got = swap_x(jnp.where(first, value_1, value_0))
        mine = jnp.where(first, value_0, value_1)
        return jnp.where(first, jnp.stack([mine, got]), jnp.stack([got, mine]))[None, :, None]

    own_cot = pick(out_cotangent, section)[0]
    own_in = pick(block_input, section)[0]

    weights_0 = attn_weights(after(attn_parts[:, 0], cot_rows[1], expert_shard[0]))
    mid_0, n_two_0, kept_0 = forward_attention(own_in.astype(F32), weights_0)
    rows_0 = gather_rows(n_two_0)
    experts_0 = lax.all_gather(expert_shard[0], "dp", axis=0, tiled=True)
    router_0 = weights_0[3]
    weights_1 = attn_weights(after(attn_parts[:, 1], rows_0[1]))
    experts_1 = lax.all_gather(after(expert_shard[1], experts_0), "dp", axis=0, tiled=True)
    far_0 = experts_call(ff, experts_0, forward=(rows_0[1], hits[1], router_0))
    near_0 = experts_call(ff, experts_0, forward=(rows_0[0], hits[0], router_0))
    out_0 = (mid_0 + scatter_group(blocks4(near_0[0]), blocks4(far_0[0]))).astype(BF)

    mid_1, n_two_1, kept_1 = forward_attention(out_0.astype(F32), weights_1)
    rows_1 = gather_rows(n_two_1)
    router_1 = weights_1[3]
    far_1 = experts_call(
        ff, experts_1, forward=(rows_1[1], hits[1], router_1), backward=(cot_rows[1], sums)
    )
    near_1 = experts_call(
        ff, experts_1, forward=(rows_1[0], hits[0], router_1), backward=(cot_rows[0], sums)
    )
    summed_1 = scatter_group(blocks4(near_1[2]), blocks4(far_1[2]))
    grads_1 = expert_grads(rows_1, cot_rows, [near_1[3], far_1[3]], [near_1[4], far_1[4]])
    experts_g1 = reduce_dp(grads_1)
    moe_1 = scatter_group(
        blocks4(after(near_1[0], summed_1)), blocks4(after(far_1[0], summed_1))
    )
    out_1 = (mid_1 + moe_1).astype(BF)
    link, out_g1, pieces_1 = backward_attention(
        own_cot, summed_1, near_1[1][:own], weights_1, kept_1, out_1
    )

    link_rows = gather_rows(link)
    far_b = experts_call(ff, experts_0, backward=(link_rows[1], sums), kept=far_0[1:])
    near_b = experts_call(ff, experts_0, backward=(link_rows[0], sums), kept=near_0[1:])
    late_g1 = attn_grads(after(pieces_1, link_rows[1]))
    summed_0 = scatter_group(blocks4(near_b[0]), blocks4(far_b[0]))
    grads_0 = expert_grads(rows_0, link_rows, [near_b[1], far_b[1]], [near_b[2], far_b[2]])
    experts_g0 = reduce_dp(grads_0)
    summed_0 = after(summed_0, late_g1)
    section_outputs = both_batches(out_0, after(out_1, summed_0))
    grad_in, out_g0, pieces_0 = backward_attention(
        link, summed_0, near_0[1][:own], weights_0, kept_0, section_outputs
    )
    late_g0 = attn_grads(pieces_0)
    attn_g = jnp.concatenate([out_g1, late_g1, out_g0, late_g0], 1)
    attn_g = reduce_dp(attn_g.reshape(-1, part_cols))
    out_g1, late_g1, out_g0, late_g0 = jnp.split(
        attn_g, [shard // 2, shard + little, shard + little + shard // 2], 0
    )

    input_grads = both_batches(grad_in, link)

    def to_owner(value_0, value_1):
        got = swap_x(jnp.where(first, value_1, value_0))
        mine = jnp.where(first, value_0, value_1)
        return jnp.where(first, mine, got), jnp.where(first, got, mine)

    low, high = to_owner(
        jnp.concatenate([out_g0, late_g0], 0), jnp.concatenate([out_g1, late_g1], 0)
    )
    h = shard // 2
    output_g = jnp.concatenate([low[:h], high[:h]], 0).astype(F32)
    query_g = jnp.concatenate([low[h : 2 * h], high[h : 2 * h]], 0).astype(F32)
    key_g = low[2 * h :].astype(F32)
    value_g = high[2 * h :].astype(F32)
    low_e, high_e = to_owner(experts_g0, experts_g1)

    def split(at):
        part = slice(at * cols, (at + 1) * cols)
        both = jnp.stack([low_e[:, part], high_e[:, part]], 0).astype(F32)
        return both.reshape(2, shard, half_e, ff)

    gate_g = split(0).transpose(0, 2, 1, 3).reshape(E, shard, ff)
    up_g = split(1).transpose(0, 2, 1, 3).reshape(E, shard, ff)
    down_g = split(2).transpose(0, 2, 3, 1).reshape(E, ff, shard)
    return (
        section_outputs,
        input_grads,
        key_g[:, kv_width + E][None],
        key_g[:, kv_width + E + 1][None],
        key_g[:, :kv_width][None],
        value_g[:, :kv_width][None],
        key_g[:, kv_width : kv_width + E][None],
        query_g[None],
        output_g.T[None],
        gate_g[None],
        up_g[None],
        down_g[None],
    )


def solution(mesh):
    placed = (
        P(None, "dp", "tensor", None),
        P(None, "dp", "tensor", None),
        P(None, "dp", None, None),
        P("section", ("dp", "tensor")),
        P("section", ("dp", "tensor")),
        P("section", ("dp", "tensor"), None),
        P("section", ("dp", "tensor"), None),
        P("section", ("dp", "tensor"), None),
        P("section", "dp", "tensor"),
        P("section", "tensor", "dp"),
        P("section", None, "dp", "tensor"),
        P("section", None, "dp", "tensor"),
        P("section", None, "tensor", "dp"),
    )
    return jax.shard_map(
        per_device,
        mesh=mesh,
        in_specs=placed,
        out_specs=(
            P("section", None, "dp", "tensor", None),
            P("section", None, "dp", "tensor", None),
            P("section", ("dp", "tensor")),
            P("section", ("dp", "tensor")),
            P("section", ("dp", "tensor"), None),
            P("section", ("dp", "tensor"), None),
            P("section", ("dp", "tensor"), None),
            P("section", "dp", "tensor"),
            P("section", "tensor", "dp"),
            P("section", None, "dp", "tensor"),
            P("section", None, "dp", "tensor"),
            P("section", None, "tensor", "dp"),
        ),
        check_vma=False,
    )
```

```python
import jax
import jax.numpy as jnp
from jax import lax
from jax.sharding import PartitionSpec as P

QUERY_HEADS = 12
KEY_VALUE_HEADS = 2
HEAD_SIZE = 128
TOP = 4
E = 8
EPS = 1e-06
NEG = -1e30
BF = jnp.bfloat16
F32 = jnp.float32


def dot(a, b, contract):
    return lax.dot_general(a, b, (contract, ((), ())), preferred_element_type=F32)


def mm(a, b):
    return dot(a, b, ((1,), (0,)))


def mm_nt(a, b):
    return dot(a, b, ((1,), (1,)))


def mm_tn(a, b):
    return dot(a, b, ((0,), (0,)))


def masked_softmax(logits, hit):
    logits = jnp.where(hit, logits, NEG)
    top = jnp.max(logits, -1, keepdims=True)
    exps = jnp.where(hit, jnp.exp(logits - top), 0.0)
    return exps / jnp.sum(exps, -1, keepdims=True)


def spread(gates, ff):
    count = E // 2
    lane = lax.broadcasted_iota(jnp.int32, (gates.shape[0], count * ff), 1)
    wide = jnp.broadcast_to(gates[:, count - 1][:, None], lane.shape)
    for e in range(count - 2, -1, -1):
        wide = jnp.where(lane < (e + 1) * ff, gates[:, e][:, None], wide)
    return wide


def experts_forward(ff, rows, hit, router, up_w, down_w):
    cols = (E // 2) * ff
    gates = masked_softmax(mm(rows, router[:, :E]), hit)
    both = mm(rows, up_w)
    pre_gate, pre_up = both[:, :cols], both[:, cols:]
    gated = (jax.nn.silu(pre_gate) * pre_up * spread(gates, ff)).astype(BF)
    out = mm_nt(gated, down_w).astype(BF)
    return out, (gates, pre_gate.astype(BF), pre_up.astype(BF))


def experts_backward(ff, grad, sums, up_w, down_w, kept):
    gates, pre_gate, pre_up = kept
    pre_gate, pre_up = pre_gate.astype(F32), pre_up.astype(F32)
    wide = spread(gates, ff)
    sig = jax.nn.sigmoid(pre_gate)
    active = pre_gate * sig
    hidden = active * pre_up
    gated = (hidden * wide).astype(BF)
    back = mm(grad, down_w)
    tail = mm((hidden * back).astype(BF), sums)
    d_hidden = back * wide
    d_gate = (d_hidden * pre_up * (sig * (1.0 + pre_gate * (1.0 - sig)))).astype(BF)
    d_both = jnp.concatenate([d_gate, (d_hidden * active).astype(BF)], -1)
    d_rows = mm_nt(d_both, up_w).astype(BF)
    return jnp.concatenate([d_rows, tail.astype(BF)], -1), d_both, gated


def expert_grads(dp, rows, grads, d_both, gated):
    up = sum(mm_tn(d, r) for d, r in zip(d_both, rows)).astype(BF)
    down = sum(mm_tn(h, g) for h, g in zip(gated, grads)).astype(BF)
    both = jnp.concatenate([up, down], 0)
    return both.reshape(both.shape[0], dp, -1).swapaxes(0, 1)


def turn(value, cosine, sine):
    heads = value.reshape(value.shape[0], -1, HEAD_SIZE)
    moved = jnp.roll(heads, HEAD_SIZE // 2, -1)
    return (heads * cosine[:, None] + moved * sine[:, None]).reshape(value.shape)


def relative_heads(place, value):
    value = value.reshape(value.shape[0], 2, KEY_VALUE_HEADS, HEAD_SIZE)
    return jnp.where(place[4] == 0, value, value[:, :, ::-1])


def seen(place, own):
    key = jnp.arange(own, dtype=jnp.int32)
    key = jnp.concatenate([key + place[b] for b in range(4)])
    return key[None, :] <= jnp.arange(own, dtype=jnp.int32)[:, None]


def attend(place, q_raw, near, far, cosine, sine):
    own, width = q_raw.shape
    queries = turn(q_raw, cosine, sine).astype(BF)
    q_group = queries.reshape(own, KEY_VALUE_HEADS, -1, HEAD_SIZE)
    kv = relative_heads(place, jnp.concatenate([near, far], 0))
    scores = jnp.einsum("qgje,kge->gjqk", q_group, kv[:, 0], preferred_element_type=F32)
    scores = jnp.where(seen(place, own), scores * HEAD_SIZE ** (-0.5), NEG)
    top = jnp.max(scores, -1, keepdims=True)
    exps = jnp.exp(scores - top)
    total = jnp.sum(exps, -1, keepdims=True)
    low = (exps / total).astype(BF)
    attended = jnp.einsum("gjqk,kge->qgje", low, kv[:, 1], preferred_element_type=F32)
    return queries, attended.astype(BF).reshape(own, width), top + jnp.log(total)


def attend_back(place, queries, grad, near, far, lse, cosine, sine):
    own, width = queries.shape
    scale = HEAD_SIZE ** (-0.5)
    q_group = queries.reshape(own, KEY_VALUE_HEADS, -1, HEAD_SIZE)
    g_group = grad.reshape(own, KEY_VALUE_HEADS, -1, HEAD_SIZE)
    kv = relative_heads(place, jnp.concatenate([near, far], 0))
    scores = jnp.einsum("qgje,kge->gjqk", q_group, kv[:, 0], preferred_element_type=F32)
    probs = jnp.exp(jnp.where(seen(place, own), scores * scale, NEG) - lse)
    d_probs = jnp.einsum("qgje,kge->gjqk", g_group, kv[:, 1], preferred_element_type=F32)
    weighed = probs * d_probs
    delta = jnp.sum(weighed, -1, keepdims=True)
    d_scores = ((weighed - probs * delta) * scale).astype(BF)
    low, d_scores = lax.optimization_barrier((probs.astype(BF), d_scores))
    d_values = jnp.einsum("gjqk,qgje->kge", low, g_group, preferred_element_type=F32)
    d_keys = jnp.einsum("gjqk,qgje->kge", d_scores, q_group, preferred_element_type=F32)
    dq = jnp.einsum("gjqk,kge->qgje", d_scores, kv[:, 0], preferred_element_type=F32)
    dq = turn(dq.reshape(own, width), cosine, -sine).astype(BF)
    d_kv = jnp.stack([d_keys, d_values], 1).astype(BF).reshape(near.shape[0] * 2, -1)
    d_kv = relative_heads(place, d_kv).reshape(d_kv.shape)
    return dq, d_kv[: near.shape[0]], d_kv[near.shape[0] :]


def swap_x(value):
    return lax.ppermute(value, "section", [(0, 1), (1, 0)])


def swap_y(value):
    return lax.ppermute(value, "tensor", [(t, t ^ 2) for t in range(4)])


def swap_c(value):
    return lax.ppermute(value, "tensor", [(t, t ^ 1) for t in range(4)])


def after(value, *first):
    return lax.optimization_barrier((value, first))[0]


def gather_chips(value):
    half = value.shape[0] // 2
    from_x = swap_x(value)
    from_y = swap_y(value)
    top = swap_x(from_y[:half])
    low = swap_y(from_x[half:])
    return jnp.stack([value, from_y, from_x, jnp.concatenate([top, low], 0)])


def gather_chunks(value):
    half = value.shape[0] // 2
    from_y = swap_y(value)
    from_x = swap_x(value)
    corner = jnp.concatenate([swap_x(from_y[:half]), swap_y(from_x[half:])], 0)
    return [jnp.concatenate([v, swap_c(v)], 0) for v in (value, from_y, from_x, corner)]


def add(one, two):
    return one.astype(F32) + two.astype(F32)


def scatter_chips(parts):
    half = parts.shape[1] // 2
    top = swap_x(parts[3][:half])
    low = swap_y(parts[3][half:])
    to_y = jnp.concatenate([add(parts[1][:half], top).astype(BF), parts[1][half:]], 0)
    to_x = jnp.concatenate([parts[2][:half], add(parts[2][half:], low).astype(BF)], 0)
    return parts[0].astype(F32) + swap_y(to_y).astype(F32) + swap_x(to_x).astype(F32)


def scatter_group(near, far):
    return scatter_chips(add(near, swap_c(far)).astype(BF))


def scatter_chunks(chunks):
    rows = chunks[0].shape[0] // 2
    half = rows // 2
    own, to_y, to_x, corner = [add(c[:rows], swap_c(c[rows:])).astype(BF) for c in chunks]
    top = swap_y(swap_x(corner[:half]))
    low = swap_x(swap_y(corner[half:]))
    return add(own, swap_y(to_y)) + add(swap_x(to_x), jnp.concatenate([top, low], 0))


def norm_forward(value, gain):
    inverse = lax.rsqrt(jnp.mean(value * value, -1, keepdims=True) + EPS)
    return value * inverse * gain


def norm_backward(value, gain, grad):
    inverse = lax.rsqrt(jnp.mean(value * value, -1, keepdims=True) + EPS)
    scaled = value * inverse
    weighted = grad * gain
    gain_grad = jnp.sum(grad * scaled, axis=0)
    return inverse * (weighted - scaled * jnp.mean(weighted * scaled, -1, keepdims=True)), gain_grad


def per_device(
    block_input,
    out_cotangent,
    routes,
    attn_gain,
    ffn_gain,
    key_projection_weight,
    value_projection_weight,
    router_weight,
    query_weight,
    output_weight,
    expert_gate,
    expert_up,
    expert_down,
):
    own = block_input.shape[2]
    width = block_input.shape[3]
    length = routes.shape[2]
    ff = expert_gate.shape[3]
    shard = expert_gate.shape[2]
    dp = width // shard
    little = attn_gain.shape[1]
    half_e = E // 2
    cols = half_e * ff
    kv_width = KEY_VALUE_HEADS * HEAD_SIZE
    part_cols = query_weight.shape[2]
    section = lax.axis_index("section")
    tensor = lax.axis_index("tensor")
    first = section == 0
    chip = tensor // 2
    core = tensor % 2

    def pick(pair, at):
        return lax.dynamic_index_in_dim(pair, at, 0, keepdims=False)

    sh = shard // 2

    extras = jnp.concatenate(
        [
            router_weight[0],
            attn_gain[0][:, None],
            ffn_gain[0][:, None],
            jnp.zeros((little, 128 - E - 2), BF),
        ],
        -1,
    )
    littles = jnp.stack(
        [
            jnp.concatenate([key_projection_weight[0], extras], -1),
            jnp.pad(value_projection_weight[0], ((0, 0), (0, 128))),
        ]
    )
    output_t = output_weight[0].T

    def attn_pack(h):
        return jnp.concatenate(
            [
                lax.dynamic_slice_in_dim(query_weight[0], h * sh, sh, 0),
                pick(littles, h),
                lax.dynamic_slice_in_dim(output_t, h * sh, sh, 0),
            ],
            0,
        )

    got = swap_x(attn_pack(1 - section))
    kept = attn_pack(section)
    attn_shard = jnp.concatenate(
        [jnp.where(first, kept, got), jnp.where(first, got, kept)], 0
    )
    attn_parts = lax.all_gather(attn_shard, "dp", axis=0, tiled=True)
    attn_parts = attn_parts.reshape(dp, 2, shard + little, part_cols)

    def expert_pack(start):
        def across(weight):
            piece = lax.dynamic_slice_in_dim(weight[0], start, half_e, 0)
            return piece.transpose(1, 0, 2).reshape(shard, cols)

        down = lax.dynamic_slice_in_dim(expert_down[0], start, half_e, 0).reshape(cols, shard)
        return jnp.concatenate([across(expert_gate), across(expert_up), down.T], -1)

    kept_e = expert_pack(half_e * section)
    got_e = swap_x(after(expert_pack(half_e * (1 - section)), got))
    expert_shard = [jnp.where(first, kept_e, got_e), jnp.where(first, got_e, kept_e)]

    cot = jnp.where(first, out_cotangent[:, 0], out_cotangent[::-1, 0])
    cot_near = after(jnp.stack([cot, swap_y(after(cot, got))], 1), got_e)
    cot_far = swap_c(cot_near)
    cot_chunks = [
        jnp.concatenate([cot_near[x, y], cot_far[x, y]], 0) for x in range(2) for y in range(2)
    ]

    def absolute(blocks):
        blocks = jnp.where(core == 0, blocks, blocks[::-1])
        return jnp.where(chip == 0, blocks, blocks[:, ::-1])

    def to_rel(value):
        value = value.reshape(own, dp, 2, sh).swapaxes(1, 2)
        value = jnp.where(first, value, value[:, ::-1]).reshape(own, 2, width // 2)
        return value[:, 0], value[:, 1]

    def from_rel(halves):
        value = jnp.stack(halves, 1).reshape(own, 2, dp, sh)
        return jnp.where(first, value, value[:, ::-1]).swapaxes(1, 2).reshape(own, width)

    def attn_weights(parts, *first_done):
        near_q = gather_chips(
            after(parts[:, : sh + little], *first_done).reshape(-1, part_cols)
        )
        sides = [near_q, swap_c(near_q)]
        near_o = gather_chips(after(parts[:, sh + little :], sides[1]).reshape(-1, part_cols))
        far_o = swap_c(near_o)
        sides = [side.reshape(2, 2, dp, sh + little, part_cols) for side in sides]
        query_w = [
            [sides[c][x, y, :, :sh].reshape(width // 2, part_cols) for y in range(2) for c in range(2)]
            for x in range(2)
        ]
        output_w = [[(near_o, far_o)[c][2 * x + y] for y in range(2) for c in range(2)] for x in range(2)]
        smalls = []
        for kind in (section, 1 - section):
            small = absolute(jnp.stack([pick(side[:, :, :, sh:], kind) for side in sides]))
            smalls.append(small.transpose(2, 1, 0, 3, 4).reshape(width, part_cols))
        extra = smalls[0][:, kv_width:]
        router = rolled(extra[:, :E])
        kv_w = jnp.concatenate([smalls[0][:, :kv_width], smalls[1][:, :kv_width]], -1)
        gains = extra[:, E : E + 2].astype(F32).T
        return query_w, output_w, kv_w, router, gains

    def rolled(columns):
        return jnp.where(first, columns, jnp.roll(columns, half_e, -1))

    def hits_of(rel_x, rel_y):
        pieces = []
        for rel_core in range(2):
            start = (tensor ^ (2 * rel_y + rel_core)) * own
            piece = lax.dynamic_slice(routes, (section ^ rel_x, 0, start, 0), (1, 1, own, TOP))
            pieces.append(piece.reshape(own, TOP))
        picked = jnp.concatenate(pieces, 0)
        ids = (jnp.arange(E, dtype=jnp.int32) + half_e * section) % E
        return jnp.any(picked[:, :, None] == ids[None, None, :], 1)

    hits = [hits_of(x, y) for x in range(2) for y in range(2)]
    sums = (
        jnp.arange(cols)[:, None] // ff + half_e * section == jnp.arange(128)[None, :]
    ).astype(BF)

    halfway = HEAD_SIZE // 2
    places = (tensor * own + jnp.arange(own)).astype(F32)
    rates = 10000.0 ** (-(jnp.arange(halfway, dtype=F32) * 2.0) / HEAD_SIZE)
    angles = places[:, None] * rates[None, :]
    cosine = jnp.concatenate([jnp.cos(angles)] * 2, -1)
    sine = jnp.concatenate([-jnp.sin(angles), jnp.sin(angles)], -1)
    place = jnp.stack(
        [((tensor ^ (2 * y + c)) - tensor) * own for c in range(2) for y in range(2)]
        + [chip] * 4
    ).astype(jnp.int32)

    def turned(value, sign):
        heads = value.reshape(own, -1, HEAD_SIZE)
        moved = jnp.roll(heads, halfway, -1)
        return (heads * cosine[:, None] + sign * moved * sine[:, None]).reshape(own, -1)

    def part(value, i):
        return value[:, i * part_cols : (i + 1) * part_cols]

    def forward_attention(x, weights, *first_done):
        query_w, output_w, kv_w, _, gains = weights
        n_one = norm_forward(x, gains[0]).astype(BF)
        n_rel = to_rel(n_one)
        kv_raw = mm(n_one, kv_w)
        kv_own = jnp.concatenate([turned(kv_raw[:, :kv_width], 1.0), kv_raw[:, kv_width:]], -1)
        kv_own = after(kv_own.astype(BF), *first_done)
        kv_near = jnp.concatenate([kv_own, swap_y(kv_own)], 0)
        kv_far = swap_c(kv_near)
        q_raw = jnp.concatenate(
            [mm(n_rel[0], query_w[0][i]) + mm(n_rel[1], query_w[1][i]) for i in range(4)], -1
        )
        queries, attended, lse = attend(place, q_raw, kv_near, kv_far, cosine, sine)
        mid = x + from_rel(
            [sum(mm_nt(part(attended, i), output_w[h][i]) for i in range(4)) for h in range(2)]
        )
        n_two = norm_forward(mid, gains[1]).astype(BF)
        return mid, n_two, (x, n_one, n_rel, queries, kv_near, kv_far, attended, lse, mid, n_two)

    def reduce_group(blocks):
        sides = [jnp.stack([blocks[h][2 * y + c] for h in range(2) for y in range(2)]) for c in range(2)]
        return scatter_group(sides[0], sides[1]).astype(BF)

    def backward_attention(grad, summed, gates, weights, kept, *first_done):
        query_w, output_w, kv_w, router, gains = weights
        x, n_one, n_rel, queries, kv_near, kv_far, attended, lse, mid, n_two = kept
        d_gates = rolled(summed[:, width : width + E])
        spread_low = (gates * (d_gates - jnp.sum(gates * d_gates, -1, keepdims=True))).astype(BF)
        d_n_two = summed[:, :width] + mm_nt(spread_low, router)
        d_norm, gain_two_grad = norm_backward(mid, gains[1], d_n_two)
        d_mid = grad.astype(F32) + d_norm
        d_rel = to_rel(d_mid.astype(BF))
        d_attended = jnp.concatenate(
            [mm(d_rel[0], output_w[0][i]) + mm(d_rel[1], output_w[1][i]) for i in range(4)], -1
        ).astype(BF)
        out_grad = [mm_tn(d, attended).astype(BF) for d in d_rel]
        out_part = reduce_group([[part(g, i) for i in range(4)] for g in out_grad])
        dq, d_near, d_far = after(
            attend_back(place, queries, d_attended, kv_near, kv_far, lse, cosine, sine),
            out_part,
            *first_done,
        )
        d_kv = add(d_near, swap_c(d_far))
        d_kv = d_kv[:own] + swap_y(d_kv[own:].astype(BF)).astype(F32)
        d_kv = jnp.concatenate([turned(d_kv[:, :kv_width], -1.0), d_kv[:, kv_width:]], -1)
        d_kv = d_kv.astype(BF)
        d_n_one = mm_nt(d_kv, kv_w) + from_rel(
            [sum(mm_nt(part(dq, i), query_w[h][i]) for i in range(4)) for h in range(2)]
        )
        d_norm, gain_one_grad = norm_backward(x, gains[0], d_n_one)
        d_in = (d_mid + d_norm).astype(BF)
        pieces = (n_one, n_rel, n_two, dq, d_kv, spread_low, gain_one_grad, gain_two_grad)
        return d_in, out_part.reshape(dp, -1, part_cols), pieces

    def attn_grads(pieces):
        n_one, n_rel, n_two, dq, d_kv, spread_low, gain_one_grad, gain_two_grad = pieces
        kv_grad = mm_tn(n_one, d_kv)
        extra = jnp.concatenate(
            [
                rolled(mm_tn(n_two, spread_low)),
                gain_one_grad[:, None],
                gain_two_grad[:, None],
                jnp.zeros((width, 128 - E - 2), F32),
            ],
            -1,
        )
        small = jnp.stack(
            [
                jnp.concatenate([kv_grad[:, :kv_width], extra], -1),
                jnp.pad(kv_grad[:, kv_width:], ((0, 0), (0, 128))),
            ]
        ).astype(BF)
        small = jnp.where(first, small, small[::-1])
        small = small.reshape(2, dp, 2, 2, little, part_cols).transpose(3, 2, 0, 1, 4, 5)
        small = absolute(small)
        late = []
        for h in range(2):
            main = mm_tn(n_rel[h], dq).astype(BF)
            late.append(
                [
                    jnp.concatenate(
                        [part(main, i).reshape(dp, sh, part_cols), small[i % 2, i // 2, h]], 1
                    ).reshape(-1, part_cols)
                    for i in range(4)
                ]
            )
        return reduce_group(late).reshape(dp, -1, part_cols)

    def reduce_dp(value):
        return lax.psum_scatter(value, "dp", scatter_dimension=0, tiled=True)

    def both_batches(value_0, value_1):
        got = swap_x(jnp.where(first, value_1, value_0))
        mine = jnp.where(first, value_0, value_1)
        return jnp.where(first, jnp.stack([mine, got]), jnp.stack([got, mine]))[None, :, None]

    def to_owner(value_0, value_1):
        got = swap_x(jnp.where(first, value_1, value_0))
        mine = jnp.where(first, value_0, value_1)
        return jnp.where(first, mine, got), jnp.where(first, got, mine)

    own_cot = pick(out_cotangent, section)[0]
    own_in = pick(block_input, section)[0]

    def gather_dp(value):
        return lax.all_gather(value, "dp", axis=0, tiled=True)

    weights_0 = attn_weights(attn_parts[:, 0], cot_far, expert_shard[0])
    down_0 = gather_dp(expert_shard[0][:, 2 * cols :])
    up_0 = gather_dp(after(expert_shard[0][:, : 2 * cols], down_0))
    mid_0, n_two_0, kept_0 = forward_attention(own_in.astype(F32), weights_0, down_0)
    rows_0 = gather_chunks(n_two_0)
    weights_1 = attn_weights(attn_parts[:, 1], rows_0[3])
    down_1 = gather_dp(after(expert_shard[1][:, 2 * cols :], up_0))
    up_1 = gather_dp(after(expert_shard[1][:, : 2 * cols], down_1))
    run_0 = [experts_forward(ff, r, h, weights_0[3], up_0, down_0) for r, h in zip(rows_0, hits)]
    out_0 = (mid_0 + after(scatter_chunks([r[0] for r in run_0]), down_1)).astype(BF)

    mid_1, n_two_1, kept_1 = forward_attention(out_0.astype(F32), weights_1)
    rows_1 = gather_chunks(n_two_1)
    run_1 = [experts_forward(ff, r, h, weights_1[3], up_1, down_1) for r, h in zip(rows_1, hits)]
    back_1 = [
        experts_backward(ff, g, sums, up_1, down_1, r[1]) for g, r in zip(cot_chunks, run_1)
    ]
    summed_1 = scatter_chunks([b[0] for b in back_1])
    experts_g1 = reduce_dp(
        expert_grads(dp, rows_1, cot_chunks, [b[1] for b in back_1], [b[2] for b in back_1])
        .reshape(-1, shard)
    )
    link, out_g1, pieces_1 = backward_attention(
        own_cot, summed_1, run_1[0][1][0][:own], weights_1, kept_1
    )

    link_chunks = gather_chunks(link)
    moe_1 = after([r[0] for r in run_1], link_chunks[3])
    moe_1 = scatter_group(
        jnp.stack([m[:own] for m in moe_1]), jnp.stack([m[own:] for m in moe_1])
    )
    out_1 = (mid_1 + moe_1).astype(BF)
    late_g1 = attn_grads(after(pieces_1, link_chunks[3]))
    back_0 = [
        experts_backward(ff, g, sums, up_0, down_0, r[1]) for g, r in zip(link_chunks, run_0)
    ]
    summed_0 = scatter_chunks([b[0] for b in back_0])
    experts_g0 = reduce_dp(
        expert_grads(dp, rows_0, link_chunks, [b[1] for b in back_0], [b[2] for b in back_0])
        .reshape(-1, shard)
    )
    summed_0 = after(summed_0, late_g1)
    grad_in, out_g0, pieces_0 = backward_attention(
        link, summed_0, run_0[0][1][0][:own], weights_0, kept_0, out_1
    )
    section_outputs = both_batches(out_0, out_1)
    early = jnp.concatenate([out_g1, late_g1, out_g0], 1)
    early = reduce_dp(early.reshape(-1, part_cols))
    late_g0 = attn_grads(pieces_0)
    low_e, high_e = to_owner(experts_g0, experts_g1)
    late_g0 = reduce_dp(after(late_g0, low_e, section_outputs).reshape(-1, part_cols))

    input_grads = both_batches(grad_in, link)
    late_rows = sh + little
    low, high = to_owner(
        jnp.concatenate([early[sh + late_rows :], late_g0], 0), early[: sh + late_rows]
    )
    output_g = jnp.concatenate([low[:sh], high[:sh]], 0).astype(F32)
    query_g = jnp.concatenate([low[sh : 2 * sh], high[sh : 2 * sh]], 0).astype(F32)
    key_g = low[2 * sh :].astype(F32)
    value_g = high[2 * sh :].astype(F32)

    def split(at):
        rows = slice(at * cols, (at + 1) * cols)
        return jnp.concatenate([low_e[rows], high_e[rows]], 0).astype(F32).reshape(E, ff, shard)

    return (
        section_outputs,
        input_grads,
        key_g[:, kv_width + E][None],
        key_g[:, kv_width + E + 1][None],
        key_g[:, :kv_width][None],
        value_g[:, :kv_width][None],
        key_g[:, kv_width : kv_width + E][None],
        query_g[None],
        output_g.T[None],
        split(0).swapaxes(1, 2)[None],
        split(1).swapaxes(1, 2)[None],
        split(2)[None],
    )


def solution(mesh):
    placed = (
        P(None, "dp", "tensor", None),
        P(None, "dp", "tensor", None),
        P(None, "dp", None, None),
        P("section", ("dp", "tensor")),
        P("section", ("dp", "tensor")),
        P("section", ("dp", "tensor"), None),
        P("section", ("dp", "tensor"), None),
        P("section", ("dp", "tensor"), None),
        P("section", "dp", "tensor"),
        P("section", "tensor", "dp"),
        P("section", None, "dp", "tensor"),
        P("section", None, "dp", "tensor"),
        P("section", None, "tensor", "dp"),
    )
    return jax.shard_map(
        per_device,
        mesh=mesh,
        in_specs=placed,
        out_specs=(
            P("section", None, "dp", "tensor", None),
            P("section", None, "dp", "tensor", None),
            P("section", ("dp", "tensor")),
            P("section", ("dp", "tensor")),
            P("section", ("dp", "tensor"), None),
            P("section", ("dp", "tensor"), None),
            P("section", ("dp", "tensor"), None),
            P("section", "dp", "tensor"),
            P("section", "tensor", "dp"),
            P("section", None, "dp", "tensor"),
            P("section", None, "dp", "tensor"),
            P("section", None, "tensor", "dp"),
        ),
        check_vma=False,
    )
```

```python
import jax
import jax.numpy as jnp
from jax import lax
from jax.sharding import PartitionSpec as P

QUERY_HEADS = 12
KEY_VALUE_HEADS = 2
HEAD_SIZE = 128
TOP = 4
E = 8
EPS = 1e-06
NEG = -1e30
BF = jnp.bfloat16
F32 = jnp.float32


def dot(a, b, contract):
    return lax.dot_general(a, b, (contract, ((), ())), preferred_element_type=F32)


def mm(a, b):
    return dot(a, b, ((1,), (0,)))


def mm_nt(a, b):
    return dot(a, b, ((1,), (1,)))


def mm_tn(a, b):
    return dot(a, b, ((0,), (0,)))


def masked_softmax(logits, hit):
    logits = jnp.where(hit, logits, NEG)
    top = jnp.max(logits, -1, keepdims=True)
    exps = jnp.where(hit, jnp.exp(logits - top), 0.0)
    return exps / jnp.sum(exps, -1, keepdims=True)


def spread(gates, ff):
    count = E // 2
    lane = lax.broadcasted_iota(jnp.int32, (gates.shape[0], count * ff), 1)
    wide = jnp.broadcast_to(gates[:, count - 1][:, None], lane.shape)
    for e in range(count - 2, -1, -1):
        wide = jnp.where(lane < (e + 1) * ff, gates[:, e][:, None], wide)
    return wide


def experts_call(ff, weight, forward=None, backward=None, kept=None):
    up_w, down_w = weight
    cols = (E // 2) * ff
    outs = []
    if forward:
        rows, hit, router = forward
        gates = masked_softmax(mm(rows, router[:, :E]), hit > 0.0)
        both = mm(rows, up_w)
        pre_gate, pre_up = both[:, :cols], both[:, cols:]
    else:
        gates, pre_gate, pre_up = kept
        pre_gate, pre_up = pre_gate.astype(F32), pre_up.astype(F32)
    wide = spread(gates, ff)
    sig = jax.nn.sigmoid(pre_gate)
    active = pre_gate * sig
    hidden = active * pre_up
    gated = (hidden * wide).astype(BF)
    if forward:
        outs += [mm_nt(gated, down_w).astype(BF), gates]
        if not backward:
            outs += [pre_gate.astype(BF), pre_up.astype(BF)]
    if backward:
        grad, sums = backward
        back = mm(grad, down_w)
        tail = mm((hidden * back).astype(BF), sums)
        d_hidden = back * wide
        d_gate = (d_hidden * pre_up * (sig * (1.0 + pre_gate * (1.0 - sig)))).astype(BF)
        d_both = jnp.concatenate([d_gate, (d_hidden * active).astype(BF)], -1)
        d_rows = mm_nt(d_both, up_w).astype(BF)
        outs += [jnp.concatenate([d_rows, tail.astype(BF)], -1), d_both, gated]
    return outs


def expert_grads(rows, grads, d_both, gated):
    up = mm_tn(rows[1], d_both[1]) + mm_tn(rows[0], d_both[0])
    down = mm_tn(grads[1], gated[1]) + mm_tn(grads[0], gated[0])
    return jnp.concatenate([up.astype(BF), down.astype(BF)], -1)


def turn(value, cosine, sine):
    heads = value.reshape(value.shape[0], -1, HEAD_SIZE)
    moved = jnp.roll(heads, HEAD_SIZE // 2, -1)
    return (heads * cosine[:, None] + moved * sine[:, None]).reshape(value.shape)


def relative_heads(place, value):
    value = value.reshape(value.shape[0], 2, KEY_VALUE_HEADS, HEAD_SIZE)
    return jnp.where(place[4] == 0, value, value[:, :, ::-1])


def seen(place, own):
    key = jnp.arange(own, dtype=jnp.int32)
    key = jnp.concatenate([key + place[b] for b in range(4)])
    return key[None, :] <= jnp.arange(own, dtype=jnp.int32)[:, None]


def attend(place, q_raw, near, far, cosine, sine):
    own, width = q_raw.shape
    queries = turn(q_raw, cosine, sine).astype(BF)
    q_group = queries.reshape(own, KEY_VALUE_HEADS, -1, HEAD_SIZE)
    kv = relative_heads(place, jnp.concatenate([near, far], 0))
    scores = jnp.einsum("qgje,kge->gjqk", q_group, kv[:, 0], preferred_element_type=F32)
    scores = jnp.where(seen(place, own), scores * HEAD_SIZE ** (-0.5), NEG)
    top = jnp.max(scores, -1, keepdims=True)
    exps = jnp.exp(scores - top)
    total = jnp.sum(exps, -1, keepdims=True)
    low = lax.optimization_barrier((exps / total).astype(BF))
    attended = jnp.einsum("gjqk,kge->qgje", low, kv[:, 1], preferred_element_type=F32)
    return queries, attended.astype(BF).reshape(own, width), low


def attend_back(place, queries, attended, grad, near, far, low, cosine, sine):
    own, width = queries.shape
    q_group = queries.reshape(own, KEY_VALUE_HEADS, -1, HEAD_SIZE)
    g_group = grad.reshape(own, KEY_VALUE_HEADS, -1, HEAD_SIZE)
    kv = relative_heads(place, jnp.concatenate([near, far], 0))
    delta = jnp.sum(g_group.astype(F32) * attended.reshape(g_group.shape).astype(F32), -1)
    delta = delta.transpose(1, 2, 0)[..., None]
    d_probs = jnp.einsum("qgje,kge->gjqk", g_group, kv[:, 1], preferred_element_type=F32)
    d_scores = (low.astype(F32) * (d_probs - delta) * HEAD_SIZE ** (-0.5)).astype(BF)
    d_scores = lax.optimization_barrier(d_scores)
    d_values = jnp.einsum("gjqk,qgje->kge", low, g_group, preferred_element_type=F32)
    d_keys = jnp.einsum("gjqk,qgje->kge", d_scores, q_group, preferred_element_type=F32)
    dq = jnp.einsum("gjqk,kge->qgje", d_scores, kv[:, 0], preferred_element_type=F32)
    dq = turn(dq.reshape(own, width), cosine, -sine).astype(BF)
    d_kv = jnp.stack([d_keys, d_values], 1).astype(BF).reshape(near.shape[0] * 2, -1)
    d_kv = relative_heads(place, d_kv).reshape(d_kv.shape)
    return dq, d_kv[: near.shape[0]], d_kv[near.shape[0] :]


def swap_x(value):
    return lax.ppermute(value, "section", [(0, 1), (1, 0)])


def swap_y(value):
    return lax.ppermute(value, "tensor", [(t, t ^ 2) for t in range(4)])


def swap_c(value):
    return lax.ppermute(value, "tensor", [(t, t ^ 1) for t in range(4)])


def after(value, *first):
    return lax.optimization_barrier((value, first))[0]


def gather_chips(value):
    half = value.shape[0] // 2
    from_x = swap_x(value)
    from_y = swap_y(value)
    top = swap_x(from_y[:half])
    low = swap_y(from_x[half:])
    return jnp.stack([value, from_y, from_x, jnp.concatenate([top, low], 0)])


def add(one, two):
    return one.astype(F32) + two.astype(F32)


def scatter_chips(parts):
    half = parts.shape[1] // 2
    top = swap_x(parts[3][:half])
    low = swap_y(parts[3][half:])
    to_y = jnp.concatenate([add(parts[1][:half], top).astype(BF), parts[1][half:]], 0)
    to_x = jnp.concatenate([parts[2][:half], add(parts[2][half:], low).astype(BF)], 0)
    return parts[0].astype(F32) + swap_y(to_y).astype(F32) + swap_x(to_x).astype(F32)


def scatter_group(near, far):
    return scatter_chips(add(near, swap_c(far)).astype(BF))


def norm_forward(value, gain):
    inverse = lax.rsqrt(jnp.mean(value * value, -1, keepdims=True) + EPS)
    return value * inverse * gain


def norm_backward(value, gain, grad):
    inverse = lax.rsqrt(jnp.mean(value * value, -1, keepdims=True) + EPS)
    scaled = value * inverse
    weighted = grad * gain
    gain_grad = jnp.sum(grad * scaled, axis=0)
    return inverse * (weighted - scaled * jnp.mean(weighted * scaled, -1, keepdims=True)), gain_grad


def per_device(
    block_input,
    out_cotangent,
    routes,
    attn_gain,
    ffn_gain,
    key_projection_weight,
    value_projection_weight,
    router_weight,
    query_weight,
    output_weight,
    expert_gate,
    expert_up,
    expert_down,
):
    own = block_input.shape[2]
    width = block_input.shape[3]
    length = routes.shape[2]
    ff = expert_gate.shape[3]
    shard = expert_gate.shape[2]
    dp = width // shard
    little = attn_gain.shape[1]
    half_e = E // 2
    cols = half_e * ff
    kv_width = KEY_VALUE_HEADS * HEAD_SIZE
    part_cols = query_weight.shape[2]
    section = lax.axis_index("section")
    tensor = lax.axis_index("tensor")
    first = section == 0
    chip = tensor // 2
    core = tensor % 2

    def pick(pair, at):
        return lax.dynamic_index_in_dim(pair, at, 0, keepdims=False)

    extras = jnp.concatenate(
        [
            router_weight[0],
            attn_gain[0][:, None],
            ffn_gain[0][:, None],
            jnp.zeros((little, 128 - E - 2), BF),
        ],
        -1,
    )
    pack_q = jnp.concatenate(
        [query_weight[0], jnp.concatenate([key_projection_weight[0], extras], -1)], 0
    )
    pack_o = jnp.concatenate(
        [output_weight[0].T, jnp.pad(value_projection_weight[0], ((0, 0), (0, 128)))], 0
    )
    got = swap_x(jnp.where(first, pack_o, pack_q))
    kept = jnp.where(first, pack_q, pack_o)
    attn_shard = [jnp.where(first, kept, got), jnp.where(first, got, kept)]
    pack_rows = shard + little

    def gather_dp(value):
        return lax.all_gather(value, "dp", axis=0, tiled=True)

    attn_part_0 = gather_dp(attn_shard[0])

    def expert_pack(start):
        def across(weight):
            piece = lax.dynamic_slice_in_dim(weight[0], start, half_e, 0)
            return piece.transpose(1, 0, 2).reshape(shard, cols)

        down = lax.dynamic_slice_in_dim(expert_down[0], start, half_e, 0).reshape(cols, shard)
        return jnp.concatenate([across(expert_gate), across(expert_up), down.T], -1)

    kept_e = expert_pack(half_e * section)
    got_e = swap_x(after(expert_pack(half_e * (1 - section)), got))
    expert_shard = [jnp.where(first, kept_e, got_e), jnp.where(first, got_e, kept_e)]

    cot = jnp.where(first, out_cotangent[:, 0], out_cotangent[::-1, 0])
    cot_near = after(jnp.stack([cot, swap_y(after(cot, got))], 1), got_e, attn_part_0)
    cot_far = swap_c(cot_near)
    cot_rows = [v.reshape(4 * own, width) for v in (cot_near, cot_far)]

    def absolute(blocks):
        blocks = jnp.where(core == 0, blocks, blocks[::-1])
        return jnp.where(chip == 0, blocks, blocks[:, ::-1])

    def attn_weights(part, *first_done):
        near = gather_chips(part)
        sides = [
            side.reshape(2, 2, dp, pack_rows, part_cols)
            for side in (near, swap_c(after(near, *first_done)))
        ]
        mains, smalls = [], []
        for kind in (section, 1 - section):
            chosen = [pick(side, kind) for side in sides]
            mains.append(
                [
                    chosen[c][y, :, :shard].reshape(width, part_cols)
                    for y in range(2)
                    for c in range(2)
                ]
            )
            small = absolute(jnp.stack([c[:, :, shard:] for c in chosen]))
            smalls.append(small.transpose(2, 1, 0, 3, 4).reshape(width, part_cols))
        extra = smalls[0][:, kv_width:]
        router = jnp.concatenate([rolled(extra[:, :E]), extra[:, E:]], -1)
        kv_w = jnp.concatenate([smalls[0][:, :kv_width], smalls[1][:, :kv_width]], -1)
        gains = extra[:, E : E + 2].astype(F32).T
        return mains[0], mains[1], kv_w, router, gains

    def rolled(columns):
        return jnp.where(first, columns, jnp.roll(columns, half_e, -1))

    def hits_of(rel_core):
        pieces = []
        for rel_x in range(2):
            for rel_y in range(2):
                start = (tensor ^ (2 * rel_y + rel_core)) * own
                piece = lax.dynamic_slice(routes, (section ^ rel_x, 0, start, 0), (1, 1, own, TOP))
                pieces.append(piece.reshape(own, TOP))
        picked = jnp.concatenate(pieces, 0)
        ids = (jnp.arange(E, dtype=jnp.int32) + half_e * section) % E
        return jnp.any(picked[:, :, None] == ids[None, None, :], 1).astype(F32)

    hits = [hits_of(0), hits_of(1)]
    sums = (
        jnp.arange(cols)[:, None] // ff + half_e * section == jnp.arange(128)[None, :]
    ).astype(BF)

    halfway = HEAD_SIZE // 2
    places = (tensor * own + jnp.arange(own)).astype(F32)
    rates = 10000.0 ** (-(jnp.arange(halfway, dtype=F32) * 2.0) / HEAD_SIZE)
    angles = places[:, None] * rates[None, :]
    cosine = jnp.concatenate([jnp.cos(angles)] * 2, -1)
    sine = jnp.concatenate([-jnp.sin(angles), jnp.sin(angles)], -1)
    place = jnp.stack(
        [((tensor ^ (2 * y + c)) - tensor) * own for c in range(2) for y in range(2)]
        + [chip] * 4
    ).astype(jnp.int32)

    def turned(value, sign):
        heads = value.reshape(own, -1, HEAD_SIZE)
        moved = jnp.roll(heads, halfway, -1)
        return (heads * cosine[:, None] + sign * moved * sine[:, None]).reshape(own, -1)

    def gather_rows(value):
        near = gather_chips(value)
        return near.reshape(4 * own, width), swap_c(near).reshape(4 * own, width)

    def forward_attention(x, weights):
        query_w, output_w, kv_w, _, gains = weights
        n_one = norm_forward(x, gains[0]).astype(BF)
        q_raw = jnp.concatenate([mm(n_one, w) for w in query_w], -1)
        kv_raw = mm(n_one, kv_w)
        kv_own = jnp.concatenate([turned(kv_raw[:, :kv_width], 1.0), kv_raw[:, kv_width:]], -1)
        kv_own = kv_own.astype(BF)
        kv_near = jnp.concatenate([kv_own, swap_y(kv_own)], 0)
        kv_far = swap_c(kv_near)
        queries, attended, low = attend(place, q_raw, kv_near, kv_far, cosine, sine)
        mid = x
        for i, w in enumerate(output_w):
            mid = mid + mm_nt(attended[:, i * part_cols : (i + 1) * part_cols], w)
        n_two = norm_forward(mid, gains[1]).astype(BF)
        kept = (x, n_one, queries, kv_near, kv_far, attended, low, mid, n_two)
        return mid, n_two, kept

    def halves(value):
        return value.reshape(dp, 2, shard // 2, -1).swapaxes(0, 1)

    def by_section(pair):
        return jnp.where(first, pair, pair[::-1])

    def reduce_group(blocks):
        sides = [jnp.stack([b[s] for s in range(2) for b in side]) for side in blocks]
        return scatter_group(sides[0], sides[1]).astype(BF)

    def part(value, chip_at, core_at):
        at = (2 * chip_at + core_at) * part_cols
        return value[:, at : at + part_cols]

    def backward_attention(grad, summed, gates, weights, kept, first_done=()):
        query_w, output_w, kv_w, router, gains = weights
        x, n_one, queries, kv_near, kv_far, attended, low, mid, n_two = kept
        d_gates = rolled(summed[:, width : width + E])
        spread = gates * (d_gates - jnp.sum(gates * d_gates, -1, keepdims=True))
        spread_low = spread.astype(BF)
        router_grad = rolled(mm_tn(n_two, spread_low))
        d_n_two = summed[:, :width] + mm_nt(spread_low, router[:, :E])
        d_norm, gain_two_grad = norm_backward(mid, gains[1], d_n_two)
        d_mid = grad.astype(F32) + d_norm
        d_attn = d_mid.astype(BF)
        d_attended = jnp.concatenate([mm(d_attn, w) for w in output_w], -1).astype(BF)
        out_part = reduce_group(
            [
                [
                    by_section(halves(mm_tn(d_attn, part(attended, y, c)).astype(BF)))
                    .reshape(2, width // 2, part_cols)
                    for y in range(2)
                ]
                for c in range(2)
            ]
        )
        dq, d_near, d_far = after(
            attend_back(
                place, queries, attended, d_attended, kv_near, kv_far, low, cosine, sine
            ),
            out_part,
            first_done,
        )
        d_kv = add(d_near, swap_c(d_far))
        d_kv = d_kv[:own] + swap_y(d_kv[own:].astype(BF)).astype(F32)
        d_kv = jnp.concatenate([turned(d_kv[:, :kv_width], -1.0), d_kv[:, kv_width:]], -1)
        d_kv = d_kv.astype(BF)
        d_n_one = mm_nt(d_kv, kv_w)
        for i, w in enumerate(query_w):
            d_n_one = d_n_one + mm_nt(dq[:, i * part_cols : (i + 1) * part_cols], w)
        d_norm, gain_one_grad = norm_backward(x, gains[0], d_n_one)
        d_in = (d_mid + d_norm).astype(BF)
        pieces = (n_one, dq, d_kv, router_grad, gain_one_grad, gain_two_grad)
        return d_in, out_part.reshape(dp, -1, part_cols), pieces

    def attn_grads(pieces):
        n_one, dq, d_kv, router_grad, gain_one_grad, gain_two_grad = pieces
        kv_grad = mm_tn(n_one, d_kv)
        extra = jnp.concatenate(
            [
                router_grad,
                gain_one_grad[:, None],
                gain_two_grad[:, None],
                jnp.zeros((width, 128 - E - 2), F32),
            ],
            -1,
        )
        small = jnp.stack(
            [
                jnp.concatenate([kv_grad[:, :kv_width], extra], -1),
                jnp.pad(kv_grad[:, kv_width:], ((0, 0), (0, 128))),
            ]
        ).astype(BF)
        small = small.reshape(2, dp, 2, 2, little, part_cols).transpose(3, 2, 0, 1, 4, 5)
        small = absolute(small)
        late = []
        for c in range(2):
            side = []
            for y in range(2):
                main = halves(mm_tn(n_one, part(dq, y, c)).astype(BF))
                main = main.reshape(2, dp, shard // 2, part_cols)
                both = jnp.concatenate([main, small[c, y]], 2)
                side.append(by_section(both.reshape(2, -1, part_cols)))
            late.append(side)
        return reduce_group(late).reshape(dp, -1, part_cols)

    def reduce_dp(value):
        return lax.psum_scatter(value, "dp", scatter_dimension=0, tiled=True)

    def blocks4(value):
        return value.reshape(4, own, -1)

    def both_batches(value_0, value_1):
        got = swap_x(jnp.where(first, value_1, value_0))
        mine = jnp.where(first, value_0, value_1)
        return jnp.where(first, jnp.stack([mine, got]), jnp.stack([got, mine]))[None, :, None]

    own_cot = pick(out_cotangent, section)[0]
    own_in = pick(block_input, section)[0]

    down_0 = gather_dp(expert_shard[0][:, 2 * cols :])
    up_0 = gather_dp(after(expert_shard[0][:, : 2 * cols], down_0))
    weights_0 = attn_weights(after(attn_part_0, cot_rows[1], expert_shard[0]), down_0)
    mid_0, n_two_0, kept_0 = forward_attention(own_in.astype(F32), weights_0)
    rows_0 = gather_rows(n_two_0)
    experts_0 = (up_0, down_0)
    router_0 = weights_0[3]
    attn_part_1 = gather_dp(after(attn_shard[1], up_0))
    down_1 = gather_dp(after(expert_shard[1][:, 2 * cols :], attn_part_1))
    up_1 = gather_dp(after(expert_shard[1][:, : 2 * cols], down_1))
    experts_1 = (up_1, down_1)
    weights_1 = attn_weights(after(attn_part_1, rows_0[1]))
    far_0 = experts_call(ff, experts_0, forward=(rows_0[1], hits[1], router_0))
    near_0 = experts_call(ff, experts_0, forward=(rows_0[0], hits[0], router_0))
    moe_0 = scatter_group(blocks4(near_0[0]), blocks4(far_0[0]))
    out_0 = (mid_0 + after(moe_0, down_1)).astype(BF)

    mid_1, n_two_1, kept_1 = forward_attention(out_0.astype(F32), weights_1)
    rows_1 = gather_rows(n_two_1)
    router_1 = weights_1[3]
    far_1 = experts_call(
        ff, experts_1, forward=(rows_1[1], hits[1], router_1), backward=(cot_rows[1], sums)
    )
    near_1 = experts_call(
        ff, experts_1, forward=(rows_1[0], hits[0], router_1), backward=(cot_rows[0], sums)
    )
    summed_1 = scatter_group(blocks4(near_1[2]), blocks4(far_1[2]))
    grads_1 = expert_grads(rows_1, cot_rows, [near_1[3], far_1[3]], [near_1[4], far_1[4]])
    experts_g1 = reduce_dp(grads_1)
    link, out_g1, pieces_1 = backward_attention(
        own_cot, summed_1, near_1[1][:own], weights_1, kept_1
    )

    link_rows = gather_rows(link)
    far_b = experts_call(ff, experts_0, backward=(link_rows[1], sums), kept=far_0[1:])
    near_b = experts_call(ff, experts_0, backward=(link_rows[0], sums), kept=near_0[1:])
    late_g1 = attn_grads(after(pieces_1, link_rows[1]))
    moe_1 = after((near_1[0], far_1[0]), link_rows[1])
    out_1 = (mid_1 + scatter_group(blocks4(moe_1[0]), blocks4(moe_1[1]))).astype(BF)
    summed_0 = scatter_group(blocks4(near_b[0]), blocks4(far_b[0]))
    grads_0 = expert_grads(rows_0, link_rows, [near_b[1], far_b[1]], [near_b[2], far_b[2]])
    experts_g0 = reduce_dp(grads_0)
    summed_0 = after(summed_0, late_g1)
    grad_in, out_g0, pieces_0 = backward_attention(
        link, summed_0, near_0[1][:own], weights_0, kept_0, out_1
    )
    section_outputs = both_batches(out_0, out_1)
    early = jnp.concatenate([out_g1, late_g1, out_g0], 1)
    early = reduce_dp(early.reshape(-1, part_cols))
    late_g0 = attn_grads(pieces_0)

    def to_owner(value_0, value_1):
        got = swap_x(jnp.where(first, value_1, value_0))
        mine = jnp.where(first, value_0, value_1)
        return jnp.where(first, mine, got), jnp.where(first, got, mine)

    low_e, high_e = to_owner(experts_g0, experts_g1)
    late_g0 = reduce_dp(after(late_g0, low_e, section_outputs).reshape(-1, part_cols))

    input_grads = both_batches(grad_in, link)

    h = shard // 2
    both_parts = shard + little
    low, high = to_owner(
        jnp.concatenate([early[both_parts:], late_g0], 0), early[:both_parts]
    )
    output_g = jnp.concatenate([low[:h], high[:h]], 0).astype(F32)
    query_g = jnp.concatenate([low[h : 2 * h], high[h : 2 * h]], 0).astype(F32)
    key_g = low[2 * h :].astype(F32)
    value_g = high[2 * h :].astype(F32)
    def split(at):
        part = slice(at * cols, (at + 1) * cols)
        both = jnp.stack([low_e[:, part], high_e[:, part]], 0).astype(F32)
        return both.reshape(2, shard, half_e, ff)

    gate_g = split(0).transpose(0, 2, 1, 3).reshape(E, shard, ff)
    up_g = split(1).transpose(0, 2, 1, 3).reshape(E, shard, ff)
    down_g = split(2).transpose(0, 2, 3, 1).reshape(E, ff, shard)
    return (
        section_outputs,
        input_grads,
        key_g[:, kv_width + E][None],
        key_g[:, kv_width + E + 1][None],
        key_g[:, :kv_width][None],
        value_g[:, :kv_width][None],
        key_g[:, kv_width : kv_width + E][None],
        query_g[None],
        output_g.T[None],
        gate_g[None],
        up_g[None],
        down_g[None],
    )


def solution(mesh):
    placed = (
        P(None, "dp", "tensor", None),
        P(None, "dp", "tensor", None),
        P(None, "dp", None, None),
        P("section", ("dp", "tensor")),
        P("section", ("dp", "tensor")),
        P("section", ("dp", "tensor"), None),
        P("section", ("dp", "tensor"), None),
        P("section", ("dp", "tensor"), None),
        P("section", "dp", "tensor"),
        P("section", "tensor", "dp"),
        P("section", None, "dp", "tensor"),
        P("section", None, "dp", "tensor"),
        P("section", None, "tensor", "dp"),
    )
    return jax.shard_map(
        per_device,
        mesh=mesh,
        in_specs=placed,
        out_specs=(
            P("section", None, "dp", "tensor", None),
            P("section", None, "dp", "tensor", None),
            P("section", ("dp", "tensor")),
            P("section", ("dp", "tensor")),
            P("section", ("dp", "tensor"), None),
            P("section", ("dp", "tensor"), None),
            P("section", ("dp", "tensor"), None),
            P("section", "dp", "tensor"),
            P("section", "tensor", "dp"),
            P("section", None, "dp", "tensor"),
            P("section", None, "dp", "tensor"),
            P("section", None, "tensor", "dp"),
        ),
        check_vma=False,
    )
```

```python
import jax
import jax.numpy as jnp
from jax import lax
from jax.sharding import PartitionSpec as P

QUERY_HEADS = 12
KEY_VALUE_HEADS = 2
HEAD_SIZE = 128
TOP = 4
E = 8
EPS = 1e-06
NEG = -1e30
BF = jnp.bfloat16
F32 = jnp.float32


def dot(a, b, contract):
    return lax.dot_general(a, b, (contract, ((), ())), preferred_element_type=F32)


def mm(a, b):
    return dot(a, b, ((1,), (0,)))


def mm_nt(a, b):
    return dot(a, b, ((1,), (1,)))


def mm_tn(a, b):
    return dot(a, b, ((0,), (0,)))


def masked_softmax(logits, hit):
    logits = jnp.where(hit, logits, NEG)
    top = jnp.max(logits, -1, keepdims=True)
    exps = jnp.where(hit, jnp.exp(logits - top), 0.0)
    return exps / jnp.sum(exps, -1, keepdims=True)


def spread(gates, ff):
    count = E // 2
    lane = lax.broadcasted_iota(jnp.int32, (gates.shape[0], count * ff), 1)
    wide = jnp.broadcast_to(gates[:, count - 1][:, None], lane.shape)
    for e in range(count - 2, -1, -1):
        wide = jnp.where(lane < (e + 1) * ff, gates[:, e][:, None], wide)
    return wide


def experts_call(ff, weight, forward=None, backward=None, kept=None):
    up_w, down_w = weight
    cols = (E // 2) * ff
    outs = []
    if forward:
        rows, hit, router = forward
        gates = masked_softmax(mm(rows, router[:, :E]), hit > 0.0)
        both = mm(rows, up_w)
        pre_gate, pre_up = both[:, :cols], both[:, cols:]
    else:
        gates, pre_gate, pre_up = kept
        pre_gate, pre_up = pre_gate.astype(F32), pre_up.astype(F32)
    wide = spread(gates, ff)
    sig = jax.nn.sigmoid(pre_gate)
    active = pre_gate * sig
    hidden = active * pre_up
    gated = (hidden * wide).astype(BF)
    if forward:
        outs += [mm_nt(gated, down_w).astype(BF), gates]
        if not backward:
            outs += [pre_gate.astype(BF), pre_up.astype(BF)]
    if backward:
        grad, sums = backward
        back = mm(grad, down_w)
        tail = mm((hidden * back).astype(BF), sums)
        d_hidden = back * wide
        d_gate = (d_hidden * pre_up * (sig * (1.0 + pre_gate * (1.0 - sig)))).astype(BF)
        d_both = jnp.concatenate([d_gate, (d_hidden * active).astype(BF)], -1)
        d_rows = mm_nt(d_both, up_w).astype(BF)
        outs += [jnp.concatenate([d_rows, tail.astype(BF)], -1), d_both, gated]
    return outs


def expert_grads(rows, grads, d_both, gated):
    up = mm_tn(rows[1], d_both[1]) + mm_tn(rows[0], d_both[0])
    down = mm_tn(grads[1], gated[1]) + mm_tn(grads[0], gated[0])
    return up.astype(BF), down.astype(BF)


def turn(value, cosine, sine):
    heads = value.reshape(value.shape[0], -1, HEAD_SIZE)
    moved = jnp.roll(heads, HEAD_SIZE // 2, -1)
    return (heads * cosine[:, None] + moved * sine[:, None]).reshape(value.shape)


def relative_heads(place, value):
    value = value.reshape(value.shape[0], 2, KEY_VALUE_HEADS, HEAD_SIZE)
    return jnp.where(place[4] == 0, value, value[:, :, ::-1])


def seen(place, own):
    key = jnp.arange(own, dtype=jnp.int32)
    key = jnp.concatenate([key + place[b] for b in range(4)])
    return key[None, :] <= jnp.arange(own, dtype=jnp.int32)[:, None]


def attend(place, q_raw, near, far, cosine, sine):
    own, width = q_raw.shape
    queries = turn(q_raw, cosine, sine).astype(BF)
    q_group = queries.reshape(own, KEY_VALUE_HEADS, -1, HEAD_SIZE)
    kv = relative_heads(place, jnp.concatenate([near, far], 0))
    scores = jnp.einsum("qgje,kge->gjqk", q_group, kv[:, 0], preferred_element_type=F32)
    scores = jnp.where(seen(place, own), scores * HEAD_SIZE ** (-0.5), NEG)
    top = jnp.max(scores, -1, keepdims=True)
    exps = jnp.exp(scores - top)
    total = jnp.sum(exps, -1, keepdims=True)
    low = lax.optimization_barrier((exps / total).astype(BF))
    attended = jnp.einsum("gjqk,kge->qgje", low, kv[:, 1], preferred_element_type=F32)
    return queries, attended.astype(BF).reshape(own, width), low


def attend_back(place, queries, attended, grad, near, far, low, cosine, sine):
    own, width = queries.shape
    q_group = queries.reshape(own, KEY_VALUE_HEADS, -1, HEAD_SIZE)
    g_group = grad.reshape(own, KEY_VALUE_HEADS, -1, HEAD_SIZE)
    kv = relative_heads(place, jnp.concatenate([near, far], 0))
    delta = jnp.sum(g_group.astype(F32) * attended.reshape(g_group.shape).astype(F32), -1)
    delta = delta.transpose(1, 2, 0)[..., None]
    d_probs = jnp.einsum("qgje,kge->gjqk", g_group, kv[:, 1], preferred_element_type=F32)
    d_scores = (low.astype(F32) * (d_probs - delta) * HEAD_SIZE ** (-0.5)).astype(BF)
    d_scores = lax.optimization_barrier(d_scores)
    d_values = jnp.einsum("gjqk,qgje->kge", low, g_group, preferred_element_type=F32)
    d_keys = jnp.einsum("gjqk,qgje->kge", d_scores, q_group, preferred_element_type=F32)
    dq = jnp.einsum("gjqk,kge->qgje", d_scores, kv[:, 0], preferred_element_type=F32)
    dq = turn(dq.reshape(own, width), cosine, -sine).astype(BF)
    d_kv = jnp.stack([d_keys, d_values], 1).astype(BF).reshape(near.shape[0] * 2, -1)
    d_kv = relative_heads(place, d_kv).reshape(d_kv.shape)
    return dq, d_kv[: near.shape[0]], d_kv[near.shape[0] :]


def swap_x(value):
    return lax.ppermute(value, "section", [(0, 1), (1, 0)])


def swap_y(value):
    return lax.ppermute(value, "tensor", [(t, t ^ 2) for t in range(4)])


def swap_c(value):
    return lax.ppermute(value, "tensor", [(t, t ^ 1) for t in range(4)])


def after(value, *first):
    return lax.optimization_barrier((value, first))[0]


def gather_chips(value):
    half = value.shape[0] // 2
    from_x = swap_x(value)
    from_y = swap_y(value)
    top = swap_x(from_y[:half])
    low = swap_y(from_x[half:])
    return jnp.stack([value, from_y, from_x, jnp.concatenate([top, low], 0)])


def add(one, two):
    return one.astype(F32) + two.astype(F32)


def scatter_chips(parts):
    half = parts.shape[1] // 2
    top = swap_x(parts[3][:half])
    low = swap_y(parts[3][half:])
    to_y = jnp.concatenate([add(parts[1][:half], top).astype(BF), parts[1][half:]], 0)
    to_x = jnp.concatenate([parts[2][:half], add(parts[2][half:], low).astype(BF)], 0)
    return parts[0].astype(F32) + swap_y(to_y).astype(F32) + swap_x(to_x).astype(F32)


def scatter_group(near, far):
    return scatter_chips(add(near, swap_c(far)).astype(BF))


def norm_forward(value, gain):
    inverse = lax.rsqrt(jnp.mean(value * value, -1, keepdims=True) + EPS)
    return value * inverse * gain


def norm_backward(value, gain, grad):
    inverse = lax.rsqrt(jnp.mean(value * value, -1, keepdims=True) + EPS)
    scaled = value * inverse
    weighted = grad * gain
    gain_grad = jnp.sum(grad * scaled, axis=0)
    return inverse * (weighted - scaled * jnp.mean(weighted * scaled, -1, keepdims=True)), gain_grad


def per_device(
    block_input,
    out_cotangent,
    routes,
    attn_gain,
    ffn_gain,
    key_projection_weight,
    value_projection_weight,
    router_weight,
    query_weight,
    output_weight,
    expert_gate,
    expert_up,
    expert_down,
):
    own = block_input.shape[2]
    width = block_input.shape[3]
    length = routes.shape[2]
    ff = expert_gate.shape[3]
    shard = expert_gate.shape[2]
    dp = width // shard
    little = attn_gain.shape[1]
    half_e = E // 2
    cols = half_e * ff
    kv_width = KEY_VALUE_HEADS * HEAD_SIZE
    part_cols = query_weight.shape[2]
    section = lax.axis_index("section")
    tensor = lax.axis_index("tensor")
    first = section == 0
    chip = tensor // 2
    core = tensor % 2

    def pick(pair, at):
        return lax.dynamic_index_in_dim(pair, at, 0, keepdims=False)

    extras = jnp.concatenate(
        [
            router_weight[0],
            attn_gain[0][:, None],
            ffn_gain[0][:, None],
            jnp.zeros((little, 128 - E - 2), BF),
        ],
        -1,
    )
    pack_q = jnp.concatenate(
        [query_weight[0], jnp.concatenate([key_projection_weight[0], extras], -1)], 0
    )
    pack_o = jnp.concatenate(
        [output_weight[0].T, jnp.pad(value_projection_weight[0], ((0, 0), (0, 128)))], 0
    )
    got = swap_x(jnp.where(first, pack_o, pack_q))
    kept = jnp.where(first, pack_q, pack_o)
    attn_shard = [jnp.where(first, kept, got), jnp.where(first, got, kept)]
    pack_rows = shard + little

    def gather_dp(value):
        return lax.all_gather(value, "dp", axis=0, tiled=True)

    attn_part_0 = gather_dp(attn_shard[0])

    def expert_pack(start):
        def across(weight):
            piece = lax.dynamic_slice_in_dim(weight[0], start, half_e, 0)
            return piece.transpose(1, 0, 2).reshape(shard, cols)

        down = lax.dynamic_slice_in_dim(expert_down[0], start, half_e, 0).reshape(cols, shard)
        return jnp.concatenate([across(expert_gate), across(expert_up), down.T], -1)

    kept_e = expert_pack(half_e * section)
    got_e = swap_x(after(expert_pack(half_e * (1 - section)), got))
    expert_shard = [jnp.where(first, kept_e, got_e), jnp.where(first, got_e, kept_e)]

    cot = jnp.where(first, out_cotangent[:, 0], out_cotangent[::-1, 0])
    cot_near = after(jnp.stack([cot, swap_y(after(cot, got))], 1), got_e, attn_part_0)
    cot_far = swap_c(cot_near)
    cot_rows = [v.reshape(4 * own, width) for v in (cot_near, cot_far)]

    def absolute(blocks):
        blocks = jnp.where(core == 0, blocks, blocks[::-1])
        return jnp.where(chip == 0, blocks, blocks[:, ::-1])

    def attn_weights(part, *first_done):
        near = gather_chips(part)
        sides = [
            side.reshape(2, 2, dp, pack_rows, part_cols)
            for side in (near, swap_c(after(near, *first_done)))
        ]
        mains, smalls = [], []
        for kind in (section, 1 - section):
            chosen = [pick(side, kind) for side in sides]
            mains.append(
                [
                    chosen[c][y, :, :shard].reshape(width, part_cols)
                    for y in range(2)
                    for c in range(2)
                ]
            )
            small = absolute(jnp.stack([c[:, :, shard:] for c in chosen]))
            smalls.append(small.transpose(2, 1, 0, 3, 4).reshape(width, part_cols))
        extra = smalls[0][:, kv_width:]
        router = jnp.concatenate([rolled(extra[:, :E]), extra[:, E:]], -1)
        kv_w = jnp.concatenate([smalls[0][:, :kv_width], smalls[1][:, :kv_width]], -1)
        gains = extra[:, E : E + 2].astype(F32).T
        return mains[0], mains[1], kv_w, router, gains

    def rolled(columns):
        return jnp.where(first, columns, jnp.roll(columns, half_e, -1))

    def hits_of(rel_core):
        pieces = []
        for rel_x in range(2):
            for rel_y in range(2):
                start = (tensor ^ (2 * rel_y + rel_core)) * own
                piece = lax.dynamic_slice(routes, (section ^ rel_x, 0, start, 0), (1, 1, own, TOP))
                pieces.append(piece.reshape(own, TOP))
        picked = jnp.concatenate(pieces, 0)
        ids = (jnp.arange(E, dtype=jnp.int32) + half_e * section) % E
        return jnp.any(picked[:, :, None] == ids[None, None, :], 1).astype(F32)

    hits = [hits_of(0), hits_of(1)]
    sums = (
        jnp.arange(cols)[:, None] // ff + half_e * section == jnp.arange(128)[None, :]
    ).astype(BF)

    halfway = HEAD_SIZE // 2
    places = (tensor * own + jnp.arange(own)).astype(F32)
    rates = 10000.0 ** (-(jnp.arange(halfway, dtype=F32) * 2.0) / HEAD_SIZE)
    angles = places[:, None] * rates[None, :]
    cosine = jnp.concatenate([jnp.cos(angles)] * 2, -1)
    sine = jnp.concatenate([-jnp.sin(angles), jnp.sin(angles)], -1)
    place = jnp.stack(
        [((tensor ^ (2 * y + c)) - tensor) * own for c in range(2) for y in range(2)]
        + [chip] * 4
    ).astype(jnp.int32)

    def turned(value, sign):
        heads = value.reshape(own, -1, HEAD_SIZE)
        moved = jnp.roll(heads, halfway, -1)
        return (heads * cosine[:, None] + sign * moved * sine[:, None]).reshape(own, -1)

    def gather_rows(value):
        near = gather_chips(value)
        return near.reshape(4 * own, width), swap_c(near).reshape(4 * own, width)

    def forward_attention(x, weights):
        query_w, output_w, kv_w, _, gains = weights
        n_one = norm_forward(x, gains[0]).astype(BF)
        q_raw = jnp.concatenate([mm(n_one, w) for w in query_w], -1)
        kv_raw = mm(n_one, kv_w)
        kv_own = jnp.concatenate([turned(kv_raw[:, :kv_width], 1.0), kv_raw[:, kv_width:]], -1)
        kv_own = kv_own.astype(BF)
        kv_near = jnp.concatenate([kv_own, swap_y(kv_own)], 0)
        kv_far = swap_c(kv_near)
        queries, attended, low = attend(place, q_raw, kv_near, kv_far, cosine, sine)
        mid = x
        for i, w in enumerate(output_w):
            mid = mid + mm_nt(attended[:, i * part_cols : (i + 1) * part_cols], w)
        n_two = norm_forward(mid, gains[1]).astype(BF)
        kept = (x, n_one, queries, kv_near, kv_far, attended, low, mid, n_two)
        return mid, n_two, kept

    def halves(value):
        return value.reshape(dp, 2, shard // 2, -1).swapaxes(0, 1)

    def by_section(pair):
        return jnp.where(first, pair, pair[::-1])

    def reduce_group(blocks):
        sides = [jnp.stack([b[s] for s in range(2) for b in side]) for side in blocks]
        return scatter_group(sides[0], sides[1]).astype(BF)

    def part(value, chip_at, core_at):
        at = (2 * chip_at + core_at) * part_cols
        return value[:, at : at + part_cols]

    def backward_attention(grad, summed, gates, weights, kept, first_done=()):
        query_w, output_w, kv_w, router, gains = weights
        x, n_one, queries, kv_near, kv_far, attended, low, mid, n_two = kept
        d_gates = rolled(summed[:, width : width + E])
        spread = gates * (d_gates - jnp.sum(gates * d_gates, -1, keepdims=True))
        spread_low = spread.astype(BF)
        router_grad = rolled(mm_tn(n_two, spread_low))
        d_n_two = summed[:, :width] + mm_nt(spread_low, router[:, :E])
        d_norm, gain_two_grad = norm_backward(mid, gains[1], d_n_two)
        d_mid = grad.astype(F32) + d_norm
        d_attn = d_mid.astype(BF)
        d_attended = jnp.concatenate([mm(d_attn, w) for w in output_w], -1).astype(BF)
        out_part = reduce_group(
            [
                [
                    by_section(halves(mm_tn(d_attn, part(attended, y, c)).astype(BF)))
                    .reshape(2, width // 2, part_cols)
                    for y in range(2)
                ]
                for c in range(2)
            ]
        )
        dq, d_near, d_far = after(
            attend_back(
                place, queries, attended, d_attended, kv_near, kv_far, low, cosine, sine
            ),
            out_part,
            first_done,
        )
        d_kv = add(d_near, swap_c(d_far))
        d_kv = d_kv[:own] + swap_y(d_kv[own:].astype(BF)).astype(F32)
        d_kv = jnp.concatenate([turned(d_kv[:, :kv_width], -1.0), d_kv[:, kv_width:]], -1)
        d_kv = d_kv.astype(BF)
        d_n_one = mm_nt(d_kv, kv_w)
        for i, w in enumerate(query_w):
            d_n_one = d_n_one + mm_nt(dq[:, i * part_cols : (i + 1) * part_cols], w)
        d_norm, gain_one_grad = norm_backward(x, gains[0], d_n_one)
        d_in = (d_mid + d_norm).astype(BF)
        pieces = (n_one, dq, d_kv, router_grad, gain_one_grad, gain_two_grad)
        return d_in, out_part.reshape(dp, -1, part_cols), pieces

    def attn_grads(pieces):
        n_one, dq, d_kv, router_grad, gain_one_grad, gain_two_grad = pieces
        kv_grad = mm_tn(n_one, d_kv)
        extra = jnp.concatenate(
            [
                router_grad,
                gain_one_grad[:, None],
                gain_two_grad[:, None],
                jnp.zeros((width, 128 - E - 2), F32),
            ],
            -1,
        )
        small = jnp.stack(
            [
                jnp.concatenate([kv_grad[:, :kv_width], extra], -1),
                jnp.pad(kv_grad[:, kv_width:], ((0, 0), (0, 128))),
            ]
        ).astype(BF)
        small = small.reshape(2, dp, 2, 2, little, part_cols).transpose(3, 2, 0, 1, 4, 5)
        small = absolute(small)
        late = []
        for c in range(2):
            side = []
            for y in range(2):
                main = halves(mm_tn(n_one, part(dq, y, c)).astype(BF))
                main = main.reshape(2, dp, shard // 2, part_cols)
                both = jnp.concatenate([main, small[c, y]], 2)
                side.append(by_section(both.reshape(2, -1, part_cols)))
            late.append(side)
        return reduce_group(late).reshape(dp, -1, part_cols)

    def reduce_dp(value):
        return lax.psum_scatter(value, "dp", scatter_dimension=0, tiled=True)

    def blocks4(value):
        return value.reshape(4, own, -1)

    def both_batches(value_0, value_1):
        got = swap_x(jnp.where(first, value_1, value_0))
        mine = jnp.where(first, value_0, value_1)
        return jnp.where(first, jnp.stack([mine, got]), jnp.stack([got, mine]))[None, :, None]

    own_cot = pick(out_cotangent, section)[0]
    own_in = pick(block_input, section)[0]

    down_0 = gather_dp(expert_shard[0][:, 2 * cols :])
    up_0 = gather_dp(after(expert_shard[0][:, : 2 * cols], down_0))
    weights_0 = attn_weights(after(attn_part_0, cot_rows[1], expert_shard[0]), down_0)
    mid_0, n_two_0, kept_0 = forward_attention(own_in.astype(F32), weights_0)
    rows_0 = gather_rows(n_two_0)
    experts_0 = (up_0, down_0)
    router_0 = weights_0[3]
    attn_part_1 = gather_dp(after(attn_shard[1], up_0))
    down_1 = gather_dp(after(expert_shard[1][:, 2 * cols :], attn_part_1))
    up_1 = gather_dp(after(expert_shard[1][:, : 2 * cols], down_1))
    experts_1 = (up_1, down_1)
    far_0 = experts_call(ff, experts_0, forward=(rows_0[1], hits[1], router_0))
    near_0 = experts_call(ff, experts_0, forward=(rows_0[0], hits[0], router_0))
    weights_1 = attn_weights(after(attn_part_1, far_0[0]))
    moe_0 = scatter_group(blocks4(near_0[0]), blocks4(far_0[0]))
    out_0 = (mid_0 + after(moe_0, down_1)).astype(BF)

    mid_1, n_two_1, kept_1 = forward_attention(out_0.astype(F32), weights_1)
    rows_1 = gather_rows(n_two_1)
    router_1 = weights_1[3]
    far_1 = experts_call(
        ff, experts_1, forward=(rows_1[1], hits[1], router_1), backward=(cot_rows[1], sums)
    )
    near_1 = experts_call(
        ff, experts_1, forward=(rows_1[0], hits[0], router_1), backward=(cot_rows[0], sums)
    )
    summed_1 = scatter_group(blocks4(near_1[2]), blocks4(far_1[2]))
    back_1 = after((near_1[3:], far_1[3:]), near_1[2], far_1[2])
    grads_1 = expert_grads(rows_1, cot_rows, *zip(*back_1))
    experts_g1 = [reduce_dp(g) for g in grads_1]
    link, out_g1, pieces_1 = backward_attention(
        own_cot, summed_1, near_1[1][:own], weights_1, kept_1
    )

    link_rows = gather_rows(link)
    far_b = experts_call(ff, experts_0, backward=(link_rows[1], sums), kept=far_0[1:])
    near_b = experts_call(ff, experts_0, backward=(link_rows[0], sums), kept=near_0[1:])
    moe_1 = after((near_1[0], far_1[0]), link_rows[1])
    out_1 = (mid_1 + scatter_group(blocks4(moe_1[0]), blocks4(moe_1[1]))).astype(BF)
    near_d, far_d = after((near_b[0], far_b[0]), out_1)
    summed_0 = scatter_group(blocks4(near_d), blocks4(far_d))
    back_0 = after((near_b[1:], far_b[1:]), near_d, far_d)
    grads_0 = expert_grads(rows_0, link_rows, *zip(*back_0))
    experts_g0 = [reduce_dp(g) for g in grads_0]
    late_g1 = attn_grads(after(pieces_1, summed_0))
    grad_in, out_g0, pieces_0 = backward_attention(
        link, summed_0, near_0[1][:own], weights_0, kept_0, late_g1
    )
    section_outputs = both_batches(out_0, out_1)
    early = jnp.concatenate([out_g1, late_g1, out_g0], 1)
    early = reduce_dp(early.reshape(-1, part_cols))

    def to_owner(value_0, value_1):
        got = swap_x(jnp.where(first, value_1, value_0))
        mine = jnp.where(first, value_0, value_1)
        return jnp.where(first, mine, got), jnp.where(first, got, mine)

    low_up, high_up = to_owner(experts_g0[0], experts_g1[0])
    low_down, high_down = to_owner(experts_g0[1], experts_g1[1])
    late_g0 = attn_grads(after(pieces_0, low_up, low_down, section_outputs))
    late_g0 = reduce_dp(late_g0.reshape(-1, part_cols))

    input_grads = both_batches(after(grad_in, early), link)

    h = shard // 2
    both_parts = shard + little
    low, high = to_owner(
        jnp.concatenate([early[both_parts:], late_g0], 0), early[:both_parts]
    )
    output_g = jnp.concatenate([low[:h], high[:h]], 0).astype(F32)
    query_g = jnp.concatenate([low[h : 2 * h], high[h : 2 * h]], 0).astype(F32)
    key_g = low[2 * h :].astype(F32)
    value_g = high[2 * h :].astype(F32)
    def split(low_part, high_part):
        both = jnp.stack([low_part, high_part], 0).astype(F32)
        return both.reshape(2, shard, half_e, ff)

    gate_g = split(low_up[:, :cols], high_up[:, :cols]).transpose(0, 2, 1, 3)
    gate_g = gate_g.reshape(E, shard, ff)
    up_g = split(low_up[:, cols:], high_up[:, cols:]).transpose(0, 2, 1, 3)
    up_g = up_g.reshape(E, shard, ff)
    down_g = split(low_down, high_down).transpose(0, 2, 3, 1).reshape(E, ff, shard)
    return (
        section_outputs,
        input_grads,
        key_g[:, kv_width + E][None],
        key_g[:, kv_width + E + 1][None],
        key_g[:, :kv_width][None],
        value_g[:, :kv_width][None],
        key_g[:, kv_width : kv_width + E][None],
        query_g[None],
        output_g.T[None],
        gate_g[None],
        up_g[None],
        down_g[None],
    )


def solution(mesh):
    placed = (
        P(None, "dp", "tensor", None),
        P(None, "dp", "tensor", None),
        P(None, "dp", None, None),
        P("section", ("dp", "tensor")),
        P("section", ("dp", "tensor")),
        P("section", ("dp", "tensor"), None),
        P("section", ("dp", "tensor"), None),
        P("section", ("dp", "tensor"), None),
        P("section", "dp", "tensor"),
        P("section", "tensor", "dp"),
        P("section", None, "dp", "tensor"),
        P("section", None, "dp", "tensor"),
        P("section", None, "tensor", "dp"),
    )
    return jax.shard_map(
        per_device,
        mesh=mesh,
        in_specs=placed,
        out_specs=(
            P("section", None, "dp", "tensor", None),
            P("section", None, "dp", "tensor", None),
            P("section", ("dp", "tensor")),
            P("section", ("dp", "tensor")),
            P("section", ("dp", "tensor"), None),
            P("section", ("dp", "tensor"), None),
            P("section", ("dp", "tensor"), None),
            P("section", "dp", "tensor"),
            P("section", "tensor", "dp"),
            P("section", None, "dp", "tensor"),
            P("section", None, "dp", "tensor"),
            P("section", None, "tensor", "dp"),
        ),
        check_vma=False,
    )
```

```python
import jax
import jax.numpy as jnp
from jax import lax
from jax.sharding import PartitionSpec as P

QUERY_HEADS = 12
KEY_VALUE_HEADS = 2
HEAD_SIZE = 128
TOP = 4
E = 8
EPS = 1e-06
NEG = -1e30
BF = jnp.bfloat16
F32 = jnp.float32


def dot(a, b, contract):
    return lax.dot_general(a, b, (contract, ((), ())), preferred_element_type=F32)


def mm(a, b):
    return dot(a, b, ((1,), (0,)))


def mm_nt(a, b):
    return dot(a, b, ((1,), (1,)))


def mm_tn(a, b):
    return dot(a, b, ((0,), (0,)))


def masked_softmax(logits, hit):
    logits = jnp.where(hit, logits, NEG)
    top = jnp.max(logits, -1, keepdims=True)
    exps = jnp.where(hit, jnp.exp(logits - top), 0.0)
    return exps / jnp.sum(exps, -1, keepdims=True)


def spread(gates, ff):
    count = E // 2
    lane = lax.broadcasted_iota(jnp.int32, (gates.shape[0], count * ff), 1)
    wide = jnp.broadcast_to(gates[:, count - 1][:, None], lane.shape)
    for e in range(count - 2, -1, -1):
        wide = jnp.where(lane < (e + 1) * ff, gates[:, e][:, None], wide)
    return wide


def experts_call(ff, weight, forward=None, backward=None, kept=None):
    up_w, down_w = weight
    cols = (E // 2) * ff
    outs = []
    if forward:
        rows, hit, router = forward
        gates = masked_softmax(mm(rows, router[:, :E]), hit > 0.0)
        both = mm(rows, up_w)
        pre_gate, pre_up = both[:, :cols], both[:, cols:]
    else:
        gates, pre_gate, pre_up = kept
        pre_gate, pre_up = pre_gate.astype(F32), pre_up.astype(F32)
    wide = spread(gates, ff)
    sig = jax.nn.sigmoid(pre_gate)
    active = pre_gate * sig
    hidden = active * pre_up
    gated = (hidden * wide).astype(BF)
    if forward:
        outs += [mm_nt(gated, down_w).astype(BF), gates]
        if not backward:
            outs += [pre_gate.astype(BF), pre_up.astype(BF)]
    if backward:
        grad, sums = backward
        back = mm(grad, down_w)
        tail = mm((hidden * back).astype(BF), sums)
        d_hidden = back * wide
        d_gate = (d_hidden * pre_up * (sig * (1.0 + pre_gate * (1.0 - sig)))).astype(BF)
        d_both = jnp.concatenate([d_gate, (d_hidden * active).astype(BF)], -1)
        d_rows = mm_nt(d_both, up_w).astype(BF)
        outs += [jnp.concatenate([d_rows, tail.astype(BF)], -1), d_both, gated]
    return outs


def expert_grads(rows, grads, d_both, gated):
    up = mm_tn(rows[1], d_both[1]) + mm_tn(rows[0], d_both[0])
    down = mm_tn(grads[1], gated[1]) + mm_tn(grads[0], gated[0])
    return up.astype(BF), down.astype(BF)


def turn(value, cosine, sine):
    heads = value.reshape(value.shape[0], -1, HEAD_SIZE)
    moved = jnp.roll(heads, HEAD_SIZE // 2, -1)
    return (heads * cosine[:, None] + moved * sine[:, None]).reshape(value.shape)


def swapped(place, pair):
    one, two = pair
    return jnp.where(place[4] == 0, one, two), jnp.where(place[4] == 0, two, one)


def kv_heads(place, near, far):
    kv = jnp.concatenate([near, far], 0)
    parts = [kv[:, i * HEAD_SIZE : (i + 1) * HEAD_SIZE] for i in range(2 * KEY_VALUE_HEADS)]
    return swapped(place, parts[:KEY_VALUE_HEADS]), swapped(place, parts[KEY_VALUE_HEADS:])


def seen(place, own):
    key = jnp.arange(own, dtype=jnp.int32)
    key = jnp.concatenate([key + place[b] for b in range(4)])
    return key[None, :] <= jnp.arange(own, dtype=jnp.int32)[:, None]


def head_groups(value):
    value = value.reshape(value.shape[0], KEY_VALUE_HEADS, -1, HEAD_SIZE)
    return [value[:, g] for g in range(KEY_VALUE_HEADS)]


def attend(place, q_raw, near, far, cosine, sine):
    own, width = q_raw.shape
    queries = turn(q_raw, cosine, sine).astype(BF)
    keys, values = kv_heads(place, near, far)
    lows, outs = [], []
    for query, key, value in zip(head_groups(queries), keys, values):
        scores = jnp.einsum("qje,ke->jqk", query, key, preferred_element_type=F32)
        scores = jnp.where(seen(place, own), scores * HEAD_SIZE ** (-0.5), NEG)
        top = jnp.max(scores, -1, keepdims=True)
        exps = jnp.exp(scores - top)
        total = jnp.sum(exps, -1, keepdims=True)
        low = lax.optimization_barrier((exps / total).astype(BF))
        outs.append(jnp.einsum("jqk,ke->qje", low, value, preferred_element_type=F32).astype(BF))
        lows.append(low)
    return queries, jnp.stack(outs, 1).reshape(own, width), lows


def attend_back(place, queries, attended, grad, near, far, lows, cosine, sine):
    own, width = queries.shape
    keys, values = kv_heads(place, near, far)
    d_keys, d_values, d_query = [], [], []
    for query, out, g, low, key, value in zip(
        head_groups(queries), head_groups(attended), head_groups(grad), lows, keys, values
    ):
        delta = jnp.sum(g.astype(F32) * out.astype(F32), -1).T[..., None]
        d_probs = jnp.einsum("qje,ke->jqk", g, value, preferred_element_type=F32)
        d_scores = (low.astype(F32) * (d_probs - delta) * HEAD_SIZE ** (-0.5)).astype(BF)
        d_scores = lax.optimization_barrier(d_scores)
        d_values.append(jnp.einsum("jqk,qje->ke", low, g, preferred_element_type=F32))
        d_keys.append(jnp.einsum("jqk,qje->ke", d_scores, query, preferred_element_type=F32))
        d_query.append(jnp.einsum("jqk,ke->qje", d_scores, key, preferred_element_type=F32))
    dq = turn(jnp.stack(d_query, 1).reshape(own, width), cosine, -sine).astype(BF)
    d_kv = jnp.concatenate(swapped(place, d_keys) + swapped(place, d_values), -1).astype(BF)
    return dq, d_kv[: near.shape[0]], d_kv[near.shape[0] :]


def swap_x(value):
    return lax.ppermute(value, "section", [(0, 1), (1, 0)])


def swap_y(value):
    return lax.ppermute(value, "tensor", [(t, t ^ 2) for t in range(4)])


def swap_c(value):
    return lax.ppermute(value, "tensor", [(t, t ^ 1) for t in range(4)])


def after(value, *first):
    return lax.optimization_barrier((value, first))[0]


def gather_chips(value):
    half = value.shape[0] // 2
    from_x = swap_x(value)
    from_y = swap_y(value)
    top = swap_x(from_y[:half])
    low = swap_y(from_x[half:])
    return jnp.stack([value, from_y, from_x, jnp.concatenate([top, low], 0)])


def add(one, two):
    return one.astype(F32) + two.astype(F32)


def scatter_chips(parts):
    half = parts.shape[1] // 2
    top = swap_x(parts[3][:half])
    low = swap_y(parts[3][half:])
    to_y = jnp.concatenate([add(parts[1][:half], top).astype(BF), parts[1][half:]], 0)
    to_x = jnp.concatenate([parts[2][:half], add(parts[2][half:], low).astype(BF)], 0)
    return parts[0].astype(F32) + swap_y(to_y).astype(F32) + swap_x(to_x).astype(F32)


def scatter_group(near, far):
    return scatter_chips(add(near, swap_c(far)).astype(BF))


def norm_forward(value, gain):
    inverse = lax.rsqrt(jnp.mean(value * value, -1, keepdims=True) + EPS)
    return value * inverse * gain


def norm_backward(value, gain, grad):
    inverse = lax.rsqrt(jnp.mean(value * value, -1, keepdims=True) + EPS)
    scaled = value * inverse
    weighted = grad * gain
    gain_grad = (grad * scaled).astype(BF)
    return inverse * (weighted - scaled * jnp.mean(weighted * scaled, -1, keepdims=True)), gain_grad


def per_device(
    block_input,
    out_cotangent,
    routes,
    attn_gain,
    ffn_gain,
    key_projection_weight,
    value_projection_weight,
    router_weight,
    query_weight,
    output_weight,
    expert_gate,
    expert_up,
    expert_down,
):
    own = block_input.shape[2]
    width = block_input.shape[3]
    length = routes.shape[2]
    ff = expert_gate.shape[3]
    shard = expert_gate.shape[2]
    dp = width // shard
    little = attn_gain.shape[1]
    half_e = E // 2
    cols = half_e * ff
    kv_width = KEY_VALUE_HEADS * HEAD_SIZE
    part_cols = query_weight.shape[2]
    section = lax.axis_index("section")
    tensor = lax.axis_index("tensor")
    first = section == 0
    chip = tensor // 2
    core = tensor % 2

    def pick(pair, at):
        return lax.dynamic_index_in_dim(pair, at, 0, keepdims=False)

    extras = jnp.concatenate(
        [
            router_weight[0],
            attn_gain[0][:, None],
            ffn_gain[0][:, None],
            jnp.zeros((little, 128 - E - 2), BF),
        ],
        -1,
    )
    pack_q = jnp.concatenate(
        [query_weight[0], jnp.concatenate([key_projection_weight[0], extras], -1)], 0
    )
    pack_o = jnp.concatenate(
        [output_weight[0].T, jnp.pad(value_projection_weight[0], ((0, 0), (0, 128)))], 0
    )
    got = swap_x(jnp.where(first, pack_o, pack_q))
    kept = jnp.where(first, pack_q, pack_o)
    attn_shard = [jnp.where(first, kept, got), jnp.where(first, got, kept)]
    pack_rows = shard + little

    def gather_dp(value):
        return lax.all_gather(value, "dp", axis=0, tiled=True)

    attn_part_0 = gather_dp(attn_shard[0])

    def expert_pack(start):
        def across(weight):
            piece = lax.dynamic_slice_in_dim(weight[0], start, half_e, 0)
            return piece.transpose(1, 0, 2).reshape(shard, cols)

        down = lax.dynamic_slice_in_dim(expert_down[0], start, half_e, 0).reshape(cols, shard)
        return jnp.concatenate([across(expert_gate), across(expert_up), down.T], -1)

    kept_e = expert_pack(half_e * section)
    got_e = swap_x(after(expert_pack(half_e * (1 - section)), got))
    expert_shard = [jnp.where(first, kept_e, got_e), jnp.where(first, got_e, kept_e)]

    cot = jnp.where(first, out_cotangent[:, 0], out_cotangent[::-1, 0])
    cot_near = after(jnp.stack([cot, swap_y(after(cot, got))], 1), got_e, attn_part_0)
    cot_far = swap_c(cot_near)
    cot_rows = [v.reshape(4 * own, width) for v in (cot_near, cot_far)]

    def absolute(blocks):
        blocks = jnp.where(core == 0, blocks, blocks[::-1])
        return jnp.where(chip == 0, blocks, blocks[:, ::-1])

    def attn_gather(part, *first_done):
        near = gather_chips(part)
        return near, swap_c(after(near, *first_done))

    def attn_weights(sides):
        sides = [side.reshape(2, 2, dp, pack_rows, part_cols) for side in sides]
        mains, smalls = [], []
        for kind in (section, 1 - section):
            chosen = [pick(side, kind) for side in sides]
            mains.append(
                [
                    chosen[c][y, :, :shard].reshape(width, part_cols)
                    for y in range(2)
                    for c in range(2)
                ]
            )
            small = absolute(jnp.stack([c[:, :, shard:] for c in chosen]))
            smalls.append(small.transpose(2, 1, 0, 3, 4).reshape(width, part_cols))
        extra = smalls[0][:, kv_width:]
        router = jnp.concatenate([rolled(extra[:, :E]), extra[:, E:]], -1)
        kv_w = jnp.concatenate([smalls[0][:, :kv_width], smalls[1][:, :kv_width]], -1)
        gains = extra[:, E : E + 2].astype(F32).T
        return mains[0], mains[1], kv_w, router, gains

    def rolled(columns):
        return jnp.where(first, columns, jnp.roll(columns, half_e, -1))

    def hits_of(rel_core):
        pieces = []
        for rel_x in range(2):
            for rel_y in range(2):
                start = (tensor ^ (2 * rel_y + rel_core)) * own
                piece = lax.dynamic_slice(routes, (section ^ rel_x, 0, start, 0), (1, 1, own, TOP))
                pieces.append(piece.reshape(own, TOP))
        picked = jnp.concatenate(pieces, 0)
        ids = (jnp.arange(E, dtype=jnp.int32) + half_e * section) % E
        return jnp.any(picked[:, :, None] == ids[None, None, :], 1).astype(F32)

    hits = [hits_of(0), hits_of(1)]
    sums = (
        jnp.arange(cols)[:, None] // ff + half_e * section == jnp.arange(128)[None, :]
    ).astype(BF)

    halfway = HEAD_SIZE // 2
    places = (tensor * own + jnp.arange(own)).astype(F32)
    rates = 10000.0 ** (-(jnp.arange(halfway, dtype=F32) * 2.0) / HEAD_SIZE)
    angles = places[:, None] * rates[None, :]
    cosine = jnp.concatenate([jnp.cos(angles)] * 2, -1)
    sine = jnp.concatenate([-jnp.sin(angles), jnp.sin(angles)], -1)
    place = jnp.stack(
        [((tensor ^ (2 * y + c)) - tensor) * own for c in range(2) for y in range(2)]
        + [chip] * 4
    ).astype(jnp.int32)

    def turned(value, sign):
        heads = value.reshape(own, -1, HEAD_SIZE)
        moved = jnp.roll(heads, halfway, -1)
        return (heads * cosine[:, None] + sign * moved * sine[:, None]).reshape(own, -1)

    def gather_rows(value):
        near = gather_chips(value)
        return near.reshape(4 * own, width), swap_c(near).reshape(4 * own, width)

    def forward_attention(x, weights):
        query_w, output_w, kv_w, _, gains = weights
        n_one = norm_forward(x, gains[0]).astype(BF)
        q_raw = jnp.concatenate([mm(n_one, w) for w in query_w], -1)
        kv_raw = mm(n_one, kv_w)
        kv_own = jnp.concatenate([turned(kv_raw[:, :kv_width], 1.0), kv_raw[:, kv_width:]], -1)
        kv_own = kv_own.astype(BF)
        kv_near = jnp.concatenate([kv_own, swap_y(kv_own)], 0)
        kv_far = swap_c(kv_near)
        queries, attended, low = attend(place, q_raw, kv_near, kv_far, cosine, sine)
        mid = x
        for i, w in enumerate(output_w):
            mid = mid + mm_nt(attended[:, i * part_cols : (i + 1) * part_cols], w)
        n_two = norm_forward(mid, gains[1]).astype(BF)
        kept = (x, n_one, queries, kv_near, kv_far, attended, low, mid, n_two)
        return mid, n_two, kept

    def halves(value):
        return value.reshape(dp, 2, shard // 2, -1).swapaxes(0, 1)

    def by_section(pair):
        return jnp.where(first, pair, pair[::-1])

    def reduce_group(blocks):
        sides = [jnp.stack([b[s] for s in range(2) for b in side]) for side in blocks]
        return scatter_group(sides[0], sides[1]).astype(BF)

    def part(value, chip_at, core_at):
        at = (2 * chip_at + core_at) * part_cols
        return value[:, at : at + part_cols]

    def backward_attention(grad, summed, gates, weights, kept, first_done=()):
        query_w, output_w, kv_w, router, gains = weights
        x, n_one, queries, kv_near, kv_far, attended, low, mid, n_two = kept
        d_gates = rolled(summed[:, width : width + E])
        spread = gates * (d_gates - jnp.sum(gates * d_gates, -1, keepdims=True))
        spread_low = spread.astype(BF)
        d_n_two = summed[:, :width] + mm_nt(spread_low, router[:, :E])
        d_norm, gain_two_grad = norm_backward(mid, gains[1], d_n_two)
        d_mid = grad.astype(F32) + d_norm
        d_attn = d_mid.astype(BF)
        d_attended = jnp.concatenate([mm(d_attn, w) for w in output_w], -1).astype(BF)
        out_part = reduce_group(
            [
                [
                    by_section(halves(mm_tn(d_attn, part(attended, y, c)).astype(BF)))
                    .reshape(2, width // 2, part_cols)
                    for y in range(2)
                ]
                for c in range(2)
            ]
        )
        dq, d_near, d_far = after(
            attend_back(
                place, queries, attended, d_attended, kv_near, kv_far, low, cosine, sine
            ),
            out_part,
            first_done,
        )
        d_kv = add(d_near, swap_c(d_far))
        d_kv = d_kv[:own] + swap_y(d_kv[own:].astype(BF)).astype(F32)
        d_kv = jnp.concatenate([turned(d_kv[:, :kv_width], -1.0), d_kv[:, kv_width:]], -1)
        d_kv = d_kv.astype(BF)
        d_n_one = mm_nt(d_kv, kv_w)
        for i, w in enumerate(query_w):
            d_n_one = d_n_one + mm_nt(dq[:, i * part_cols : (i + 1) * part_cols], w)
        d_norm, gain_one_grad = norm_backward(x, gains[0], d_n_one)
        d_in = (d_mid + d_norm).astype(BF)
        pieces = (n_one, n_two, dq, d_kv, spread_low, gain_one_grad, gain_two_grad)
        return d_in, out_part.reshape(dp, -1, part_cols), pieces

    def attn_grads(pieces):
        n_one, n_two, dq, d_kv, spread_low, gain_one_grad, gain_two_grad = pieces
        at = jnp.arange(part_cols)[None, :] - kv_width

        def column(k):
            return jnp.broadcast_to((at == k).astype(BF), (own, part_cols))

        def padded(value, ahead):
            behind = part_cols - ahead - value.shape[1]
            return jnp.pad(value, ((0, 0), (ahead, behind)))

        keys_and_extras = (
            mm_tn(n_one, padded(d_kv[:, :kv_width], 0))
            + mm_tn(n_two, padded(rolled(spread_low), kv_width))
            + mm_tn(gain_one_grad, column(E))
            + mm_tn(gain_two_grad, column(E + 1))
        )
        values_part = mm_tn(n_one, padded(d_kv[:, kv_width:], 0))
        small = jnp.stack([keys_and_extras, values_part]).astype(BF)
        small = small.reshape(2, dp, 2, 2, little, part_cols).transpose(3, 2, 0, 1, 4, 5)
        small = absolute(small)
        late = []
        for c in range(2):
            side = []
            for y in range(2):
                main = halves(mm_tn(n_one, part(dq, y, c)).astype(BF))
                main = main.reshape(2, dp, shard // 2, part_cols)
                both = jnp.concatenate([main, small[c, y]], 2)
                side.append(by_section(both.reshape(2, -1, part_cols)))
            late.append(side)
        return reduce_group(late).reshape(dp, -1, part_cols)

    def reduce_dp(value):
        return lax.psum_scatter(value, "dp", scatter_dimension=0, tiled=True)

    def blocks4(value):
        return value.reshape(4, own, -1)

    def both_batches(value_0, value_1):
        got = swap_x(jnp.where(first, value_1, value_0))
        mine = jnp.where(first, value_0, value_1)
        return jnp.where(first, jnp.stack([mine, got]), jnp.stack([got, mine]))[None, :, None]

    own_cot = pick(out_cotangent, section)[0]
    own_in = pick(block_input, section)[0]

    down_0 = gather_dp(expert_shard[0][:, 2 * cols :])
    attn_part_1 = gather_dp(after(attn_shard[1], down_0))
    up_0 = gather_dp(after(expert_shard[0][:, : 2 * cols], attn_part_1))
    weights_0 = attn_weights(
        attn_gather(after(attn_part_0, cot_rows[1], expert_shard[0]), down_0)
    )
    sides_1 = attn_gather(attn_part_1)
    mid_0, n_two_0, kept_0 = forward_attention(own_in.astype(F32), weights_0)
    rows_0 = gather_rows(after(n_two_0, sides_1[1]))
    experts_0 = (up_0, down_0)
    router_0 = weights_0[3]
    down_1 = gather_dp(after(expert_shard[1][:, 2 * cols :], up_0))
    up_1 = gather_dp(after(expert_shard[1][:, : 2 * cols], down_1))
    experts_1 = (up_1, down_1)
    far_0 = experts_call(ff, experts_0, forward=(rows_0[1], hits[1], router_0))
    near_0 = experts_call(ff, experts_0, forward=(rows_0[0], hits[0], router_0))
    weights_1 = attn_weights(after(sides_1, far_0[0]))
    moe_0 = scatter_group(blocks4(near_0[0]), blocks4(far_0[0]))
    out_0 = (mid_0 + after(moe_0, down_1)).astype(BF)

    mid_1, n_two_1, kept_1 = forward_attention(out_0.astype(F32), weights_1)
    rows_1 = gather_rows(n_two_1)
    router_1 = weights_1[3]
    far_1 = experts_call(
        ff, experts_1, forward=(rows_1[1], hits[1], router_1), backward=(cot_rows[1], sums)
    )
    near_1 = experts_call(
        ff, experts_1, forward=(rows_1[0], hits[0], router_1), backward=(cot_rows[0], sums)
    )
    summed_1 = scatter_group(blocks4(near_1[2]), blocks4(far_1[2]))
    back_1 = after((near_1[3:], far_1[3:]), near_1[2], far_1[2])
    grads_1 = expert_grads(rows_1, cot_rows, *zip(*back_1))
    experts_g1 = [reduce_dp(g) for g in grads_1]
    link, out_g1, pieces_1 = backward_attention(
        own_cot, after(summed_1, grads_1[0]), near_1[1][:own], weights_1, kept_1
    )

    link_rows = after(gather_rows(link), grads_1[1])
    far_b = experts_call(ff, experts_0, backward=(link_rows[1], sums), kept=far_0[1:])
    near_b = experts_call(ff, experts_0, backward=(link_rows[0], sums), kept=near_0[1:])
    moe_1 = after((near_1[0], far_1[0]), link_rows[1])
    out_1 = (mid_1 + scatter_group(blocks4(moe_1[0]), blocks4(moe_1[1]))).astype(BF)
    near_d, far_d = after((near_b[0], far_b[0]), out_1, experts_g1[0])
    summed_0 = scatter_group(blocks4(near_d), blocks4(far_d))
    back_0 = after((near_b[1:], far_b[1:]), near_d, far_d)
    grads_0 = expert_grads(rows_0, link_rows, *zip(*back_0))
    experts_g0 = [reduce_dp(g) for g in grads_0]
    late_g1 = attn_grads(after(pieces_1, summed_0))
    grad_in, out_g0, pieces_0 = backward_attention(
        link, after(summed_0, grads_0), near_0[1][:own], weights_0, kept_0, late_g1
    )
    section_outputs = both_batches(out_0, out_1)
    early = jnp.concatenate([out_g1, late_g1, out_g0], 1)
    early = reduce_dp(early.reshape(-1, part_cols))

    def to_owner(value_0, value_1):
        got = swap_x(jnp.where(first, value_1, value_0))
        mine = jnp.where(first, value_0, value_1)
        return jnp.where(first, mine, got), jnp.where(first, got, mine)

    low_up, high_up = to_owner(experts_g0[0], experts_g1[0])
    low_down, high_down = to_owner(experts_g0[1], experts_g1[1])
    late_g0 = attn_grads(after(pieces_0, low_up, low_down, section_outputs))
    late_g0 = reduce_dp(late_g0.reshape(-1, part_cols))

    input_grads = both_batches(after(grad_in, early), link)

    h = shard // 2
    both_parts = shard + little
    low, high = to_owner(
        jnp.concatenate([early[both_parts:], late_g0], 0), early[:both_parts]
    )
    output_g = jnp.concatenate([low[:h], high[:h]], 0).astype(F32)
    query_g = jnp.concatenate([low[h : 2 * h], high[h : 2 * h]], 0).astype(F32)
    key_g = low[2 * h :].astype(F32)
    value_g = high[2 * h :].astype(F32)
    def split(low_part, high_part):
        both = jnp.stack([low_part, high_part], 0).astype(F32)
        return both.reshape(2, shard, half_e, ff)

    gate_g = split(low_up[:, :cols], high_up[:, :cols]).transpose(0, 2, 1, 3)
    gate_g = gate_g.reshape(E, shard, ff)
    up_g = split(low_up[:, cols:], high_up[:, cols:]).transpose(0, 2, 1, 3)
    up_g = up_g.reshape(E, shard, ff)
    down_g = split(low_down, high_down).transpose(0, 2, 3, 1).reshape(E, ff, shard)
    return (
        section_outputs,
        input_grads,
        key_g[:, kv_width + E][None],
        key_g[:, kv_width + E + 1][None],
        key_g[:, :kv_width][None],
        value_g[:, :kv_width][None],
        key_g[:, kv_width : kv_width + E][None],
        query_g[None],
        output_g.T[None],
        gate_g[None],
        up_g[None],
        down_g[None],
    )


def solution(mesh):
    placed = (
        P(None, "dp", "tensor", None),
        P(None, "dp", "tensor", None),
        P(None, "dp", None, None),
        P("section", ("dp", "tensor")),
        P("section", ("dp", "tensor")),
        P("section", ("dp", "tensor"), None),
        P("section", ("dp", "tensor"), None),
        P("section", ("dp", "tensor"), None),
        P("section", "dp", "tensor"),
        P("section", "tensor", "dp"),
        P("section", None, "dp", "tensor"),
        P("section", None, "dp", "tensor"),
        P("section", None, "tensor", "dp"),
    )
    return jax.shard_map(
        per_device,
        mesh=mesh,
        in_specs=placed,
        out_specs=(
            P("section", None, "dp", "tensor", None),
            P("section", None, "dp", "tensor", None),
            P("section", ("dp", "tensor")),
            P("section", ("dp", "tensor")),
            P("section", ("dp", "tensor"), None),
            P("section", ("dp", "tensor"), None),
            P("section", ("dp", "tensor"), None),
            P("section", "dp", "tensor"),
            P("section", "tensor", "dp"),
            P("section", None, "dp", "tensor"),
            P("section", None, "dp", "tensor"),
            P("section", None, "tensor", "dp"),
        ),
        check_vma=False,
    )
```

```python
import jax
import jax.numpy as jnp
from jax import lax
from jax.sharding import PartitionSpec as P

QUERY_HEADS = 12
KEY_VALUE_HEADS = 2
HEAD_SIZE = 128
TOP = 4
E = 8
EPS = 1e-06
NEG = -1e30
BF = jnp.bfloat16
F32 = jnp.float32


def dot(a, b, contract):
    return lax.dot_general(a, b, (contract, ((), ())), preferred_element_type=F32)


def mm(a, b):
    return dot(a, b, ((1,), (0,)))


def mm_nt(a, b):
    return dot(a, b, ((1,), (1,)))


def mm_tn(a, b):
    return dot(a, b, ((0,), (0,)))


def masked_softmax(logits, hit):
    logits = jnp.where(hit, logits, NEG)
    top = jnp.max(logits, -1, keepdims=True)
    exps = jnp.where(hit, jnp.exp(logits - top), 0.0)
    return exps / jnp.sum(exps, -1, keepdims=True)


def spread(gates, ff):
    count = E // 2
    lane = lax.broadcasted_iota(jnp.int32, (gates.shape[0], count * ff), 1)
    wide = jnp.broadcast_to(gates[:, count - 1][:, None], lane.shape)
    for e in range(count - 2, -1, -1):
        wide = jnp.where(lane < (e + 1) * ff, gates[:, e][:, None], wide)
    return wide


def experts_call(ff, weight, forward=None, backward=None, kept=None):
    up_w, down_w = weight
    cols = (E // 2) * ff
    outs = []
    if forward:
        rows, hit, router = forward
        gates = masked_softmax(mm(rows, router[:, :E]), hit > 0.0)
        both = mm(rows, up_w)
        pre_gate, pre_up = both[:, :cols], both[:, cols:]
    else:
        gates, pre_gate, pre_up = kept
        pre_gate, pre_up = pre_gate.astype(F32), pre_up.astype(F32)
    wide = spread(gates, ff)
    sig = jax.nn.sigmoid(pre_gate)
    active = pre_gate * sig
    hidden = active * pre_up
    gated = (hidden * wide).astype(BF)
    if forward:
        outs += [mm_nt(gated, down_w).astype(BF), gates]
        if not backward:
            outs += [pre_gate.astype(BF), pre_up.astype(BF)]
    if backward:
        grad, sums = backward
        back = mm(grad, down_w)
        tail = mm((hidden * back).astype(BF), sums)
        d_hidden = back * wide
        d_gate = (d_hidden * pre_up * (sig * (1.0 + pre_gate * (1.0 - sig)))).astype(BF)
        d_both = jnp.concatenate([d_gate, (d_hidden * active).astype(BF)], -1)
        d_rows = mm_nt(d_both, up_w).astype(BF)
        outs += [jnp.concatenate([d_rows, tail.astype(BF)], -1), d_both, gated]
    return outs


def expert_grads(rows, grads, d_both, gated):
    up = mm_tn(rows[1], d_both[1]) + mm_tn(rows[0], d_both[0])
    down = mm_tn(grads[1], gated[1]) + mm_tn(grads[0], gated[0])
    return up.astype(BF), down.astype(BF)


def turn(value, cosine, sine):
    heads = value.reshape(value.shape[0], -1, HEAD_SIZE)
    moved = jnp.roll(heads, HEAD_SIZE // 2, -1)
    return (heads * cosine[:, None] + moved * sine[:, None]).reshape(value.shape)


def relative_heads(place, value):
    value = value.reshape(value.shape[0], 2, KEY_VALUE_HEADS, HEAD_SIZE)
    return jnp.where(place[4] == 0, value, value[:, :, ::-1])


def seen(place, own):
    key = jnp.arange(own, dtype=jnp.int32)
    key = jnp.concatenate([key + place[b] for b in range(4)])
    return key[None, :] <= jnp.arange(own, dtype=jnp.int32)[:, None]


def attend(place, q_raw, near, far, cosine, sine):
    own, width = q_raw.shape
    queries = turn(q_raw, cosine, sine).astype(BF)
    q_group = queries.reshape(own, KEY_VALUE_HEADS, -1, HEAD_SIZE)
    kv = relative_heads(place, jnp.concatenate([near, far], 0))
    scores = jnp.einsum("qgje,kge->gjqk", q_group, kv[:, 0], preferred_element_type=F32)
    scores = jnp.where(seen(place, own), scores * HEAD_SIZE ** (-0.5), NEG)
    top = jnp.max(scores, -1, keepdims=True)
    exps = jnp.exp(scores - top)
    total = jnp.sum(exps, -1, keepdims=True)
    low = lax.optimization_barrier((exps / total).astype(BF))
    attended = jnp.einsum("gjqk,kge->qgje", low, kv[:, 1], preferred_element_type=F32)
    return queries, attended.astype(BF).reshape(own, width), low


def attend_back(place, queries, attended, grad, near, far, low, cosine, sine):
    own, width = queries.shape
    q_group = queries.reshape(own, KEY_VALUE_HEADS, -1, HEAD_SIZE)
    g_group = grad.reshape(own, KEY_VALUE_HEADS, -1, HEAD_SIZE)
    kv = relative_heads(place, jnp.concatenate([near, far], 0))
    delta = jnp.sum(g_group.astype(F32) * attended.reshape(g_group.shape).astype(F32), -1)
    delta = delta.transpose(1, 2, 0)[..., None]
    d_probs = jnp.einsum("qgje,kge->gjqk", g_group, kv[:, 1], preferred_element_type=F32)
    d_scores = (low.astype(F32) * (d_probs - delta) * HEAD_SIZE ** (-0.5)).astype(BF)
    d_scores = lax.optimization_barrier(d_scores)
    d_values = jnp.einsum("gjqk,qgje->kge", low, g_group, preferred_element_type=F32)
    d_keys = jnp.einsum("gjqk,qgje->kge", d_scores, q_group, preferred_element_type=F32)
    dq = jnp.einsum("gjqk,kge->qgje", d_scores, kv[:, 0], preferred_element_type=F32)
    dq = turn(dq.reshape(own, width), cosine, -sine).astype(BF)
    pieces = []
    for value in (d_keys, d_values):
        one, two = value[:, 0].astype(BF), value[:, 1].astype(BF)
        pieces += [jnp.where(place[4] == 0, one, two), jnp.where(place[4] == 0, two, one)]
    d_kv = jnp.concatenate(pieces, -1)
    return dq, d_kv[: near.shape[0]], d_kv[near.shape[0] :]


def swap_x(value):
    return lax.ppermute(value, "section", [(0, 1), (1, 0)])


def swap_y(value):
    return lax.ppermute(value, "tensor", [(t, t ^ 2) for t in range(4)])


def swap_c(value):
    return lax.ppermute(value, "tensor", [(t, t ^ 1) for t in range(4)])


def after(value, *first):
    return lax.optimization_barrier((value, first))[0]


def gather_chips(value, *hold):
    half = value.shape[0] // 2
    from_x, from_y = swap_x(value), swap_y(value)
    if hold:
        from_x, from_y = after((from_x, from_y), *hold)
    top = swap_x(from_y[:half])
    low = swap_y(from_x[half:])
    return jnp.stack([value, from_y, from_x, jnp.concatenate([top, low], 0)])


def add(one, two):
    return one.astype(F32) + two.astype(F32)


def scatter_chips(parts):
    half = parts.shape[1] // 2
    top = swap_x(parts[3][:half])
    low = swap_y(parts[3][half:])
    to_y = jnp.concatenate([add(parts[1][:half], top).astype(BF), parts[1][half:]], 0)
    to_x = jnp.concatenate([parts[2][:half], add(parts[2][half:], low).astype(BF)], 0)
    return parts[0].astype(F32) + swap_y(to_y).astype(F32) + swap_x(to_x).astype(F32)


def scatter_group(near, far):
    return scatter_chips(add(near, swap_c(far)).astype(BF))


def norm_forward(value, gain):
    inverse = lax.rsqrt(jnp.mean(value * value, -1, keepdims=True) + EPS)
    return value * inverse * gain


def norm_backward(value, gain, grad):
    inverse = lax.rsqrt(jnp.mean(value * value, -1, keepdims=True) + EPS)
    scaled = value * inverse
    weighted = grad * gain
    gain_grad = (grad * scaled).astype(BF)
    return inverse * (weighted - scaled * jnp.mean(weighted * scaled, -1, keepdims=True)), gain_grad


def per_device(
    block_input,
    out_cotangent,
    routes,
    attn_gain,
    ffn_gain,
    key_projection_weight,
    value_projection_weight,
    router_weight,
    query_weight,
    output_weight,
    expert_gate,
    expert_up,
    expert_down,
):
    own = block_input.shape[2]
    width = block_input.shape[3]
    length = routes.shape[2]
    ff = expert_gate.shape[3]
    shard = expert_gate.shape[2]
    dp = width // shard
    little = attn_gain.shape[1]
    half_e = E // 2
    cols = half_e * ff
    kv_width = KEY_VALUE_HEADS * HEAD_SIZE
    part_cols = query_weight.shape[2]
    section = lax.axis_index("section")
    tensor = lax.axis_index("tensor")
    first = section == 0
    chip = tensor // 2
    core = tensor % 2

    def pick(pair, at):
        return lax.dynamic_index_in_dim(pair, at, 0, keepdims=False)

    extras = jnp.concatenate(
        [
            router_weight[0],
            attn_gain[0][:, None],
            ffn_gain[0][:, None],
            jnp.zeros((little, 128 - E - 2), BF),
        ],
        -1,
    )
    pack_q = jnp.concatenate(
        [query_weight[0], jnp.concatenate([key_projection_weight[0], extras], -1)], 0
    )
    pack_o = jnp.concatenate(
        [output_weight[0].T, jnp.pad(value_projection_weight[0], ((0, 0), (0, 128)))], 0
    )
    got = swap_x(jnp.where(first, pack_o, pack_q))
    kept = jnp.where(first, pack_q, pack_o)
    attn_shard = [jnp.where(first, kept, got), jnp.where(first, got, kept)]
    pack_rows = shard + little

    def gather_dp(value):
        return lax.all_gather(value, "dp", axis=0, tiled=True)

    attn_part_0 = gather_dp(attn_shard[0])

    def expert_pack(start):
        def across(weight):
            piece = lax.dynamic_slice_in_dim(weight[0], start, half_e, 0)
            return piece.transpose(1, 0, 2).reshape(shard, cols)

        down = lax.dynamic_slice_in_dim(expert_down[0], start, half_e, 0).reshape(cols, shard)
        return jnp.concatenate([across(expert_gate), across(expert_up), down.T], -1)

    kept_e = expert_pack(half_e * section)
    got_e = swap_x(after(expert_pack(half_e * (1 - section)), got))
    expert_shard = [jnp.where(first, kept_e, got_e), jnp.where(first, got_e, kept_e)]

    cot = jnp.where(first, out_cotangent[:, 0], out_cotangent[::-1, 0])
    cot_near = after(jnp.stack([cot, swap_y(after(cot, got))], 1), got_e, attn_part_0)
    cot_far = swap_c(cot_near)
    cot_rows = [v.reshape(4 * own, width) for v in (cot_near, cot_far)]

    def absolute(blocks):
        blocks = jnp.where(core == 0, blocks, blocks[::-1])
        return jnp.where(chip == 0, blocks, blocks[:, ::-1])

    def attn_gather(part, *first_done):
        near = gather_chips(part)
        return near, swap_c(after(near, *first_done))

    def attn_weights(sides):
        sides = [side.reshape(2, 2, dp, pack_rows, part_cols) for side in sides]
        mains, smalls = [], []
        for kind in (section, 1 - section):
            chosen = [pick(side, kind) for side in sides]
            mains.append(
                [
                    chosen[c][y, :, :shard].reshape(width, part_cols)
                    for y in range(2)
                    for c in range(2)
                ]
            )
            small = absolute(jnp.stack([c[:, :, shard:] for c in chosen]))
            smalls.append(small.transpose(2, 1, 0, 3, 4).reshape(width, part_cols))
        extra = smalls[0][:, kv_width:]
        router = jnp.concatenate([rolled(extra[:, :E]), extra[:, E:]], -1)
        kv_w = jnp.concatenate([smalls[0][:, :kv_width], smalls[1][:, :kv_width]], -1)
        gains = extra[:, E : E + 2].astype(F32).T
        return mains[0], mains[1], kv_w, router, gains

    def rolled(columns):
        return jnp.where(first, columns, jnp.roll(columns, half_e, -1))

    def hits_of(rel_core):
        pieces = []
        for rel_x in range(2):
            for rel_y in range(2):
                start = (tensor ^ (2 * rel_y + rel_core)) * own
                piece = lax.dynamic_slice(routes, (section ^ rel_x, 0, start, 0), (1, 1, own, TOP))
                pieces.append(piece.reshape(own, TOP))
        picked = jnp.concatenate(pieces, 0)
        ids = (jnp.arange(E, dtype=jnp.int32) + half_e * section) % E
        return jnp.any(picked[:, :, None] == ids[None, None, :], 1).astype(F32)

    hits = [hits_of(0), hits_of(1)]
    sums = (
        jnp.arange(cols)[:, None] // ff + half_e * section == jnp.arange(128)[None, :]
    ).astype(BF)

    halfway = HEAD_SIZE // 2
    places = (tensor * own + jnp.arange(own)).astype(F32)
    rates = 10000.0 ** (-(jnp.arange(halfway, dtype=F32) * 2.0) / HEAD_SIZE)
    angles = places[:, None] * rates[None, :]
    cosine = jnp.concatenate([jnp.cos(angles)] * 2, -1)
    sine = jnp.concatenate([-jnp.sin(angles), jnp.sin(angles)], -1)
    place = jnp.stack(
        [((tensor ^ (2 * y + c)) - tensor) * own for c in range(2) for y in range(2)]
        + [chip] * 4
    ).astype(jnp.int32)

    def turned(value, sign):
        heads = value.reshape(own, -1, HEAD_SIZE)
        moved = jnp.roll(heads, halfway, -1)
        return (heads * cosine[:, None] + sign * moved * sine[:, None]).reshape(own, -1)

    def gather_rows(value):
        near = gather_chips(value)
        return near.reshape(4 * own, width), swap_c(near).reshape(4 * own, width)

    def forward_attention(x, weights):
        query_w, output_w, kv_w, _, gains = weights
        n_one = norm_forward(x, gains[0]).astype(BF)
        q_raw = jnp.concatenate([mm(n_one, w) for w in query_w], -1)
        kv_raw = mm(n_one, kv_w)
        kv_own = jnp.concatenate([turned(kv_raw[:, :kv_width], 1.0), kv_raw[:, kv_width:]], -1)
        kv_own = kv_own.astype(BF)
        kv_near = jnp.concatenate([kv_own, swap_y(kv_own)], 0)
        kv_far = swap_c(kv_near)
        queries, attended, low = attend(place, q_raw, kv_near, kv_far, cosine, sine)
        mid = x
        for i, w in enumerate(output_w):
            mid = mid + mm_nt(attended[:, i * part_cols : (i + 1) * part_cols], w)
        n_two = norm_forward(mid, gains[1]).astype(BF)
        kept = (x, n_one, queries, kv_near, kv_far, attended, low, mid, n_two)
        return mid, n_two, kept

    def halves(value):
        return value.reshape(dp, 2, shard // 2, -1).swapaxes(0, 1)

    def by_section(pair):
        return jnp.where(first, pair, pair[::-1])

    def reduce_group(blocks):
        sides = [jnp.stack([b[s] for s in range(2) for b in side]) for side in blocks]
        return scatter_group(sides[0], sides[1]).astype(BF)

    def part(value, chip_at, core_at):
        at = (2 * chip_at + core_at) * part_cols
        return value[:, at : at + part_cols]

    def backward_attention(grad, summed, gates, weights, kept, first_done=()):
        query_w, output_w, kv_w, router, gains = weights
        x, n_one, queries, kv_near, kv_far, attended, low, mid, n_two = kept
        d_gates = rolled(summed[:, width : width + E])
        spread = gates * (d_gates - jnp.sum(gates * d_gates, -1, keepdims=True))
        spread_low = spread.astype(BF)
        d_n_two = summed[:, :width] + mm_nt(spread_low, router[:, :E])
        d_norm, gain_two_grad = norm_backward(mid, gains[1], d_n_two)
        d_mid = grad.astype(F32) + d_norm
        d_attn = d_mid.astype(BF)
        d_attended = jnp.concatenate([mm(d_attn, w) for w in output_w], -1).astype(BF)
        out_part = reduce_group(
            [
                [
                    by_section(halves(mm_tn(d_attn, part(attended, y, c)).astype(BF)))
                    .reshape(2, width // 2, part_cols)
                    for y in range(2)
                ]
                for c in range(2)
            ]
        )
        dq, d_near, d_far = after(
            attend_back(
                place, queries, attended, d_attended, kv_near, kv_far, low, cosine, sine
            ),
            out_part,
            first_done,
        )
        d_kv = add(d_near, swap_c(d_far))
        d_kv = d_kv[:own] + swap_y(d_kv[own:].astype(BF)).astype(F32)
        d_kv = jnp.concatenate([turned(d_kv[:, :kv_width], -1.0), d_kv[:, kv_width:]], -1)
        d_kv = d_kv.astype(BF)
        d_n_one = mm_nt(d_kv, kv_w)
        for i, w in enumerate(query_w):
            d_n_one = d_n_one + mm_nt(dq[:, i * part_cols : (i + 1) * part_cols], w)
        d_norm, gain_one_grad = norm_backward(x, gains[0], d_n_one)
        d_in = (d_mid + d_norm).astype(BF)
        pieces = (n_one, n_two, dq, d_kv, spread_low, gain_one_grad, gain_two_grad)
        return d_in, out_part.reshape(dp, -1, part_cols), pieces

    def attn_grads(pieces):
        n_one, n_two, dq, d_kv, spread_low, gain_one_grad, gain_two_grad = pieces
        at = jnp.arange(part_cols)[None, :] - kv_width

        def column(k):
            return jnp.broadcast_to((at == k).astype(BF), (own, part_cols))

        def padded(value, ahead):
            behind = part_cols - ahead - value.shape[1]
            return jnp.pad(value, ((0, 0), (ahead, behind)))

        keys_and_extras = (
            mm_tn(n_one, padded(d_kv[:, :kv_width], 0))
            + mm_tn(n_two, padded(rolled(spread_low), kv_width))
            + mm_tn(gain_one_grad, column(E))
            + mm_tn(gain_two_grad, column(E + 1))
        )
        values_part = mm_tn(n_one, padded(d_kv[:, kv_width:], 0))
        small = jnp.stack([keys_and_extras, values_part]).astype(BF)
        small = small.reshape(2, dp, 2, 2, little, part_cols).transpose(3, 2, 0, 1, 4, 5)
        small = absolute(small)
        late = []
        for c in range(2):
            side = []
            for y in range(2):
                main = halves(mm_tn(n_one, part(dq, y, c)).astype(BF))
                main = main.reshape(2, dp, shard // 2, part_cols)
                both = jnp.concatenate([main, small[c, y]], 2)
                side.append(by_section(both.reshape(2, -1, part_cols)))
            late.append(side)
        return reduce_group(late).reshape(dp, -1, part_cols)

    def reduce_dp(value):
        return lax.psum_scatter(value, "dp", scatter_dimension=0, tiled=True)

    def blocks4(value):
        return value.reshape(4, own, -1)

    def both_batches(value_0, value_1):
        got = swap_x(jnp.where(first, value_1, value_0))
        mine = jnp.where(first, value_0, value_1)
        return jnp.where(first, jnp.stack([mine, got]), jnp.stack([got, mine]))[None, :, None]

    own_cot = pick(out_cotangent, section)[0]
    own_in = pick(block_input, section)[0]

    down_0 = gather_dp(expert_shard[0][:, 2 * cols :])
    up_0 = gather_dp(after(expert_shard[0][:, : 2 * cols], down_0))
    weights_0 = attn_weights(
        attn_gather(after(attn_part_0, cot_rows[1], expert_shard[0]), down_0)
    )
    mid_0, n_two_0, kept_0 = forward_attention(own_in.astype(F32), weights_0)
    rows_0 = gather_rows(n_two_0)
    experts_0 = (up_0, down_0)
    router_0 = weights_0[3]
    attn_part_1 = gather_dp(after(attn_shard[1], up_0, rows_0[0]))
    far_0 = experts_call(ff, experts_0, forward=(rows_0[1], hits[1], router_0))
    near_0 = experts_call(ff, experts_0, forward=(rows_0[0], hits[0], router_0))
    down_1 = gather_dp(after(expert_shard[1][:, 2 * cols :], attn_part_1, near_0[0]))
    up_1 = gather_dp(after(expert_shard[1][:, : 2 * cols], down_1))
    experts_1 = (up_1, down_1)
    near_1 = gather_chips(after(attn_part_1, near_0[0]), far_0[0])
    weights_1 = attn_weights((near_1, swap_c(near_1)))
    moe_0 = scatter_group(blocks4(near_0[0]), blocks4(far_0[0]))
    out_0 = (mid_0 + after(moe_0, down_1)).astype(BF)

    mid_1, n_two_1, kept_1 = forward_attention(out_0.astype(F32), weights_1)
    rows_1 = gather_rows(n_two_1)
    router_1 = weights_1[3]
    far_1 = experts_call(
        ff, experts_1, forward=(rows_1[1], hits[1], router_1), backward=(cot_rows[1], sums)
    )
    near_1 = experts_call(
        ff, experts_1, forward=(rows_1[0], hits[0], router_1), backward=(cot_rows[0], sums)
    )
    summed_1 = scatter_group(blocks4(near_1[2]), blocks4(far_1[2]))
    back_1 = after((near_1[3:], far_1[3:]), near_1[2], far_1[2])
    grads_1 = expert_grads(rows_1, cot_rows, *zip(*back_1))
    experts_g1 = [reduce_dp(g) for g in grads_1]
    link, out_g1, pieces_1 = backward_attention(
        own_cot, after(summed_1, grads_1[0]), near_1[1][:own], weights_1, kept_1
    )

    link_rows = after(gather_rows(link), grads_1[1])
    far_b = experts_call(ff, experts_0, backward=(link_rows[1], sums), kept=far_0[1:])
    near_b = experts_call(ff, experts_0, backward=(link_rows[0], sums), kept=near_0[1:])
    moe_1 = after((near_1[0], far_1[0]), link_rows[1])
    out_1 = (mid_1 + scatter_group(blocks4(moe_1[0]), blocks4(moe_1[1]))).astype(BF)
    near_d, far_d = after((near_b[0], far_b[0]), out_1, experts_g1[0])
    summed_0 = scatter_group(blocks4(near_d), blocks4(far_d))
    back_0 = after((near_b[1:], far_b[1:]), near_d, far_d)
    grads_0 = expert_grads(rows_0, link_rows, *zip(*back_0))
    experts_g0 = [reduce_dp(g) for g in grads_0]
    late_g1 = attn_grads(after(pieces_1, summed_0))
    grad_in, out_g0, pieces_0 = backward_attention(
        link, after(summed_0, grads_0), near_0[1][:own], weights_0, kept_0, late_g1
    )
    section_outputs = both_batches(out_0, out_1)
    early = jnp.concatenate([out_g1, late_g1, out_g0], 1)
    early = reduce_dp(early.reshape(-1, part_cols))

    def to_owner(value_0, value_1):
        got = swap_x(jnp.where(first, value_1, value_0))
        mine = jnp.where(first, value_0, value_1)
        return jnp.where(first, mine, got), jnp.where(first, got, mine)

    low_up, high_up = to_owner(experts_g0[0], experts_g1[0])
    low_down, high_down = to_owner(experts_g0[1], experts_g1[1])
    late_g0 = attn_grads(after(pieces_0, low_up, low_down, section_outputs))
    late_g0 = reduce_dp(late_g0.reshape(-1, part_cols))

    input_grads = both_batches(after(grad_in, early), link)

    h = shard // 2
    both_parts = shard + little
    low, high = to_owner(
        jnp.concatenate([early[both_parts:], late_g0], 0), early[:both_parts]
    )
    output_g = jnp.concatenate([low[:h], high[:h]], 0).astype(F32)
    query_g = jnp.concatenate([low[h : 2 * h], high[h : 2 * h]], 0).astype(F32)
    key_g = low[2 * h :].astype(F32)
    value_g = high[2 * h :].astype(F32)
    def split(low_part, high_part):
        both = jnp.stack([low_part, high_part], 0).astype(F32)
        return both.reshape(2, shard, half_e, ff)

    gate_g = split(low_up[:, :cols], high_up[:, :cols]).transpose(0, 2, 1, 3)
    gate_g = gate_g.reshape(E, shard, ff)
    up_g = split(low_up[:, cols:], high_up[:, cols:]).transpose(0, 2, 1, 3)
    up_g = up_g.reshape(E, shard, ff)
    down_g = split(low_down, high_down).transpose(0, 2, 3, 1).reshape(E, ff, shard)
    return (
        section_outputs,
        input_grads,
        key_g[:, kv_width + E][None],
        key_g[:, kv_width + E + 1][None],
        key_g[:, :kv_width][None],
        value_g[:, :kv_width][None],
        key_g[:, kv_width : kv_width + E][None],
        query_g[None],
        output_g.T[None],
        gate_g[None],
        up_g[None],
        down_g[None],
    )


def solution(mesh):
    placed = (
        P(None, "dp", "tensor", None),
        P(None, "dp", "tensor", None),
        P(None, "dp", None, None),
        P("section", ("dp", "tensor")),
        P("section", ("dp", "tensor")),
        P("section", ("dp", "tensor"), None),
        P("section", ("dp", "tensor"), None),
        P("section", ("dp", "tensor"), None),
        P("section", "dp", "tensor"),
        P("section", "tensor", "dp"),
        P("section", None, "dp", "tensor"),
        P("section", None, "dp", "tensor"),
        P("section", None, "tensor", "dp"),
    )
    return jax.shard_map(
        per_device,
        mesh=mesh,
        in_specs=placed,
        out_specs=(
            P("section", None, "dp", "tensor", None),
            P("section", None, "dp", "tensor", None),
            P("section", ("dp", "tensor")),
            P("section", ("dp", "tensor")),
            P("section", ("dp", "tensor"), None),
            P("section", ("dp", "tensor"), None),
            P("section", ("dp", "tensor"), None),
            P("section", "dp", "tensor"),
            P("section", "tensor", "dp"),
            P("section", None, "dp", "tensor"),
            P("section", None, "dp", "tensor"),
            P("section", None, "tensor", "dp"),
        ),
        check_vma=False,
    )
```

```python
import jax
import jax.numpy as jnp
from jax import lax
from jax.sharding import PartitionSpec as P

QUERY_HEADS = 12
KEY_VALUE_HEADS = 2
HEAD_SIZE = 128
TOP = 4
E = 8
EPS = 1e-06
NEG = -1e30
BF = jnp.bfloat16
F32 = jnp.float32


def dot(a, b, contract):
    return lax.dot_general(a, b, (contract, ((), ())), preferred_element_type=F32)


def mm(a, b):
    return dot(a, b, ((1,), (0,)))


def mm_nt(a, b):
    return dot(a, b, ((1,), (1,)))


def mm_tn(a, b):
    return dot(a, b, ((0,), (0,)))


def masked_softmax(logits, hit):
    logits = jnp.where(hit, logits, NEG)
    top = jnp.max(logits, -1, keepdims=True)
    exps = jnp.where(hit, jnp.exp(logits - top), 0.0)
    return exps / jnp.sum(exps, -1, keepdims=True)


def spread(gates, ff):
    count = E // 2
    lane = lax.broadcasted_iota(jnp.int32, (gates.shape[0], count * ff), 1)
    wide = jnp.broadcast_to(gates[:, count - 1][:, None], lane.shape)
    for e in range(count - 2, -1, -1):
        wide = jnp.where(lane < (e + 1) * ff, gates[:, e][:, None], wide)
    return wide


def experts_call(ff, weight, forward=None, backward=None, kept=None):
    up_w, down_w = weight
    cols = (E // 2) * ff
    outs = []
    if forward:
        rows, hit, router = forward
        gates = masked_softmax(mm(rows, router[:, :E]), hit > 0.0)
        both = mm(rows, up_w)
        pre_gate, pre_up = both[:, :cols], both[:, cols:]
    else:
        gates, pre_gate, pre_up = kept
        pre_gate, pre_up = pre_gate.astype(F32), pre_up.astype(F32)
    wide = spread(gates, ff)
    sig = jax.nn.sigmoid(pre_gate)
    active = pre_gate * sig
    hidden = active * pre_up
    gated = (hidden * wide).astype(BF)
    if forward:
        outs += [mm_nt(gated, down_w).astype(BF), gates]
        if not backward:
            outs += [pre_gate.astype(BF), pre_up.astype(BF)]
    if backward:
        grad, sums = backward
        back = mm(grad, down_w)
        tail = mm((hidden * back).astype(BF), sums)
        d_hidden = back * wide
        d_gate = (d_hidden * pre_up * (sig * (1.0 + pre_gate * (1.0 - sig)))).astype(BF)
        d_both = jnp.concatenate([d_gate, (d_hidden * active).astype(BF)], -1)
        d_rows = mm_nt(d_both, up_w).astype(BF)
        outs += [jnp.concatenate([d_rows, tail.astype(BF)], -1), d_both, gated]
    return outs


def expert_grads(rows, grads, d_both, gated):
    up = mm_tn(rows[1], d_both[1]) + mm_tn(rows[0], d_both[0])
    down = mm_tn(grads[1], gated[1]) + mm_tn(grads[0], gated[0])
    return up.astype(BF), down.astype(BF)


def turn(value, cosine, sine):
    heads = value.reshape(value.shape[0], -1, HEAD_SIZE)
    moved = jnp.roll(heads, HEAD_SIZE // 2, -1)
    return (heads * cosine[:, None] + moved * sine[:, None]).reshape(value.shape)


def relative_heads(place, value):
    value = value.reshape(value.shape[0], 2, KEY_VALUE_HEADS, HEAD_SIZE)
    return jnp.where(place[4] == 0, value, value[:, :, ::-1])


def seen(place, own):
    key = jnp.arange(own, dtype=jnp.int32)
    key = jnp.concatenate([key + place[b] for b in range(4)])
    return key[None, :] <= jnp.arange(own, dtype=jnp.int32)[:, None]


def attend(place, q_raw, near, far, cosine, sine):
    own, width = q_raw.shape
    queries = turn(q_raw, cosine, sine).astype(BF)
    q_group = queries.reshape(own, KEY_VALUE_HEADS, -1, HEAD_SIZE)
    kv = relative_heads(place, jnp.concatenate([near, far], 0))
    scores = jnp.einsum("qgje,kge->gjqk", q_group, kv[:, 0], preferred_element_type=F32)
    scores = jnp.where(seen(place, own), scores * HEAD_SIZE ** (-0.5), NEG)
    top = jnp.max(scores, -1, keepdims=True)
    exps = jnp.exp(scores - top)
    total = jnp.sum(exps, -1, keepdims=True)
    low = lax.optimization_barrier((exps / total).astype(BF))
    attended = jnp.einsum("gjqk,kge->qgje", low, kv[:, 1], preferred_element_type=F32)
    return queries, attended.astype(BF).reshape(own, width), low


def attend_back(place, queries, attended, grad, near, far, low, cosine, sine):
    own, width = queries.shape
    q_group = queries.reshape(own, KEY_VALUE_HEADS, -1, HEAD_SIZE)
    g_group = grad.reshape(own, KEY_VALUE_HEADS, -1, HEAD_SIZE)
    kv = relative_heads(place, jnp.concatenate([near, far], 0))
    delta = jnp.sum(g_group.astype(F32) * attended.reshape(g_group.shape).astype(F32), -1)
    delta = delta.transpose(1, 2, 0)[..., None]
    d_probs = jnp.einsum("qgje,kge->gjqk", g_group, kv[:, 1], preferred_element_type=F32)
    d_scores = (low.astype(F32) * (d_probs - delta) * HEAD_SIZE ** (-0.5)).astype(BF)
    d_scores = lax.optimization_barrier(d_scores)
    d_values = jnp.einsum("gjqk,qgje->kge", low, g_group, preferred_element_type=F32)
    d_keys = jnp.einsum("gjqk,qgje->kge", d_scores, q_group, preferred_element_type=F32)
    dq = jnp.einsum("gjqk,kge->qgje", d_scores, kv[:, 0], preferred_element_type=F32)
    dq = turn(dq.reshape(own, width), cosine, -sine).astype(BF)
    pieces = []
    for value in (d_keys, d_values):
        one, two = value[:, 0].astype(BF), value[:, 1].astype(BF)
        pieces += [jnp.where(place[4] == 0, one, two), jnp.where(place[4] == 0, two, one)]
    d_kv = jnp.concatenate(pieces, -1)
    return dq, d_kv[: near.shape[0]], d_kv[near.shape[0] :]


def swap_x(value):
    return lax.ppermute(value, "section", [(0, 1), (1, 0)])


def swap_y(value):
    return lax.ppermute(value, "tensor", [(t, t ^ 2) for t in range(4)])


def swap_c(value):
    return lax.ppermute(value, "tensor", [(t, t ^ 1) for t in range(4)])


def after(value, *first):
    return lax.optimization_barrier((value, first))[0]


def gather_chips(value, *hold):
    half = value.shape[0] // 2
    from_x, from_y = swap_x(value), swap_y(value)
    if hold:
        from_x, from_y = after((from_x, from_y), *hold)
    top = swap_x(from_y[:half])
    low = swap_y(from_x[half:])
    return jnp.stack([value, from_y, from_x, jnp.concatenate([top, low], 0)])


def add(one, two):
    return one.astype(F32) + two.astype(F32)


def scatter_chips(parts):
    half = parts.shape[1] // 2
    top = swap_x(parts[3][:half])
    low = swap_y(parts[3][half:])
    to_y = jnp.concatenate([add(parts[1][:half], top).astype(BF), parts[1][half:]], 0)
    to_x = jnp.concatenate([parts[2][:half], add(parts[2][half:], low).astype(BF)], 0)
    return parts[0].astype(F32) + swap_y(to_y).astype(F32) + swap_x(to_x).astype(F32)


def scatter_group(near, far):
    return scatter_chips(add(near, swap_c(far)).astype(BF))


def norm_forward(value, gain):
    inverse = lax.rsqrt(jnp.mean(value * value, -1, keepdims=True) + EPS)
    return value * inverse * gain


def norm_backward(value, gain, grad):
    inverse = lax.rsqrt(jnp.mean(value * value, -1, keepdims=True) + EPS)
    scaled = value * inverse
    weighted = grad * gain
    gain_grad = (grad * scaled).astype(BF)
    return inverse * (weighted - scaled * jnp.mean(weighted * scaled, -1, keepdims=True)), gain_grad


def per_device(
    block_input,
    out_cotangent,
    routes,
    attn_gain,
    ffn_gain,
    key_projection_weight,
    value_projection_weight,
    router_weight,
    query_weight,
    output_weight,
    expert_gate,
    expert_up,
    expert_down,
):
    own = block_input.shape[2]
    width = block_input.shape[3]
    length = routes.shape[2]
    ff = expert_gate.shape[3]
    shard = expert_gate.shape[2]
    dp = width // shard
    little = attn_gain.shape[1]
    half_e = E // 2
    cols = half_e * ff
    kv_width = KEY_VALUE_HEADS * HEAD_SIZE
    part_cols = query_weight.shape[2]
    section = lax.axis_index("section")
    tensor = lax.axis_index("tensor")
    first = section == 0
    chip = tensor // 2
    core = tensor % 2

    def pick(pair, at):
        return lax.dynamic_index_in_dim(pair, at, 0, keepdims=False)

    extras = jnp.concatenate(
        [
            router_weight[0],
            attn_gain[0][:, None],
            ffn_gain[0][:, None],
            jnp.zeros((little, 128 - E - 2), BF),
        ],
        -1,
    )
    pack_q = jnp.concatenate(
        [query_weight[0], jnp.concatenate([key_projection_weight[0], extras], -1)], 0
    )
    pack_o = jnp.concatenate(
        [output_weight[0].T, jnp.pad(value_projection_weight[0], ((0, 0), (0, 128)))], 0
    )
    got = swap_x(jnp.where(first, pack_o, pack_q))
    kept = jnp.where(first, pack_q, pack_o)
    attn_shard = [jnp.where(first, kept, got), jnp.where(first, got, kept)]
    pack_rows = shard + little

    def gather_dp(value):
        return lax.all_gather(value, "dp", axis=0, tiled=True)

    attn_part_0 = gather_dp(attn_shard[0])

    def expert_pack(start):
        def across(weight):
            piece = lax.dynamic_slice_in_dim(weight[0], start, half_e, 0)
            return piece.transpose(1, 0, 2).reshape(shard, cols)

        down = lax.dynamic_slice_in_dim(expert_down[0], start, half_e, 0).reshape(cols, shard)
        return jnp.concatenate([across(expert_gate), across(expert_up), down.T], -1)

    kept_e = expert_pack(half_e * section)
    got_e = swap_x(after(expert_pack(half_e * (1 - section)), got))
    expert_shard = [jnp.where(first, kept_e, got_e), jnp.where(first, got_e, kept_e)]

    cot = jnp.where(first, out_cotangent[:, 0], out_cotangent[::-1, 0])
    cot_near = after(jnp.stack([cot, swap_y(after(cot, got))], 1), got_e, attn_part_0)
    cot_far = swap_c(cot_near)
    cot_rows = [v.reshape(4 * own, width) for v in (cot_near, cot_far)]

    def absolute(blocks):
        blocks = jnp.where(core == 0, blocks, blocks[::-1])
        return jnp.where(chip == 0, blocks, blocks[:, ::-1])

    def attn_gather(part, *first_done):
        near = gather_chips(part)
        return near, swap_c(after(near, *first_done))

    def attn_weights(sides):
        sides = [side.reshape(2, 2, dp, pack_rows, part_cols) for side in sides]
        mains, smalls = [], []
        for kind in (section, 1 - section):
            chosen = [pick(side, kind) for side in sides]
            mains.append(
                [
                    chosen[c][y, :, :shard].reshape(width, part_cols)
                    for y in range(2)
                    for c in range(2)
                ]
            )
            small = absolute(jnp.stack([c[:, :, shard:] for c in chosen]))
            smalls.append(small.transpose(2, 1, 0, 3, 4).reshape(width, part_cols))
        extra = smalls[0][:, kv_width:]
        router = jnp.concatenate([rolled(extra[:, :E]), extra[:, E:]], -1)
        kv_w = jnp.concatenate([smalls[0][:, :kv_width], smalls[1][:, :kv_width]], -1)
        gains = extra[:, E : E + 2].astype(F32).T
        return mains[0], mains[1], kv_w, router, gains

    def rolled(columns):
        return jnp.where(first, columns, jnp.roll(columns, half_e, -1))

    def hits_of(rel_core):
        pieces = []
        for rel_x in range(2):
            for rel_y in range(2):
                start = (tensor ^ (2 * rel_y + rel_core)) * own
                piece = lax.dynamic_slice(routes, (section ^ rel_x, 0, start, 0), (1, 1, own, TOP))
                pieces.append(piece.reshape(own, TOP))
        picked = jnp.concatenate(pieces, 0)
        ids = (jnp.arange(E, dtype=jnp.int32) + half_e * section) % E
        return jnp.any(picked[:, :, None] == ids[None, None, :], 1).astype(F32)

    hits = [hits_of(0), hits_of(1)]
    sums = (
        jnp.arange(cols)[:, None] // ff + half_e * section == jnp.arange(128)[None, :]
    ).astype(BF)

    halfway = HEAD_SIZE // 2
    places = (tensor * own + jnp.arange(own)).astype(F32)
    rates = 10000.0 ** (-(jnp.arange(halfway, dtype=F32) * 2.0) / HEAD_SIZE)
    angles = places[:, None] * rates[None, :]
    cosine = jnp.concatenate([jnp.cos(angles)] * 2, -1)
    sine = jnp.concatenate([-jnp.sin(angles), jnp.sin(angles)], -1)
    place = jnp.stack(
        [((tensor ^ (2 * y + c)) - tensor) * own for c in range(2) for y in range(2)]
        + [chip] * 4
    ).astype(jnp.int32)

    def turned(value, sign):
        heads = value.reshape(own, -1, HEAD_SIZE)
        moved = jnp.roll(heads, halfway, -1)
        return (heads * cosine[:, None] + sign * moved * sine[:, None]).reshape(own, -1)

    def gather_rows(value):
        near = gather_chips(value)
        return near.reshape(4 * own, width), swap_c(near).reshape(4 * own, width)

    def forward_attention(x, weights):
        query_w, output_w, kv_w, _, gains = weights
        n_one = norm_forward(x, gains[0]).astype(BF)
        q_raw = jnp.concatenate([mm(n_one, w) for w in query_w], -1)
        kv_raw = mm(n_one, kv_w)
        kv_own = jnp.concatenate([turned(kv_raw[:, :kv_width], 1.0), kv_raw[:, kv_width:]], -1)
        kv_own = kv_own.astype(BF)
        kv_near = jnp.concatenate([kv_own, swap_y(kv_own)], 0)
        kv_far = swap_c(kv_near)
        queries, attended, low = attend(place, q_raw, kv_near, kv_far, cosine, sine)
        mid = x
        for i, w in enumerate(output_w):
            mid = mid + mm_nt(attended[:, i * part_cols : (i + 1) * part_cols], w)
        n_two = norm_forward(mid, gains[1]).astype(BF)
        kept = (x, n_one, queries, kv_near, kv_far, attended, low, mid, n_two)
        return mid, n_two, kept

    def halves(value):
        return value.reshape(dp, 2, shard // 2, -1).swapaxes(0, 1)

    def by_section(pair):
        return jnp.where(first, pair, pair[::-1])

    def reduce_group(blocks):
        sides = [jnp.stack([b[s] for s in range(2) for b in side]) for side in blocks]
        return scatter_group(sides[0], sides[1]).astype(BF)

    def part(value, chip_at, core_at):
        at = (2 * chip_at + core_at) * part_cols
        return value[:, at : at + part_cols]

    def backward_attention(grad, summed, gates, weights, kept, first_done=()):
        query_w, output_w, kv_w, router, gains = weights
        x, n_one, queries, kv_near, kv_far, attended, low, mid, n_two = kept
        d_gates = rolled(summed[:, width : width + E])
        spread = gates * (d_gates - jnp.sum(gates * d_gates, -1, keepdims=True))
        spread_low = spread.astype(BF)
        d_n_two = summed[:, :width] + mm_nt(spread_low, router[:, :E])
        d_norm, gain_two_grad = norm_backward(mid, gains[1], d_n_two)
        d_mid = grad.astype(F32) + d_norm
        d_attn = d_mid.astype(BF)
        d_attended = jnp.concatenate([mm(d_attn, w) for w in output_w], -1).astype(BF)
        out_part = reduce_group(
            [
                [
                    by_section(halves(mm_tn(d_attn, part(attended, y, c)).astype(BF)))
                    .reshape(2, width // 2, part_cols)
                    for y in range(2)
                ]
                for c in range(2)
            ]
        )
        dq, d_near, d_far = after(
            attend_back(
                place, queries, attended, d_attended, kv_near, kv_far, low, cosine, sine
            ),
            out_part,
            first_done,
        )
        d_kv = add(d_near, swap_c(d_far))
        d_kv = d_kv[:own] + swap_y(d_kv[own:].astype(BF)).astype(F32)
        d_kv = jnp.concatenate([turned(d_kv[:, :kv_width], -1.0), d_kv[:, kv_width:]], -1)
        d_kv = d_kv.astype(BF)
        d_n_one = mm_nt(d_kv, kv_w)
        for i, w in enumerate(query_w):
            d_n_one = d_n_one + mm_nt(dq[:, i * part_cols : (i + 1) * part_cols], w)
        d_norm, gain_one_grad = norm_backward(x, gains[0], d_n_one)
        d_in = (d_mid + d_norm).astype(BF)
        pieces = (n_one, n_two, dq, d_kv, spread_low, gain_one_grad, gain_two_grad)
        return d_in, out_part.reshape(dp, -1, part_cols), pieces

    def attn_grads(pieces):
        n_one, n_two, dq, d_kv, spread_low, gain_one_grad, gain_two_grad = pieces
        at = jnp.arange(part_cols)[None, :] - kv_width

        def column(k):
            return jnp.broadcast_to((at == k).astype(BF), (own, part_cols))

        def padded(value, ahead):
            behind = part_cols - ahead - value.shape[1]
            return jnp.pad(value, ((0, 0), (ahead, behind)))

        keys_and_extras = (
            mm_tn(n_one, padded(d_kv[:, :kv_width], 0))
            + mm_tn(n_two, padded(rolled(spread_low), kv_width))
            + mm_tn(gain_one_grad, column(E))
            + mm_tn(gain_two_grad, column(E + 1))
        )
        values_part = mm_tn(n_one, padded(d_kv[:, kv_width:], 0))
        small = jnp.stack([keys_and_extras, values_part]).astype(BF)
        small = small.reshape(2, dp, 2, 2, little, part_cols).transpose(3, 2, 0, 1, 4, 5)
        small = absolute(small)
        late = []
        for c in range(2):
            side = []
            for y in range(2):
                main = halves(mm_tn(n_one, part(dq, y, c)).astype(BF))
                main = main.reshape(2, dp, shard // 2, part_cols)
                both = jnp.concatenate([main, small[c, y]], 2)
                side.append(by_section(both.reshape(2, -1, part_cols)))
            late.append(side)
        return reduce_group(late).reshape(dp, -1, part_cols)

    def reduce_dp(value):
        return lax.psum_scatter(value, "dp", scatter_dimension=0, tiled=True)

    def blocks4(value):
        return value.reshape(4, own, -1)

    def both_batches(value_0, value_1):
        got = swap_x(jnp.where(first, value_1, value_0))
        mine = jnp.where(first, value_0, value_1)
        return jnp.where(first, jnp.stack([mine, got]), jnp.stack([got, mine]))[None, :, None]

    own_cot = pick(out_cotangent, section)[0]
    own_in = pick(block_input, section)[0]

    down_0 = gather_dp(expert_shard[0][:, 2 * cols :])
    up_0 = gather_dp(after(expert_shard[0][:, : 2 * cols], down_0))
    weights_0 = attn_weights(
        attn_gather(after(attn_part_0, cot_rows[1], expert_shard[0]), down_0)
    )
    mid_0, n_two_0, kept_0 = forward_attention(own_in.astype(F32), weights_0)
    rows_0 = gather_rows(n_two_0)
    experts_0 = (up_0, down_0)
    router_0 = weights_0[3]
    attn_part_1 = gather_dp(after(attn_shard[1], up_0, rows_0[0]))
    far_0 = experts_call(ff, experts_0, forward=(rows_0[1], hits[1], router_0))
    near_0 = experts_call(ff, experts_0, forward=(rows_0[0], hits[0], router_0))
    experts_1 = gather_dp(after(expert_shard[1], attn_part_1, near_0[0]))
    experts_1 = experts_1[:, : 2 * cols], experts_1[:, 2 * cols :]
    near_1 = gather_chips(after(attn_part_1, far_0[0], near_0[0]))
    weights_1 = attn_weights((near_1, swap_c(near_1)))
    moe_0 = scatter_group(blocks4(near_0[0]), blocks4(far_0[0]))
    out_0 = (mid_0 + moe_0).astype(BF)

    mid_1, n_two_1, kept_1 = forward_attention(out_0.astype(F32), weights_1)
    rows_1 = gather_rows(n_two_1)
    router_1 = weights_1[3]
    far_1 = experts_call(
        ff, experts_1, forward=(rows_1[1], hits[1], router_1), backward=(cot_rows[1], sums)
    )
    near_1 = experts_call(
        ff, experts_1, forward=(rows_1[0], hits[0], router_1), backward=(cot_rows[0], sums)
    )
    summed_1 = scatter_group(blocks4(near_1[2]), blocks4(far_1[2]))
    back_1 = after((near_1[3:], far_1[3:]), near_1[2], far_1[2])
    grads_1 = expert_grads(rows_1, cot_rows, *zip(*back_1))
    experts_g1 = [reduce_dp(g) for g in grads_1]
    link, out_g1, pieces_1 = backward_attention(
        own_cot, after(summed_1, grads_1[0]), near_1[1][:own], weights_1, kept_1
    )

    link_rows = after(gather_rows(link), grads_1[1])
    far_b = experts_call(ff, experts_0, backward=(link_rows[1], sums), kept=far_0[1:])
    near_b = experts_call(ff, experts_0, backward=(link_rows[0], sums), kept=near_0[1:])
    moe_1 = after((near_1[0], far_1[0]), link_rows[1])
    out_1 = (mid_1 + scatter_group(blocks4(moe_1[0]), blocks4(moe_1[1]))).astype(BF)
    near_d, far_d = after((near_b[0], far_b[0]), out_1, experts_g1[0])
    summed_0 = scatter_group(blocks4(near_d), blocks4(far_d))
    back_0 = after((near_b[1:], far_b[1:]), near_d, far_d)
    grads_0 = expert_grads(rows_0, link_rows, *zip(*back_0))
    experts_g0 = [reduce_dp(g) for g in grads_0]
    late_g1 = attn_grads(after(pieces_1, summed_0))
    grad_in, out_g0, pieces_0 = backward_attention(
        link, after(summed_0, grads_0), near_0[1][:own], weights_0, kept_0, late_g1
    )
    section_outputs = both_batches(out_0, out_1)
    early = jnp.concatenate([out_g1, late_g1, out_g0], 1)
    early = reduce_dp(early.reshape(-1, part_cols))

    def to_owner(value_0, value_1):
        got = swap_x(jnp.where(first, value_1, value_0))
        mine = jnp.where(first, value_0, value_1)
        return jnp.where(first, mine, got), jnp.where(first, got, mine)

    low_up, high_up = to_owner(experts_g0[0], experts_g1[0])
    low_down, high_down = to_owner(experts_g0[1], experts_g1[1])
    late_g0 = attn_grads(after(pieces_0, low_up, low_down, section_outputs))
    late_g0 = reduce_dp(late_g0.reshape(-1, part_cols))

    input_grads = both_batches(after(grad_in, early), link)

    h = shard // 2
    both_parts = shard + little
    low, high = to_owner(
        jnp.concatenate([early[both_parts:], late_g0], 0), early[:both_parts]
    )
    output_g = jnp.concatenate([low[:h], high[:h]], 0).astype(F32)
    query_g = jnp.concatenate([low[h : 2 * h], high[h : 2 * h]], 0).astype(F32)
    key_g = low[2 * h :].astype(F32)
    value_g = high[2 * h :].astype(F32)
    def split(low_part, high_part):
        both = jnp.stack([low_part, high_part], 0).astype(F32)
        return both.reshape(2, shard, half_e, ff)

    gate_g = split(low_up[:, :cols], high_up[:, :cols]).transpose(0, 2, 1, 3)
    gate_g = gate_g.reshape(E, shard, ff)
    up_g = split(low_up[:, cols:], high_up[:, cols:]).transpose(0, 2, 1, 3)
    up_g = up_g.reshape(E, shard, ff)
    down_g = split(low_down, high_down).transpose(0, 2, 3, 1).reshape(E, ff, shard)
    return (
        section_outputs,
        input_grads,
        key_g[:, kv_width + E][None],
        key_g[:, kv_width + E + 1][None],
        key_g[:, :kv_width][None],
        value_g[:, :kv_width][None],
        key_g[:, kv_width : kv_width + E][None],
        query_g[None],
        output_g.T[None],
        gate_g[None],
        up_g[None],
        down_g[None],
    )


def solution(mesh):
    placed = (
        P(None, "dp", "tensor", None),
        P(None, "dp", "tensor", None),
        P(None, "dp", None, None),
        P("section", ("dp", "tensor")),
        P("section", ("dp", "tensor")),
        P("section", ("dp", "tensor"), None),
        P("section", ("dp", "tensor"), None),
        P("section", ("dp", "tensor"), None),
        P("section", "dp", "tensor"),
        P("section", "tensor", "dp"),
        P("section", None, "dp", "tensor"),
        P("section", None, "dp", "tensor"),
        P("section", None, "tensor", "dp"),
    )
    return jax.shard_map(
        per_device,
        mesh=mesh,
        in_specs=placed,
        out_specs=(
            P("section", None, "dp", "tensor", None),
            P("section", None, "dp", "tensor", None),
            P("section", ("dp", "tensor")),
            P("section", ("dp", "tensor")),
            P("section", ("dp", "tensor"), None),
            P("section", ("dp", "tensor"), None),
            P("section", ("dp", "tensor"), None),
            P("section", "dp", "tensor"),
            P("section", "tensor", "dp"),
            P("section", None, "dp", "tensor"),
            P("section", None, "dp", "tensor"),
            P("section", None, "tensor", "dp"),
        ),
        check_vma=False,
    )
```

```python
import jax
import jax.numpy as jnp
from jax import lax
from jax.sharding import PartitionSpec as P

QUERY_HEADS = 12
KEY_VALUE_HEADS = 2
HEAD_SIZE = 128
TOP = 4
E = 8
EPS = 1e-06
NEG = -1e30
BF = jnp.bfloat16
F32 = jnp.float32


def dot(a, b, contract):
    return lax.dot_general(a, b, (contract, ((), ())), preferred_element_type=F32)


def mm(a, b):
    return dot(a, b, ((1,), (0,)))


def mm_nt(a, b):
    return dot(a, b, ((1,), (1,)))


def mm_tn(a, b):
    return dot(a, b, ((0,), (0,)))


def masked_softmax(logits, hit):
    logits = jnp.where(hit, logits, NEG)
    top = jnp.max(logits, -1, keepdims=True)
    exps = jnp.where(hit, jnp.exp(logits - top), 0.0)
    return exps / jnp.sum(exps, -1, keepdims=True)


def spread(gates, ff):
    count = E // 2
    lane = lax.broadcasted_iota(jnp.int32, (gates.shape[0], count * ff), 1)
    wide = jnp.broadcast_to(gates[:, count - 1][:, None], lane.shape)
    for e in range(count - 2, -1, -1):
        wide = jnp.where(lane < (e + 1) * ff, gates[:, e][:, None], wide)
    return wide


def experts_call(ff, weight, forward=None, backward=None, kept=None):
    up_w, down_w = weight
    cols = (E // 2) * ff
    outs = []
    if forward:
        rows, hit, router = forward
        gates = masked_softmax(mm(rows, router[:, :E]), hit > 0.0)
        both = mm(rows, up_w)
        pre_gate, pre_up = both[:, :cols], both[:, cols:]
    else:
        gates, pre_gate, pre_up = kept
        pre_gate, pre_up = pre_gate.astype(F32), pre_up.astype(F32)
    wide = spread(gates, ff)
    sig = jax.nn.sigmoid(pre_gate)
    active = pre_gate * sig
    hidden = active * pre_up
    gated = (hidden * wide).astype(BF)
    if forward:
        outs += [mm_nt(gated, down_w).astype(BF), gates]
        if not backward:
            outs += [pre_gate.astype(BF), pre_up.astype(BF)]
    if backward:
        grad, sums = backward
        back = mm(grad, down_w)
        tail = mm((hidden * back).astype(BF), sums)
        d_hidden = back * wide
        d_gate = (d_hidden * pre_up * (sig * (1.0 + pre_gate * (1.0 - sig)))).astype(BF)
        d_both = jnp.concatenate([d_gate, (d_hidden * active).astype(BF)], -1)
        d_rows = mm_nt(d_both, up_w).astype(BF)
        outs += [jnp.concatenate([d_rows, tail.astype(BF)], -1), d_both, gated]
    return outs


def expert_grads(rows, grads, d_both, gated):
    up = mm_tn(rows[1], d_both[1]) + mm_tn(rows[0], d_both[0])
    down = mm_tn(grads[1], gated[1]) + mm_tn(grads[0], gated[0])
    return up.astype(BF), down.astype(BF)


def turn(value, cosine, sine):
    heads = value.reshape(value.shape[0], -1, HEAD_SIZE)
    moved = jnp.roll(heads, HEAD_SIZE // 2, -1)
    return (heads * cosine[:, None] + moved * sine[:, None]).reshape(value.shape)


def relative_heads(place, value):
    value = value.reshape(value.shape[0], 2, KEY_VALUE_HEADS, HEAD_SIZE)
    return jnp.where(place[4] == 0, value, value[:, :, ::-1])


def seen(place, own):
    key = jnp.arange(own, dtype=jnp.int32)
    key = jnp.concatenate([key + place[b] for b in range(4)])
    return key[None, :] <= jnp.arange(own, dtype=jnp.int32)[:, None]


def attend(place, q_raw, near, far, cosine, sine):
    own, width = q_raw.shape
    queries = turn(q_raw, cosine, sine).astype(BF)
    q_group = queries.reshape(own, KEY_VALUE_HEADS, -1, HEAD_SIZE)
    kv = relative_heads(place, jnp.concatenate([near, far], 0))
    scores = jnp.einsum("qgje,kge->gjqk", q_group, kv[:, 0], preferred_element_type=F32)
    scores = jnp.where(seen(place, own), scores * HEAD_SIZE ** (-0.5), NEG)
    top = jnp.max(scores, -1, keepdims=True)
    exps = jnp.exp(scores - top)
    total = jnp.sum(exps, -1, keepdims=True)
    low = lax.optimization_barrier((exps / total).astype(BF))
    attended = jnp.einsum("gjqk,kge->qgje", low, kv[:, 1], preferred_element_type=F32)
    return queries, attended.astype(BF).reshape(own, width), low


def attend_back(place, queries, attended, grad, near, far, low, cosine, sine):
    own, width = queries.shape
    q_group = queries.reshape(own, KEY_VALUE_HEADS, -1, HEAD_SIZE)
    g_group = grad.reshape(own, KEY_VALUE_HEADS, -1, HEAD_SIZE)
    kv = relative_heads(place, jnp.concatenate([near, far], 0))
    delta = jnp.sum(g_group.astype(F32) * attended.reshape(g_group.shape).astype(F32), -1)
    delta = delta.transpose(1, 2, 0)[..., None]
    d_probs = jnp.einsum("qgje,kge->gjqk", g_group, kv[:, 1], preferred_element_type=F32)
    d_scores = (low.astype(F32) * (d_probs - delta) * HEAD_SIZE ** (-0.5)).astype(BF)
    d_scores = lax.optimization_barrier(d_scores)
    d_values = jnp.einsum("gjqk,qgje->kge", low, g_group, preferred_element_type=F32)
    d_keys = jnp.einsum("gjqk,qgje->kge", d_scores, q_group, preferred_element_type=F32)
    dq = jnp.einsum("gjqk,kge->qgje", d_scores, kv[:, 0], preferred_element_type=F32)
    dq = turn(dq.reshape(own, width), cosine, -sine).astype(BF)
    pieces = []
    for value in (d_keys, d_values):
        one, two = value[:, 0].astype(BF), value[:, 1].astype(BF)
        pieces += [jnp.where(place[4] == 0, one, two), jnp.where(place[4] == 0, two, one)]
    d_kv = jnp.concatenate(pieces, -1)
    return dq, d_kv[: near.shape[0]], d_kv[near.shape[0] :]


def swap_x(value):
    return lax.ppermute(value, "section", [(0, 1), (1, 0)])


def swap_y(value):
    return lax.ppermute(value, "tensor", [(t, t ^ 2) for t in range(4)])


def swap_c(value):
    return lax.ppermute(value, "tensor", [(t, t ^ 1) for t in range(4)])


def after(value, *first):
    return lax.optimization_barrier((value, first))[0]


def gather_chips(value, *hold):
    half = value.shape[0] // 2
    from_x, from_y = swap_x(value), swap_y(value)
    if hold:
        from_x, from_y = after((from_x, from_y), *hold)
    top = swap_x(from_y[:half])
    low = swap_y(from_x[half:])
    return jnp.stack([value, from_y, from_x, jnp.concatenate([top, low], 0)])


def add(one, two):
    return one.astype(F32) + two.astype(F32)


def scatter_chips(parts):
    half = parts.shape[1] // 2
    top = swap_x(parts[3][:half])
    low = swap_y(parts[3][half:])
    to_y = jnp.concatenate([add(parts[1][:half], top).astype(BF), parts[1][half:]], 0)
    to_x = jnp.concatenate([parts[2][:half], add(parts[2][half:], low).astype(BF)], 0)
    return parts[0].astype(F32) + swap_y(to_y).astype(F32) + swap_x(to_x).astype(F32)


def scatter_group(near, far):
    return scatter_chips(add(near, swap_c(far)).astype(BF))


def norm_forward(value, gain):
    inverse = lax.rsqrt(jnp.mean(value * value, -1, keepdims=True) + EPS)
    return value * inverse * gain


def norm_backward(value, gain, grad):
    inverse = lax.rsqrt(jnp.mean(value * value, -1, keepdims=True) + EPS)
    scaled = value * inverse
    weighted = grad * gain
    gain_grad = (grad * scaled).astype(BF)
    return inverse * (weighted - scaled * jnp.mean(weighted * scaled, -1, keepdims=True)), gain_grad


def per_device(
    block_input,
    out_cotangent,
    routes,
    attn_gain,
    ffn_gain,
    key_projection_weight,
    value_projection_weight,
    router_weight,
    query_weight,
    output_weight,
    expert_gate,
    expert_up,
    expert_down,
):
    own = block_input.shape[2]
    width = block_input.shape[3]
    length = routes.shape[2]
    ff = expert_gate.shape[3]
    shard = expert_gate.shape[2]
    dp = width // shard
    little = attn_gain.shape[1]
    half_e = E // 2
    cols = half_e * ff
    kv_width = KEY_VALUE_HEADS * HEAD_SIZE
    part_cols = query_weight.shape[2]
    section = lax.axis_index("section")
    tensor = lax.axis_index("tensor")
    first = section == 0
    chip = tensor // 2
    core = tensor % 2

    def pick(pair, at):
        return lax.dynamic_index_in_dim(pair, at, 0, keepdims=False)

    extras = jnp.concatenate(
        [
            router_weight[0],
            attn_gain[0][:, None],
            ffn_gain[0][:, None],
            jnp.zeros((little, 128 - E - 2), BF),
        ],
        -1,
    )
    pack_q = jnp.concatenate(
        [query_weight[0], jnp.concatenate([key_projection_weight[0], extras], -1)], 0
    )
    pack_o = jnp.concatenate(
        [output_weight[0].T, jnp.pad(value_projection_weight[0], ((0, 0), (0, 128)))], 0
    )
    got = swap_x(jnp.where(first, pack_o, pack_q))
    kept = jnp.where(first, pack_q, pack_o)
    attn_shard = [jnp.where(first, kept, got), jnp.where(first, got, kept)]
    pack_rows = shard + little

    def gather_dp(value):
        return lax.all_gather(value, "dp", axis=0, tiled=True)

    attn_part_0 = gather_dp(attn_shard[0])

    def expert_pack(start):
        def across(weight):
            piece = lax.dynamic_slice_in_dim(weight[0], start, half_e, 0)
            return piece.transpose(1, 0, 2).reshape(shard, cols)

        down = lax.dynamic_slice_in_dim(expert_down[0], start, half_e, 0).reshape(cols, shard)
        return jnp.concatenate([across(expert_gate), across(expert_up), down.T], -1)

    kept_e = expert_pack(half_e * section)
    got_e = swap_x(after(expert_pack(half_e * (1 - section)), got))
    expert_shard = [jnp.where(first, kept_e, got_e), jnp.where(first, got_e, kept_e)]

    cot = jnp.where(first, out_cotangent[:, 0], out_cotangent[::-1, 0])
    cot_near = after(jnp.stack([cot, swap_y(after(cot, got))], 1), got_e, attn_part_0)
    cot_far = swap_c(cot_near)
    cot_rows = [v.reshape(4 * own, width) for v in (cot_near, cot_far)]

    def absolute(blocks):
        blocks = jnp.where(core == 0, blocks, blocks[::-1])
        return jnp.where(chip == 0, blocks, blocks[:, ::-1])

    def attn_gather(part, *first_done):
        near = gather_chips(part)
        return near, swap_c(after(near, *first_done))

    def attn_weights(sides):
        sides = [side.reshape(2, 2, dp, pack_rows, part_cols) for side in sides]
        mains, smalls = [], []
        for kind in (section, 1 - section):
            chosen = [pick(side, kind) for side in sides]
            mains.append(
                [
                    chosen[c][y, :, :shard].reshape(width, part_cols)
                    for y in range(2)
                    for c in range(2)
                ]
            )
            small = absolute(jnp.stack([c[:, :, shard:] for c in chosen]))
            smalls.append(small.transpose(2, 1, 0, 3, 4).reshape(width, part_cols))
        extra = smalls[0][:, kv_width:]
        router = jnp.concatenate([rolled(extra[:, :E]), extra[:, E:]], -1)
        kv_w = jnp.concatenate([smalls[0][:, :kv_width], smalls[1][:, :kv_width]], -1)
        gains = extra[:, E : E + 2].astype(F32).T
        return mains[0], mains[1], kv_w, router, gains

    def rolled(columns):
        return jnp.where(first, columns, jnp.roll(columns, half_e, -1))

    def hits_of(rel_core):
        pieces = []
        for rel_x in range(2):
            for rel_y in range(2):
                start = (tensor ^ (2 * rel_y + rel_core)) * own
                piece = lax.dynamic_slice(routes, (section ^ rel_x, 0, start, 0), (1, 1, own, TOP))
                pieces.append(piece.reshape(own, TOP))
        picked = jnp.concatenate(pieces, 0)
        ids = (jnp.arange(E, dtype=jnp.int32) + half_e * section) % E
        return jnp.any(picked[:, :, None] == ids[None, None, :], 1).astype(F32)

    hits = [hits_of(0), hits_of(1)]
    sums = (
        jnp.arange(cols)[:, None] // ff + half_e * section == jnp.arange(128)[None, :]
    ).astype(BF)

    halfway = HEAD_SIZE // 2
    places = (tensor * own + jnp.arange(own)).astype(F32)
    rates = 10000.0 ** (-(jnp.arange(halfway, dtype=F32) * 2.0) / HEAD_SIZE)
    angles = places[:, None] * rates[None, :]
    cosine = jnp.concatenate([jnp.cos(angles)] * 2, -1)
    sine = jnp.concatenate([-jnp.sin(angles), jnp.sin(angles)], -1)
    place = jnp.stack(
        [((tensor ^ (2 * y + c)) - tensor) * own for c in range(2) for y in range(2)]
        + [chip] * 4
    ).astype(jnp.int32)

    def turned(value, sign):
        heads = value.reshape(own, -1, HEAD_SIZE)
        moved = jnp.roll(heads, halfway, -1)
        return (heads * cosine[:, None] + sign * moved * sine[:, None]).reshape(own, -1)

    def gather_rows(value):
        near = gather_chips(value)
        return near.reshape(4 * own, width), swap_c(near).reshape(4 * own, width)

    def forward_attention(x, weights):
        query_w, output_w, kv_w, _, gains = weights
        n_one = norm_forward(x, gains[0]).astype(BF)
        q_raw = jnp.concatenate([mm(n_one, w) for w in query_w], -1)
        kv_raw = mm(n_one, kv_w)
        kv_own = jnp.concatenate([turned(kv_raw[:, :kv_width], 1.0), kv_raw[:, kv_width:]], -1)
        kv_own = kv_own.astype(BF)
        kv_near = jnp.concatenate([kv_own, swap_y(kv_own)], 0)
        kv_far = swap_c(kv_near)
        queries, attended, low = attend(place, q_raw, kv_near, kv_far, cosine, sine)
        mid = x
        for i, w in enumerate(output_w):
            mid = mid + mm_nt(attended[:, i * part_cols : (i + 1) * part_cols], w)
        n_two = norm_forward(mid, gains[1]).astype(BF)
        kept = (x, n_one, queries, kv_near, kv_far, attended, low, mid, n_two)
        return mid, n_two, kept

    def halves(value):
        return value.reshape(dp, 2, shard // 2, -1).swapaxes(0, 1)

    def by_section(pair):
        return jnp.where(first, pair, pair[::-1])

    def reduce_group(blocks):
        sides = [jnp.stack([b[s] for s in range(2) for b in side]) for side in blocks]
        return scatter_group(sides[0], sides[1]).astype(BF)

    def part(value, chip_at, core_at):
        at = (2 * chip_at + core_at) * part_cols
        return value[:, at : at + part_cols]

    def backward_attention(grad, summed, gates, weights, kept, first_done=()):
        query_w, output_w, kv_w, router, gains = weights
        x, n_one, queries, kv_near, kv_far, attended, low, mid, n_two = kept
        d_gates = rolled(summed[:, width : width + E])
        spread = gates * (d_gates - jnp.sum(gates * d_gates, -1, keepdims=True))
        spread_low = spread.astype(BF)
        d_n_two = summed[:, :width] + mm_nt(spread_low, router[:, :E])
        d_norm, gain_two_grad = norm_backward(mid, gains[1], d_n_two)
        d_mid = grad.astype(F32) + d_norm
        d_attn = d_mid.astype(BF)
        d_attended = jnp.concatenate([mm(d_attn, w) for w in output_w], -1).astype(BF)
        out_part = reduce_group(
            [
                [
                    by_section(halves(mm_tn(d_attn, part(attended, y, c)).astype(BF)))
                    .reshape(2, width // 2, part_cols)
                    for y in range(2)
                ]
                for c in range(2)
            ]
        )
        dq, d_near, d_far = after(
            attend_back(
                place, queries, attended, d_attended, kv_near, kv_far, low, cosine, sine
            ),
            out_part,
            first_done,
        )
        d_kv = add(d_near, swap_c(d_far))
        d_kv = d_kv[:own] + swap_y(d_kv[own:].astype(BF)).astype(F32)
        d_kv = jnp.concatenate([turned(d_kv[:, :kv_width], -1.0), d_kv[:, kv_width:]], -1)
        d_kv = d_kv.astype(BF)
        d_n_one = mm_nt(d_kv, kv_w)
        for i, w in enumerate(query_w):
            d_n_one = d_n_one + mm_nt(dq[:, i * part_cols : (i + 1) * part_cols], w)
        d_norm, gain_one_grad = norm_backward(x, gains[0], d_n_one)
        d_in = (d_mid + d_norm).astype(BF)
        pieces = (n_one, n_two, dq, d_kv, spread_low, gain_one_grad, gain_two_grad)
        return d_in, out_part.reshape(dp, -1, part_cols), pieces

    def attn_grads(pieces):
        n_one, n_two, dq, d_kv, spread_low, gain_one_grad, gain_two_grad = pieces
        at = jnp.arange(part_cols)[None, :] - kv_width

        def column(k):
            return jnp.broadcast_to((at == k).astype(BF), (own, part_cols))

        def padded(value, ahead):
            behind = part_cols - ahead - value.shape[1]
            return jnp.pad(value, ((0, 0), (ahead, behind)))

        keys_and_extras = (
            mm_tn(n_one, padded(d_kv[:, :kv_width], 0))
            + mm_tn(n_two, padded(rolled(spread_low), kv_width))
            + mm_tn(gain_one_grad, column(E))
            + mm_tn(gain_two_grad, column(E + 1))
        )
        values_part = mm_tn(n_one, padded(d_kv[:, kv_width:], 0))
        small = jnp.stack([keys_and_extras, values_part]).astype(BF)
        small = small.reshape(2, dp, 2, 2, little, part_cols).transpose(3, 2, 0, 1, 4, 5)
        small = absolute(small)
        late = []
        for c in range(2):
            side = []
            for y in range(2):
                main = halves(mm_tn(n_one, part(dq, y, c)).astype(BF))
                main = main.reshape(2, dp, shard // 2, part_cols)
                both = jnp.concatenate([main, small[c, y]], 2)
                side.append(by_section(both.reshape(2, -1, part_cols)))
            late.append(side)
        return reduce_group(late).reshape(dp, -1, part_cols)

    def reduce_dp(value):
        return lax.psum_scatter(value, "dp", scatter_dimension=0, tiled=True)

    def blocks4(value):
        return value.reshape(4, own, -1)

    def both_batches(value_0, value_1):
        got = swap_x(jnp.where(first, value_1, value_0))
        mine = jnp.where(first, value_0, value_1)
        return jnp.where(first, jnp.stack([mine, got]), jnp.stack([got, mine]))[None, :, None]

    own_cot = pick(out_cotangent, section)[0]
    own_in = pick(block_input, section)[0]

    down_0 = gather_dp(expert_shard[0][:, 2 * cols :])
    up_0 = gather_dp(after(expert_shard[0][:, : 2 * cols], down_0))
    weights_0 = attn_weights(
        attn_gather(after(attn_part_0, cot_rows[1], expert_shard[0]), down_0)
    )
    mid_0, n_two_0, kept_0 = forward_attention(own_in.astype(F32), weights_0)
    rows_0 = gather_rows(n_two_0)
    experts_0 = (up_0, down_0)
    router_0 = weights_0[3]
    attn_part_1 = gather_dp(after(attn_shard[1], up_0, rows_0[0]))
    far_0 = experts_call(ff, experts_0, forward=(rows_0[1], hits[1], router_0))
    near_0 = experts_call(ff, experts_0, forward=(rows_0[0], hits[0], router_0))
    experts_1 = gather_dp(after(expert_shard[1], attn_part_1, near_0[0]))
    experts_1 = experts_1[:, : 2 * cols], experts_1[:, 2 * cols :]
    moe_0 = scatter_group(blocks4(near_0[0]), blocks4(far_0[0]))
    near_1 = gather_chips(after(attn_part_1, far_0[0], near_0[0]), moe_0)
    weights_1 = attn_weights((near_1, swap_c(near_1)))
    out_0 = (mid_0 + moe_0).astype(BF)

    mid_1, n_two_1, kept_1 = forward_attention(out_0.astype(F32), weights_1)
    rows_1 = gather_rows(n_two_1)
    router_1 = weights_1[3]
    far_1 = experts_call(
        ff, experts_1, forward=(rows_1[1], hits[1], router_1), backward=(cot_rows[1], sums)
    )
    near_1 = experts_call(
        ff, experts_1, forward=(rows_1[0], hits[0], router_1), backward=(cot_rows[0], sums)
    )
    summed_1 = scatter_group(blocks4(near_1[2]), blocks4(far_1[2]))
    back_1 = after((near_1[3:], far_1[3:]), near_1[2], far_1[2])
    grads_1 = expert_grads(rows_1, cot_rows, *zip(*back_1))
    experts_g1 = [reduce_dp(g) for g in grads_1]
    link, out_g1, pieces_1 = backward_attention(
        own_cot, after(summed_1, grads_1[0]), near_1[1][:own], weights_1, kept_1
    )

    link_rows = after(gather_rows(link), grads_1[1])
    far_b = experts_call(ff, experts_0, backward=(link_rows[1], sums), kept=far_0[1:])
    near_b = experts_call(ff, experts_0, backward=(link_rows[0], sums), kept=near_0[1:])
    moe_1 = after((near_1[0], far_1[0]), link_rows[1])
    out_1 = (mid_1 + scatter_group(blocks4(moe_1[0]), blocks4(moe_1[1]))).astype(BF)
    near_d, far_d = after((near_b[0], far_b[0]), out_1, experts_g1[0])
    summed_0 = scatter_group(blocks4(near_d), blocks4(far_d))
    back_0 = after((near_b[1:], far_b[1:]), near_d, far_d)
    grads_0 = expert_grads(rows_0, link_rows, *zip(*back_0))
    experts_g0 = [reduce_dp(g) for g in grads_0]
    late_g1 = attn_grads(after(pieces_1, summed_0))
    grad_in, out_g0, pieces_0 = backward_attention(
        link, after(summed_0, grads_0), near_0[1][:own], weights_0, kept_0, late_g1
    )
    section_outputs = both_batches(out_0, out_1)
    early = jnp.concatenate([out_g1, late_g1, out_g0], 1)
    early = reduce_dp(early.reshape(-1, part_cols))

    def to_owner(value_0, value_1):
        got = swap_x(jnp.where(first, value_1, value_0))
        mine = jnp.where(first, value_0, value_1)
        return jnp.where(first, mine, got), jnp.where(first, got, mine)

    low_up, high_up = to_owner(experts_g0[0], experts_g1[0])
    low_down, high_down = to_owner(experts_g0[1], experts_g1[1])
    late_g0 = attn_grads(after(pieces_0, low_up, low_down, section_outputs))
    late_g0 = reduce_dp(late_g0.reshape(-1, part_cols))

    input_grads = both_batches(after(grad_in, early), link)

    h = shard // 2
    both_parts = shard + little
    low, high = to_owner(
        jnp.concatenate([early[both_parts:], late_g0], 0), early[:both_parts]
    )
    output_g = jnp.concatenate([low[:h], high[:h]], 0).astype(F32)
    query_g = jnp.concatenate([low[h : 2 * h], high[h : 2 * h]], 0).astype(F32)
    key_g = low[2 * h :].astype(F32)
    value_g = high[2 * h :].astype(F32)
    def split(low_part, high_part):
        both = jnp.stack([low_part, high_part], 0).astype(F32)
        return both.reshape(2, shard, half_e, ff)

    gate_g = split(low_up[:, :cols], high_up[:, :cols]).transpose(0, 2, 1, 3)
    gate_g = gate_g.reshape(E, shard, ff)
    up_g = split(low_up[:, cols:], high_up[:, cols:]).transpose(0, 2, 1, 3)
    up_g = up_g.reshape(E, shard, ff)
    down_g = split(low_down, high_down).transpose(0, 2, 3, 1).reshape(E, ff, shard)
    return (
        section_outputs,
        input_grads,
        key_g[:, kv_width + E][None],
        key_g[:, kv_width + E + 1][None],
        key_g[:, :kv_width][None],
        value_g[:, :kv_width][None],
        key_g[:, kv_width : kv_width + E][None],
        query_g[None],
        output_g.T[None],
        gate_g[None],
        up_g[None],
        down_g[None],
    )


def solution(mesh):
    placed = (
        P(None, "dp", "tensor", None),
        P(None, "dp", "tensor", None),
        P(None, "dp", None, None),
        P("section", ("dp", "tensor")),
        P("section", ("dp", "tensor")),
        P("section", ("dp", "tensor"), None),
        P("section", ("dp", "tensor"), None),
        P("section", ("dp", "tensor"), None),
        P("section", "dp", "tensor"),
        P("section", "tensor", "dp"),
        P("section", None, "dp", "tensor"),
        P("section", None, "dp", "tensor"),
        P("section", None, "tensor", "dp"),
    )
    return jax.shard_map(
        per_device,
        mesh=mesh,
        in_specs=placed,
        out_specs=(
            P("section", None, "dp", "tensor", None),
            P("section", None, "dp", "tensor", None),
            P("section", ("dp", "tensor")),
            P("section", ("dp", "tensor")),
            P("section", ("dp", "tensor"), None),
            P("section", ("dp", "tensor"), None),
            P("section", ("dp", "tensor"), None),
            P("section", "dp", "tensor"),
            P("section", "tensor", "dp"),
            P("section", None, "dp", "tensor"),
            P("section", None, "dp", "tensor"),
            P("section", None, "tensor", "dp"),
        ),
        check_vma=False,
    )
```
